32 devices in a mesh: ctx: 16 (over z, y, x), tp: 2 (over core).
Axes of the slice: x: 2, y: 2, z: 4, core: 2. Of those that a mesh axis runs over, the one named last changes fastest.
Arguments:
- query: bfloat16 [2048, 8192], P('ctx', 'tp'), may hold values from -6 to 6
- keyed: bfloat16 [2048, 8192], P('ctx', 'tp'), may hold values from -6 to 6
- valued: bfloat16 [2048, 8192], P('ctx', 'tp'), may hold values from -6 to 6
- short_taps: float32 [3, 3, 8192], P(None, None, 'tp'), may hold values from -3.5 to 3.5
- rates: float32 [8, 8192], P(None, 'tp'), may hold values from 0.00012207031 to 0.1
- residues: float32 [8, 8192], P(None, 'tp'), may hold values from -1.5 to 1.5
- skip_gain: float32 [8192], P('tp'), may hold values from -1.6 to 1.6
- doc_ids: int32 [2048], P('ctx'), may hold values from 0 to 7, never falling along the last dimension, each value on 1 to 1024 neighbouring positions
Outputs:
- mixed: bfloat16 [2048, 8192], P('ctx', 'tp')
The draws below stay inside these ranges and needn't reach their ends.
Inputs may be any that keep to these rules, and one draw needn't show every extreme that they name: doc_ids never falls along the sequence; each of the 8 documents holds 1 to 1024 consecutive tokens, one exactly 1024.
All inputs are finite; a program needn't handle non-finite values.
Results may differ from the reference program's by a relative error of at most 0.0065.
Values may be sent and summed in bfloat16 or wider, within the bound.
No kernel may reach another device: no remote copies, remote signals or barrier semaphores. Data moves between devices by JAX's collectives and lax.ppermute only.
A program may use at most 128 MiB of HBM per device.

```python
import math
import jax
import jax.numpy as jnp
import numpy as np
from jax import lax

D = 8192
ORDER = 8
SHORT = 3
TOK_DEV = 128
NDOC = 8
TOKENS = 2048
MAXDOC = 1024


def modal_filter(key):
    base_key = jax.random.fold_in(key, 4242)
    kind_key, fast_key, pair_key, spacing_key, slow_key, polarity_key, spread_key, balance_key = jax.random.split(base_key, 8)
    pairs = ORDER // 2
    pair_kind = jax.random.randint(kind_key, (pairs, D), 0, 8)
    mode_kind = jnp.stack([pair_kind, pair_kind], axis=1).reshape(ORDER, D)
    fast_rate = jnp.exp(jax.random.uniform(fast_key, (ORDER, D), jnp.float32, math.log(0.045), math.log(0.1)))
    pair_rate = jnp.exp(jax.random.uniform(pair_key, (pairs, D), jnp.float32, math.log(0.0025), math.log(0.0042)))
    slow_rate = jnp.exp(jax.random.uniform(slow_key, (ORDER, D), jnp.float32, math.log(0.25), math.log(2.0))) / TOKENS
    spread = jax.random.uniform(spread_key, (ORDER, D), jnp.float32, 0.7, 1.3)
    spacing = jax.random.uniform(spacing_key, (pairs, D), jnp.float32, 0.05, 0.12)
    pair_rates = jnp.stack([pair_rate, pair_rate * (1.0 + spacing)], axis=1).reshape(ORDER, D)
    rates = jnp.where(mode_kind < 3, fast_rate, jnp.where(mode_kind < 6, pair_rates, slow_rate))
    polarity = jnp.where(jax.random.randint(polarity_key, (ORDER, D), 0, 2) == 0, -1.0, 1.0)
    fast_res = polarity * jnp.sqrt((1.0 - jnp.exp(-2.0 * fast_rate)) * 0.2) * spread
    amplitude = jnp.sqrt(4.0 * pair_rate * 0.16 * (1.0 + spacing) * (1.0 + 0.5 * spacing)) / spacing
    amplitude = amplitude * jnp.clip(spread[0::2], 0.8, 1.2) * polarity[0::2]
    balance = jax.random.uniform(balance_key, (pairs, D), jnp.float32, 0.97, 1.03)
    pair_res = jnp.stack([amplitude, -amplitude * balance], axis=1).reshape(ORDER, D)
    slow_res = polarity * jnp.sqrt(0.12 / MAXDOC) * spread
    residues = jnp.where(mode_kind < 3, fast_res, jnp.where(mode_kind < 6, pair_res, slow_res))
    return (rates, residues)


def draw_rates(key, part):
    return modal_filter(key)[0].astype(jnp.float32)


def draw_residues(key, part):
    return modal_filter(key)[1].astype(jnp.float32)


def block_levels(rng, shape, pieces, low, high):
    gain, own = 1.0, jax.random.fold_in(rng, 6)
    for position, parts in pieces:
        draws = jnp.exp(jax.random.uniform(jax.random.fold_in(own, position), (parts,), jnp.float32, low / len(pieces), high / len(pieces)))
        gain = gain * jnp.repeat(draws, shape[position] // parts).reshape([-1 if axis == position else 1 for axis in range(len(shape))])
    return gain


def length_profile(number_of, total, most, lean):
    loads = [(1 << 20) // math.isqrt(standing ** lean) + 1 for standing in range(2, number_of + 1)]
    surplus, counts = total - most - (number_of - 1), [1] * (number_of - 1)
    while surplus > 0:
        candidates = [i for i in range(number_of - 1) if counts[i] < most]
        mass, budget = sum([loads[i] for i in candidates]), surplus
        for i in candidates:
            addition = min(most - counts[i], max(1, budget * loads[i] // mass), surplus)
            counts[i] = counts[i] + addition
            surplus = surplus - addition
    return np.array([most] + counts)


def uneven_parts(stream_key, number_of, total, most, slope):
    if number_of == 2:
        one = jax.random.randint(stream_key, (), max(1, total - most), min(most, total - 1) + 1)
        return jnp.stack([one, total - one])
    tallies = jnp.asarray(length_profile(number_of, total, most, slope), jnp.int32)
    pairs = (number_of - 1) // 2
    giver, sink = tallies[1:1 + 2 * pairs:2], tallies[2:2 + 2 * pairs:2]
    slack = jnp.minimum(giver - 1, most - sink)
    moved = jax.random.randint(jax.random.fold_in(stream_key, 1), (pairs,), 0, 1 << 20) % (slack + 1)
    tallies = tallies.at[1:1 + 2 * pairs:2].set(giver - moved).at[2:2 + 2 * pairs:2].set(sink + moved)
    return tallies[jax.random.permutation(jax.random.fold_in(stream_key, 2), number_of)]


def normal_values(stream_key, extent, scale, most, cuts=(), held_as=jnp.bfloat16):
    values = scale * jax.random.normal(stream_key, extent, jnp.float32)
    if cuts:
        values = values * block_levels(stream_key, extent, cuts, -0.22, 0.18)
    return jnp.clip(values, -most, most).astype(held_as)


def setup_inputs(seed: int = 0) -> dict:
    key_list = jax.random.split(jax.random.key(seed), 9)
    return {
        "query": normal_values(key_list[0], (TOKENS, D), 1.0, 6.0, ((0, 16), (1, 2))),
        "keyed": normal_values(key_list[1], (TOKENS, D), 1.0, 6.0, ((0, 16), (1, 2))),
        "valued": normal_values(key_list[2], (TOKENS, D), 1.0, 6.0, ((0, 16), (1, 2))),
        "short_taps": normal_values(key_list[3], (3, SHORT, D), SHORT ** -0.5, 3.5, ((2, 2),), jnp.float32),
        "rates": draw_rates(jax.random.fold_in(key_list[8], 71), 0),
        "residues": draw_residues(jax.random.fold_in(key_list[8], 71), 0),
        "skip_gain": normal_values(key_list[6], (D,), 0.4, 1.6, ((0, 2),), jnp.float32),
        "doc_ids": jnp.searchsorted(jnp.cumsum(uneven_parts(key_list[7], NDOC, TOKENS, MAXDOC, 2)), jnp.arange(TOKENS), side="right").astype(jnp.int32),
    }


def short_conv(ext, ids_ext, taps):
    width = taps.shape[1] - 1
    length = ext.shape[1] - width
    total = jnp.zeros((ext.shape[0], length, ext.shape[2]), jnp.float32)
    for tap in range(taps.shape[1]):
        seg = ext[:, width - tap:width - tap + length]
        same = (ids_ext[width - tap:width - tap + length] == ids_ext[width:]).astype(jnp.float32)
        total = total + taps[:, tap][:, None, :] * seg * same[None, :, None]
    return total


def mode_terms(gated, ids, rates, residues):
    block = gated.shape[0]
    places = jnp.arange(block, dtype=jnp.float32)
    shifted = places - float(block // 2)
    lower = places[:, None] >= places[None, :]
    mask = (lower & (ids[:, None] == ids[None, :])).astype(jnp.float32)
    channels = gated.shape[1]
    long_part = jnp.zeros((block, channels), jnp.float32)
    ends = []
    for group in range(rates.shape[0] // 4):
        rate = rates[4 * group:4 * group + 4]
        grow = jnp.exp(rate[None] * shifted[:, None, None])
        weighted = (grow * gated[:, None, :]).reshape(block, 4 * channels)
        summed = jnp.dot(mask, weighted, precision=lax.Precision.HIGHEST).reshape(block, 4, channels)
        states = summed * jnp.exp(-rate[None] * shifted[:, None, None])
        long_part = long_part + jnp.sum(residues[4 * group:4 * group + 4][None] * states, axis=1)
        ends.append(states[block - 1])
    return long_part, jnp.concatenate(ends, axis=0)


def incoming(carry, ids, prev_last, rates, residues):
    block = ids.shape[0]
    places = jnp.arange(block, dtype=jnp.float32) + 1.0
    live = (ids == prev_last).astype(jnp.float32)
    total = jnp.zeros((block, rates.shape[1]), jnp.float32)
    for group in range(rates.shape[0] // 4):
        rate = rates[4 * group:4 * group + 4]
        weight = residues[4 * group:4 * group + 4] * carry[4 * group:4 * group + 4]
        total = total + jnp.sum(weight[None] * jnp.exp(-rate[None] * places[:, None, None]), axis=1)
    return total * live[:, None]


def transition(ids, prev_last, rates):
    block = ids.shape[0]
    keep = ((ids[0] == prev_last) & (ids[0] == ids[block - 1])).astype(jnp.float32)
    return jnp.exp(-rates * block) * keep


def reference(query, keyed, valued, short_taps, rates, residues, skip_gain, doc_ids):
    width = SHORT - 1
    blocks = TOKENS // TOK_DEV
    stacked = jnp.stack([query, keyed, valued]).reshape(3, blocks, TOK_DEV, D).transpose(1, 0, 2, 3)
    ids_blocks = doc_ids.reshape(blocks, TOK_DEV)

    def step(carry, inputs):
        state, prev_rows, prev_ids = carry
        rows, ids = inputs
        ext = jnp.concatenate([prev_rows, rows], axis=1).astype(jnp.float32)
        ids_ext = jnp.concatenate([prev_ids, ids])
        conv = short_conv(ext, ids_ext, short_taps)
        gated = (conv[1] * conv[2]).astype(jnp.bfloat16)
        gated_f = gated.astype(jnp.float32)
        prev_last = prev_ids[width - 1]
        long_part, ends = mode_terms(gated_f, ids, rates, residues)
        long_all = long_part + incoming(state, ids, prev_last, rates, residues)
        mixed = (conv[0] * (long_all + skip_gain[None] * gated_f)).astype(jnp.bfloat16)
        new_state = transition(ids, prev_last, rates) * state + ends
        return (new_state, rows[:, TOK_DEV - width:], ids[TOK_DEV - width:]), mixed

    start = (jnp.zeros((ORDER, D), jnp.float32), jnp.zeros((3, width, D), jnp.bfloat16), jnp.zeros((width,), jnp.int32))
    _, outs = lax.scan(step, start, (stacked, ids_blocks))
    return outs.reshape(TOKENS, D)
```

```python
import functools

import jax
import jax.numpy as jnp
from jax import lax
from jax.experimental import pallas as pl
from jax.experimental.pallas import tpu as pltpu
from jax.sharding import PartitionSpec as P

LANES = 128
ROWS = 8
INFO = 32
F32 = jnp.float32
BF16 = jnp.bfloat16


def rounded(value):
    return value.astype(BF16).astype(F32)


def row_index(rows=ROWS):
    return lax.broadcasted_iota(jnp.int32, (rows, LANES), 0)


def shift_rows(tile, rolled_before, row, steps):
    rolled = pltpu.roll(tile, steps, 0)
    return jnp.where(row < steps, rolled_before, rolled), rolled


def ends_kernel(ids_ref, q_ref, k_ref, v_ref, taps_ref, rates_ref, info_ref, halo_ref, ids_s, one_s, two_s, last_s):
    tokens, width = k_ref.shape
    tiles = tokens // ROWS
    wide = info_ref.shape[2]
    row = row_index()

    @pl.when(pl.program_id(0) == 0)
    def _():
        ids = jnp.broadcast_to(ids_ref[...].astype(F32), (tokens, tokens)).T[:, :LANES]
        ids_s[...] = ids
        place = row_index(tokens)
        one_s[...] = (ids == pltpu.roll(ids, 1, 0)).astype(F32)
        two_s[...] = (ids == pltpu.roll(ids, 2, 0)).astype(F32)
        same = (ids == ids[tokens - 1 : tokens]).astype(F32)
        last_s[...] = jnp.where(place >= 2, same, 0.0)

    for group in range(width // LANES):
        lanes = pl.ds(group * LANES, LANES)
        rates = rates_ref[:, lanes]
        order = rates.shape[0]
        decay = [jnp.broadcast_to(jnp.exp(-ROWS * rates[n : n + 1]), (ROWS, LANES)) for n in range(order)]
        taps = [
            [jnp.broadcast_to(taps_ref[s, j : j + 1, lanes], (ROWS, LANES)) for j in range(3)] for s in (1, 2)
        ]
        zero = jnp.zeros((ROWS, LANES), F32)
        before = [[zero, zero], [zero, zero]]
        ends = [zero] * order
        heads, tails = [None, None], [None, None]
        for pair in range(tiles // 2):
            both = [ref[pl.ds(pair * 2 * ROWS, 2 * ROWS), lanes].astype(F32) for ref in (k_ref, v_ref)]
            products = []
            for half in range(2):
                at = pl.ds((pair * 2 + half) * ROWS, ROWS)
                one, two = one_s[at], two_s[at]
                conv = []
                for s in range(2):
                    tile = both[s][half * ROWS : (half + 1) * ROWS]
                    if pair == 0 and half == 0:
                        heads[s] = tile
                    tails[s] = tile
                    back1, before[s][0] = shift_rows(tile, before[s][0], row, 1)
                    back2, before[s][1] = shift_rows(tile, before[s][1], row, 2)
                    conv.append(taps[s][0] * tile + taps[s][1] * (back1 * one) + taps[s][2] * (back2 * two))
                products.append(conv[0] * conv[1])
            gated = rounded(jnp.concatenate(products, axis=0))
            for half in range(2):
                at = pl.ds((pair * 2 + half) * ROWS, ROWS)
                part = gated[half * ROWS : (half + 1) * ROWS] * last_s[at]
                ends = [ends[n] * decay[n] + part for n in range(order)]
        left = (ROWS - 1 - row).astype(F32)
        state = zero
        for n in range(order):
            weight = jnp.exp(-left * jnp.broadcast_to(rates[n : n + 1], (ROWS, LANES)))
            total = jnp.sum(ends[n] * weight, axis=0, keepdims=True)
            state = jnp.where(row == n, total, state)
        high = rounded(state)
        first_ids, last_ids = ids_s[pl.ds(0, ROWS)], ids_s[pl.ds(tokens - ROWS, ROWS)]
        edge = jnp.where(row < 2, heads[0], pltpu.roll(heads[1], 2, 0))
        edge = jnp.where(row < 4, edge, pltpu.roll(tails[0], ROWS - 2, 0))
        edge = jnp.where(row < 6, edge, tails[1])
        marks = jnp.where(row < 2, first_ids, pltpu.roll(last_ids, 4, 0))
        marks = jnp.where(row < 4, marks, 0.0)
        chunk, inner = (group * LANES) // wide, pl.ds((group * LANES) % wide, LANES)
        info_ref[chunk, pl.ds(0, 16), inner] = jnp.concatenate([high, state - high], axis=0).astype(BF16)
        info_ref[chunk, pl.ds(16, 16), inner] = jnp.concatenate([edge, marks], axis=0).astype(BF16)
        q_tail = q_ref[:, lanes].astype(F32)[ROWS:]
        halo = jnp.where(row < 2, pltpu.roll(q_tail, 2, 0), pltpu.roll(tails[0], 4, 0))
        halo = jnp.where(row < 4, halo, pltpu.roll(tails[1], 6, 0))
        halo = jnp.where(row < 6, halo, last_ids)
        halo_ref[:, lanes] = jnp.concatenate([halo, zero], axis=0).astype(BF16)


def carry_kernel(info_ref, taps_ref, rates_ref, out_ref, *, tokens):
    rates = rates_ref[...]
    order, wide = rates.shape
    whole = jnp.exp(-float(tokens) * rates)
    far = jnp.exp(-float(tokens - 1) * rates)
    near = jnp.exp(-float(tokens - 2) * rates)
    taps = [[taps_ref[s, j : j + 1] for j in range(3)] for s in (1, 2)]
    blocks = out_ref.shape[0]
    state = jnp.zeros((order, wide), F32)
    nothing = jnp.zeros((1, wide), F32)
    tails, prev0, prev1 = [[nothing, nothing], [nothing, nothing]], nothing - 1.0, nothing - 1.0
    for block in range(blocks):
        info = info_ref[block].astype(F32)
        ends = info[0:8] + info[8:16]
        first0, first1, last0, last1 = (info[24 + i : 25 + i] for i in range(4))
        factors0, factors1 = [], []
        for s in range(2):
            head0, head1 = info[16 + 2 * s : 17 + 2 * s], info[17 + 2 * s : 18 + 2 * s]
            tail0, tail1 = tails[s]
            factors0.append(
                taps[s][0] * head0
                + taps[s][1] * jnp.where(prev1 == first0, tail1, 0.0)
                + taps[s][2] * jnp.where(prev0 == first0, tail0, 0.0)
            )
            factors1.append(
                taps[s][0] * head1
                + taps[s][1] * jnp.where(first0 == first1, head0, 0.0)
                + taps[s][2] * jnp.where(prev1 == first1, tail1, 0.0)
            )
            tails[s] = [info[20 + 2 * s : 21 + 2 * s], info[21 + 2 * s : 22 + 2 * s]]
        gated0 = jnp.where(first0 == last1, rounded(factors0[0] * factors0[1]), 0.0)
        gated1 = jnp.where(first1 == last1, rounded(factors1[0] * factors1[1]), 0.0)
        out_ref[block] = state * (prev1 == first0).astype(F32)
        state = state * (whole * (prev1 == last1).astype(F32)) + (ends + far * gated0 + near * gated1)
        prev0, prev1 = last0, last1


def local_kernel(
    ids_ref, halo_ref, q_ref, k_ref, v_ref, taps_ref, rates_ref, resid_ref, skip_ref, part_ref, query_ref,
    q_s, k_s, v_s, rates_s, resid_s, row_s,
):
    tokens, width = k_ref.shape
    groups = width // LANES
    order = rates_ref.shape[0]
    pitch = tokens + ROWS
    first = ids_ref[0].astype(F32)
    for group in range(groups):
        lanes = pl.ds(group * LANES, LANES)
        halo = halo_ref[:, lanes].astype(F32)[:ROWS]
        for ref, scratch, steps in ((q_ref, q_s, 6), (k_ref, k_s, 4), (v_ref, v_s, 2)):
            scratch[pl.ds(group * pitch, ROWS)] = jnp.where(halo == first, pltpu.roll(halo, steps, 0), 0.0)
            for pair in range(tokens // (2 * ROWS)):
                at = pair * 2 * ROWS
                scratch[pl.ds(group * pitch + ROWS + at, 2 * ROWS)] = ref[pl.ds(at, 2 * ROWS), lanes].astype(F32)
        rates_s[pl.ds(group * order, order)] = jnp.exp(-rates_ref[:, lanes])
        resid_s[pl.ds(group * order, order)] = resid_ref[:, lanes]
        for s in range(3):
            for j in range(3):
                row_s[pl.ds((s * 3 + j) * groups + group, 1)] = taps_ref[s, j : j + 1, lanes]
        row_s[pl.ds(9 * groups + group, 1)] = skip_ref[:, lanes]

    decay = [rates_s[pl.ds(n, groups, stride=order)] for n in range(order)]
    resid = [resid_s[pl.ds(n, groups, stride=order)] for n in range(order)]
    taps = [[row_s[pl.ds((s * 3 + j) * groups, groups)] for j in range(3)] for s in range(3)]
    skip = row_s[pl.ds(9 * groups, groups)]
    scratches = (q_s, k_s, v_s)

    def token(t, carry):
        before, states = carry
        here = ids_ref[t]
        same1 = (here == ids_ref[jnp.maximum(t - 1, 0)]).astype(F32)
        same2 = (here == ids_ref[jnp.maximum(t - 2, 0)]).astype(F32)
        live = (here == ids_ref[0]).astype(F32)
        conv, after = [], []
        for s in range(3):
            now = scratches[s][pl.ds(t + ROWS, groups, stride=pitch)]
            back1, back2 = before[s]
            conv.append(taps[s][0] * now + taps[s][1] * (back1 * same1) + taps[s][2] * (back2 * same2))
            after.append((now, back1))
        gated = rounded(conv[1] * conv[2])
        states = [states[n] * same1 * decay[n] + gated for n in range(order)]
        terms = [states[n] * resid[n] for n in range(order)]
        while len(terms) > 1:
            terms = [sum(terms[i : i + 2]) for i in range(0, len(terms), 2)]
        part_ref[pl.ds(t, groups, stride=tokens)] = conv[0] * (terms[0] + skip * gated)
        query_ref[pl.ds(t, groups, stride=tokens)] = conv[0] * live
        return after, states

    def chunk(c, carry):
        for i in range(ROWS):
            carry = token(c * ROWS + i, carry)
        return carry

    before = [
        tuple(scratch[pl.ds(ROWS - j, groups, stride=pitch)] for j in (1, 2)) for scratch in scratches
    ]
    zero = jnp.zeros((groups, LANES), F32)
    lax.fori_loop(0, tokens // ROWS, chunk, (before, [zero] * order))


def finish_kernel(state_ref, part_ref, query_ref, rates_ref, resid_ref, out_ref):
    tokens, width = out_ref.shape
    wide = state_ref.shape[2]
    row = row_index()
    places = (row + 1).astype(F32)
    for group in range(width // LANES):
        lanes = pl.ds(group * LANES, LANES)
        rates = rates_ref[:, lanes]
        order = rates.shape[0]
        chunk, inner = (group * LANES) // wide, pl.ds((group * LANES) % wide, LANES)
        start = state_ref[chunk, :, inner] * resid_ref[:, lanes]
        stride = jnp.exp(-ROWS * rates)
        decay, weights = [], []
        for n in range(order):
            rate = jnp.broadcast_to(rates[n : n + 1], (ROWS, LANES))
            decay.append(jnp.broadcast_to(stride[n : n + 1], (ROWS, LANES)))
            weights.append(jnp.exp(-rate * places) * jnp.broadcast_to(start[n : n + 1], (ROWS, LANES)))
        for pair in range(tokens // (2 * ROWS)):
            done = []
            for half in range(2):
                at = pl.ds(group * tokens + (pair * 2 + half) * ROWS, ROWS)
                terms = list(weights)
                while len(terms) > 1:
                    terms = [sum(terms[i : i + 2]) for i in range(0, len(terms), 2)]
                done.append(part_ref[at] + query_ref[at] * terms[0])
                weights = [weights[n] * decay[n] for n in range(order)]
            out_ref[pl.ds(pair * 2 * ROWS, 2 * ROWS), lanes] = jnp.concatenate(done, axis=0).astype(BF16)


def on_device(query, keyed, valued, short_taps, rates, residues, skip_gain, doc_ids):
    tokens, channels = query.shape
    order = rates.shape[0]
    n_ctx = lax.axis_size("ctx")
    own = channels // n_ctx
    wide = own if own % LANES == 0 else LANES
    chunks = channels // wide
    width = min(channels, 8 * LANES)
    steps = channels // width
    groups = width // LANES
    params = pltpu.CompilerParams(vmem_limit_bytes=32 * 1024 * 1024)

    def stream(rows=tokens, at=0):
        return pl.BlockSpec((rows, width), lambda i: (at, i))

    taps_spec = pl.BlockSpec((3, 3, width), lambda i: (0, 0, i))
    modes_spec = pl.BlockSpec((order, width), lambda i: (0, i))
    wide_spec = lambda rows: pl.BlockSpec((width // wide, rows, wide), lambda i: (i, 0, 0))
    halo_spec = pl.BlockSpec((2 * ROWS, width), lambda i: (0, i))
    tall_spec = pl.BlockSpec((groups * tokens, LANES), lambda i: (i, 0))

    info, halo = pl.pallas_call(
        ends_kernel,
        grid=(steps,),
        in_specs=[
            pl.BlockSpec((1, tokens), lambda i: (0, 0)),
            stream(2 * ROWS, tokens // (2 * ROWS) - 1),
            stream(),
            stream(),
            taps_spec,
            modes_spec,
        ],
        out_specs=[wide_spec(INFO), halo_spec],
        out_shape=[
            jax.ShapeDtypeStruct((chunks, INFO, wide), BF16),
            jax.ShapeDtypeStruct((2 * ROWS, channels), BF16),
        ],
        scratch_shapes=[pltpu.VMEM((tokens, LANES), F32)] * 4,
        compiler_params=params,
        name="block_ends",
    )(doc_ids.reshape(1, tokens), query, keyed, valued, short_taps, rates)

    if wide != own:
        info = info.transpose(1, 0, 2).reshape(INFO, n_ctx, own).transpose(1, 0, 2)
    info = lax.all_to_all(info, "ctx", split_axis=0, concat_axis=0, tiled=True)
    halo = lax.ppermute(halo, "ctx", [(i, i + 1) for i in range(n_ctx - 1)])

    part, masked_query = pl.pallas_call(
        local_kernel,
        grid=(steps,),
        in_specs=[
            pl.BlockSpec(memory_space=pltpu.SMEM),
            halo_spec,
            stream(),
            stream(),
            stream(),
            taps_spec,
            modes_spec,
            modes_spec,
            pl.BlockSpec((1, width), lambda i: (0, i)),
        ],
        out_specs=[tall_spec, tall_spec],
        out_shape=[jax.ShapeDtypeStruct((channels // LANES * tokens, LANES), F32)] * 2,
        scratch_shapes=[pltpu.VMEM((groups * (tokens + ROWS), LANES), F32)] * 3
        + [pltpu.VMEM((groups * order, LANES), F32)] * 2
        + [pltpu.VMEM((10 * groups, LANES), F32)],
        compiler_params=params,
        cost_estimate=pl.CostEstimate(flops=tokens * channels * 64, bytes_accessed=tokens * channels * 14, transcendentals=0),
        name="local_scan",
    )(doc_ids, halo, query, keyed, valued, short_taps, rates, residues, skip_gain.reshape(1, channels))

    at = lax.axis_index("ctx") * own
    own_taps = lax.dynamic_slice_in_dim(short_taps, at, own, 2)
    own_rates = lax.dynamic_slice_in_dim(rates, at, own, 1)
    state = pl.pallas_call(
        functools.partial(carry_kernel, tokens=tokens),
        out_shape=jax.ShapeDtypeStruct((n_ctx, order, own), F32),
        name="block_carry",
    )(info, own_taps, own_rates)
    state = lax.all_to_all(state, "ctx", split_axis=0, concat_axis=0, tiled=True)
    if wide != own:
        state = state.transpose(1, 0, 2).reshape(order, chunks, wide).transpose(1, 0, 2)

    return pl.pallas_call(
        finish_kernel,
        grid=(steps,),
        in_specs=[wide_spec(order), tall_spec, tall_spec, modes_spec, modes_spec],
        out_specs=stream(),
        out_shape=jax.ShapeDtypeStruct((tokens, channels), BF16),
        compiler_params=params,
        name="add_carry",
    )(state, part, masked_query, rates, residues)


def solution(mesh):
    return jax.shard_map(
        on_device,
        mesh=mesh,
        in_specs=(
            P("ctx", "tp"),
            P("ctx", "tp"),
            P("ctx", "tp"),
            P(None, None, "tp"),
            P(None, "tp"),
            P(None, "tp"),
            P("tp"),
            P("ctx"),
        ),
        out_specs=P("ctx", "tp"),
        check_vma=False,
    )
```

```python
import functools

import jax
import jax.numpy as jnp
from jax import lax
from jax.experimental import pallas as pl
from jax.experimental.pallas import tpu as pltpu
from jax.sharding import PartitionSpec as P

LANES = 128
ROWS = 8
INFO = 32
TOLD = 24
F32 = jnp.float32
BF16 = jnp.bfloat16


def rounded(value):
    return value.astype(BF16).astype(F32)


def row_index(rows=ROWS):
    return lax.broadcasted_iota(jnp.int32, (rows, LANES), 0)


def block_at(index, size):
    start = index * size
    return pl.ds(start if isinstance(start, int) else pl.multiple_of(start, size), size)


def lanes_at(index, size, group):
    start = index * size + group * LANES
    return pl.ds(start if isinstance(start, int) else pl.multiple_of(start, LANES), LANES)


def columns(source, target, sems, width):
    return lambda i: pltpu.make_async_copy(
        source.at[..., block_at(i, width)], target.at[..., block_at(i, width)], sems.at[i]
    )


def across(scratch, rows_of):
    rows = scratch.shape[0] // rows_of.groups
    for group in range(rows_of.groups):
        scratch[pl.ds(group * rows, rows)] = rows_of(group)
    return [scratch[pl.ds(n, rows_of.groups, stride=rows)] for n in range(rows)]


class Rows:
    def __init__(self, ref, step, width):
        self.ref, self.step, self.width, self.groups = ref, step, width, width // LANES

    def __call__(self, group):
        return self.ref[..., lanes_at(self.step, self.width, group)]


def across_taps(scratch, rows_of, streams):
    groups = rows_of.groups
    for group in range(groups):
        taps = rows_of(group)
        for s in streams:
            for j in range(3):
                scratch[pl.ds((s * 3 + j) * groups + group, 1)] = taps[s, j : j + 1]
    return [[scratch[pl.ds((s * 3 + j) * groups, groups)] for j in range(3)] for s in streams]


def fill(scratch, base, pitch, rows_of):
    tokens = rows_of.ref.shape[0]
    for group in range(rows_of.groups):
        lanes = lanes_at(rows_of.step, rows_of.width, group)
        for at in range(0, tokens, 2 * ROWS):
            scratch[pl.ds(base + group * pitch + at, 2 * ROWS)] = rows_of.ref[pl.ds(at, 2 * ROWS), lanes].astype(F32)


def summed(terms):
    while len(terms) > 1:
        terms = [sum(terms[i : i + 2]) for i in range(0, len(terms), 2)]
    return terms[0]


def ends_kernel(
    width, ids_ref, q_hbm, k_hbm, v_hbm, taps_hbm, rates_hbm,
    info_hbm,
    q_v, k_v, v_v, taps_v, rates_v, info_v, k_ref, v_ref, modes_s, taps_s, sems,
):
    tokens, channels = k_v.shape
    steps = channels // width
    groups = width // LANES
    pitch = k_ref.shape[0] // groups
    wide = info_v.shape[2]
    per_step = width // wide
    order = rates_v.shape[0]
    coming = [
        columns(source, target, sems.at[i], width)
        for i, (source, target) in enumerate(
            (
                (k_hbm, k_v),
                (v_hbm, v_v),
                (rates_hbm, rates_v),
                (taps_hbm, taps_v),
                (q_hbm.at[pl.ds(0, 2 * ROWS)], q_v.at[0]),
                (q_hbm.at[pl.ds(tokens - 2 * ROWS, 2 * ROWS)], q_v.at[1]),
            )
        )
    ]
    going = lambda i: pltpu.make_async_copy(
        info_v.at[block_at(i, per_step)], info_hbm.at[block_at(i, per_step)], sems.at[6, i]
    )
    for i in range(steps):
        for copy in coming:
            copy(i).start()
    last = ids_ref[tokens - 1]
    row = row_index()
    marks = jnp.zeros((ROWS, LANES), F32)
    for i, t in enumerate((0, 1, tokens - 2, tokens - 1)):
        marks = jnp.where(row == i + 4, ids_ref[t].astype(F32), marks)

    def step(i, _):
        for copy in coming:
            copy(i).wait()
        base = 0
        fill(k_ref, base, pitch, Rows(k_v, i, width))
        fill(v_ref, base, pitch, Rows(v_v, i, width))
        decay = [jnp.exp(-rate) for rate in across(modes_s, Rows(rates_v, i, width))]
        taps = across_taps(taps_s, Rows(taps_v, i, width), (1, 2))

        def rows(t):
            live = (ids_ref[t] == last).astype(F32)
            return [ref[pl.ds(base + t, groups, stride=pitch)] * live for ref in (k_ref, v_ref)]

        def token(t, carry):
            back1, back2, ends = carry
            here = rows(t)
            conv = [taps[s][0] * here[s] + taps[s][1] * back1[s] + taps[s][2] * back2[s] for s in range(2)]
            gated = rounded(conv[0] * conv[1])
            return here, back1, [ends[n] * decay[n] + gated for n in range(order)]

        def chunk(c, carry):
            for j in range(ROWS):
                carry = token(c * ROWS + j, carry)
            return carry

        carry = (rows(1), rows(0), [jnp.zeros((groups, LANES), F32)] * order)
        for t in range(2, ROWS):
            carry = token(t, carry)
        ends = lax.fori_loop(1, tokens // ROWS, chunk, carry)[2]
        for n in range(order):
            modes_s[pl.ds(n, groups, stride=order)] = ends[n]

        for group in range(groups):
            lanes = lanes_at(i, width, group)
            state = modes_s[pl.ds(group * order, order)]
            high = rounded(state)
            heads = [ref[pl.ds(base + group * pitch, ROWS)] for ref in (k_ref, v_ref)]
            tails = [ref[pl.ds(base + group * pitch + tokens - ROWS, ROWS)] for ref in (k_ref, v_ref)]
            edge = jnp.where(row < 2, heads[0], pltpu.roll(heads[1], 2, 0))
            edge = jnp.where(row < 4, edge, pltpu.roll(tails[0], ROWS - 2, 0))
            edge = jnp.where(row < 6, edge, tails[1])
            at = i * per_step + (group * LANES) // wide
            inner = pl.ds((group * LANES) % wide, LANES)
            info_v[at, pl.ds(0, 16), inner] = jnp.concatenate([high, state - high], axis=0).astype(BF16)
            q_head, q_tail = (q_v[j, :, lanes].astype(F32) for j in range(2))
            more = jnp.where(row < 2, q_head[:ROWS], pltpu.roll(q_tail[ROWS:], 4, 0))
            more = jnp.where(row < 4, more, marks)
            info_v[at, pl.ds(16, 16), inner] = jnp.concatenate([edge, more], axis=0).astype(BF16)
        going(i).start()
        return 0

    lax.fori_loop(0, steps, step, 0)
    for i in range(steps):
        going(i).wait()


def carry_kernel(info_ref, taps_ref, rates_ref, resid_ref, skip_ref, out_ref, *, tokens):
    rates, resid, skip = rates_ref[...], resid_ref[...], skip_ref[...]
    order, wide = rates.shape
    decay = jnp.exp(-rates)
    rest = jnp.exp(-float(tokens - 2) * rates)
    taps = [[taps_ref[s, j : j + 1] for j in range(3)] for s in (1, 2, 0)]
    nothing = jnp.zeros((1, wide), F32)
    state = jnp.zeros((order, wide), F32)
    tails, prev0, prev1 = [[nothing, nothing]] * 3, nothing - 1.0, nothing - 1.0
    for block in range(out_ref.shape[0]):
        info = info_ref[block].astype(F32)
        ends = info[0:8] + info[8:16]
        line = lambda i: info[i : i + 1]
        heads = [[line(16), line(17)], [line(18), line(19)], [line(24), line(25)]]
        first0, first1, last0, last1 = (line(28 + i) for i in range(4))
        conv0, conv1 = [], []
        for s in range(3):
            (head0, head1), (tail0, tail1) = heads[s], tails[s]
            conv0.append(
                taps[s][0] * head0
                + taps[s][1] * jnp.where(prev1 == first0, tail1, 0.0)
                + taps[s][2] * jnp.where(prev0 == first0, tail0, 0.0)
            )
            conv1.append(
                taps[s][0] * head1
                + taps[s][1] * jnp.where(first0 == first1, head0, 0.0)
                + taps[s][2] * jnp.where(prev1 == first1, tail1, 0.0)
            )
        gated0, gated1 = rounded(conv0[0] * conv0[1]), rounded(conv1[0] * conv1[1])
        state0 = decay * (state * (prev1 == first0).astype(F32)) + gated0
        state1 = decay * (state0 * (first0 == first1).astype(F32)) + gated1
        long0 = jnp.sum(resid * state0, axis=0, keepdims=True)
        long1 = jnp.sum(resid * state1, axis=0, keepdims=True)
        row = lax.broadcasted_iota(jnp.int32, (order, wide), 0)
        mixed = jnp.where(row == 0, conv0[2] * (long0 + skip * gated0), conv1[2] * (long1 + skip * gated1))
        high = rounded(state1)
        out_ref[block, pl.ds(0, 16)] = jnp.concatenate([high, state1 - high], axis=0).astype(BF16)
        out_ref[block, pl.ds(16, 8)] = mixed.astype(BF16)
        state = ends + rest * (state1 * (first1 == last1).astype(F32))
        tails = [[line(20), line(21)], [line(22), line(23)], [line(26), line(27)]]
        prev0, prev1 = last0, last1


def local_kernel(width, first_step, count, ids_ref, q_hbm, k_hbm, v_hbm, taps_hbm, rates_hbm, resid_hbm, skip_hbm, *rest):
    (
        part_ref, query_ref, table_ref,
        q_v, k_v, v_v, taps_v, rates_v, resid_v, skip_v, q_s, k_s, v_s, modes_s, taps_s, sems,
    ) = rest[-16:]
    tokens, channels = q_v.shape
    groups = width // LANES
    pitch = q_s.shape[0] // groups
    order = rates_v.shape[0]
    coming = [
        columns(source, target, sems.at[i], width)
        for i, (source, target) in enumerate(
            (
                (q_hbm, q_v),
                (k_hbm, k_v),
                (v_hbm, v_v),
                (taps_hbm, taps_v),
                (rates_hbm, rates_v),
                (resid_hbm, resid_v),
                (skip_hbm, skip_v),
            )
        )
    ]
    for i in range(first_step, first_step + count):
        for copy in coming:
            copy(i).start()

    def step(i, _):
        for copy in coming:
            copy(i).wait()
        fill(q_s, 0, pitch, Rows(q_v, i, width))
        fill(k_s, 0, pitch, Rows(k_v, i, width))
        fill(v_s, 0, pitch, Rows(v_v, i, width))
        for group in range(groups):
            taps_s[pl.ds(9 * groups + group, 1)] = skip_v[:, lanes_at(i, width, group)]
        decay = [jnp.exp(-rate) for rate in across(modes_s, Rows(rates_v, i, width))]
        resid = across(modes_s, Rows(resid_v, i, width))
        taps = across_taps(taps_s, Rows(taps_v, i, width), (0, 1, 2))
        skip = taps_s[pl.ds(9 * groups, groups)]
        for n in range(order):
            at = i * (2 * order) + n
            table_ref[block_at(at, groups)] = decay[n]
            table_ref[block_at(at + order, groups)] = resid[n]

        def token(t, carry):
            back1, back2, states = carry
            here = ids_ref[t]
            same = (here == ids_ref[t - 1]).astype(F32)
            live = (here == ids_ref[1]).astype(F32)
            now = [ref[pl.ds(t, groups, stride=pitch)] for ref in (q_s, k_s, v_s)]
            back1 = [value * same for value in back1]
            back2 = [value * same for value in back2]
            conv = [taps[s][0] * now[s] + taps[s][1] * back1[s] + taps[s][2] * back2[s] for s in range(3)]
            gated = rounded(conv[1] * conv[2])
            states = [states[n] * same * decay[n] + gated for n in range(order)]
            total = summed([states[n] * resid[n] for n in range(order)])
            return (now, back1, states), conv[0] * (total + skip * gated), conv[0] * live

        def pair(t, carry):
            carry, part0, query0 = token(t, carry)
            carry, part1, query1 = token(t + 1, carry)
            at = block_at((i * tokens + t) // 2, 2 * groups)
            part_ref[at] = jnp.concatenate([part0, part1], axis=0).astype(BF16)
            query_ref[at] = jnp.concatenate([query0, query1], axis=0).astype(BF16)
            return carry

        def chunk(c, carry):
            for j in range(0, ROWS, 2):
                carry = pair(c * ROWS + j, carry)
            return carry

        back1, back2 = ([ref[pl.ds(t, groups, stride=pitch)] for ref in (q_s, k_s, v_s)] for t in (1, 0))
        same = (ids_ref[1] == ids_ref[0]).astype(F32)
        carry = (back1, [value * same for value in back2], [jnp.zeros((groups, LANES), F32)] * order)
        for t in range(2, ROWS, 2):
            carry = pair(t, carry)
        lax.fori_loop(1, tokens // ROWS, chunk, carry)
        return 0

    lax.fori_loop(first_step, first_step + count, step, 0)


def finish_kernel(width, state_ref, part_ref, query_ref, table_ref, out_hbm, out_v, out_s, modes_s, sems):
    tokens, channels = out_v.shape
    steps = channels // width
    groups = width // LANES
    pitch = out_s.shape[0] // groups
    wide = state_ref.shape[2]
    order = table_ref.shape[0] // (2 * groups * steps)
    going = columns(out_v, out_hbm, sems, width)

    def step(i, _):
        at = i * (2 * order)
        decay = [table_ref[block_at(at + n, groups)] for n in range(order)]
        for group in range(groups):
            chunk_at = i * (width // wide) + (group * LANES) // wide
            told = state_ref[chunk_at, :, pl.ds((group * LANES) % wide, LANES)].astype(F32)
            modes_s[pl.ds(group * 2 * order, order)] = told[0:order] + told[order : 2 * order]
            modes_s[pl.ds(group * 2 * order + order, order)] = told[2 * order :]
        weights = [
            modes_s[pl.ds(n, groups, stride=2 * order)] * table_ref[block_at(at + order + n, groups)] for n in range(order)
        ]

        def pair(t, weights):
            at = block_at((i * tokens + t) // 2, 2 * groups)
            part, live_query = part_ref[at].astype(F32), query_ref[at].astype(F32)
            for k in range(2):
                weights = [weights[n] * decay[n] for n in range(order)]
                rows = slice(k * groups, (k + 1) * groups)
                out_s[pl.ds(t + k, groups, stride=pitch)] = part[rows] + live_query[rows] * summed(weights)
            return weights

        def chunk(c, weights):
            for j in range(0, ROWS, 2):
                weights = pair(c * ROWS + j, weights)
            return weights

        for t in range(2):
            out_s[pl.ds(t, groups, stride=pitch)] = modes_s[pl.ds(order + t, groups, stride=2 * order)]
        for t in range(2, ROWS, 2):
            weights = pair(t, weights)
        lax.fori_loop(1, tokens // ROWS, chunk, weights)
        for group in range(groups):
            for at in range(0, tokens, 2 * ROWS):
                out_v[pl.ds(at, 2 * ROWS), lanes_at(i, width, group)] = out_s[
                    pl.ds(group * pitch + at, 2 * ROWS)
                ].astype(BF16)
        going(i).start()
        return 0

    lax.fori_loop(0, steps, step, 0)
    for i in range(steps):
        going(i).wait()


def on_device(query, keyed, valued, short_taps, rates, residues, skip_gain, doc_ids):
    tokens, channels = query.shape
    order = rates.shape[0]
    n_ctx = lax.axis_size("ctx")
    own = channels // n_ctx
    wide = own if own % LANES == 0 else LANES
    chunks = channels // wide
    width = min(channels, 8 * LANES)
    steps = channels // width
    groups = width // LANES
    pitch = tokens + ROWS
    params = pltpu.CompilerParams(vmem_limit_bytes=24 * 1024 * 1024)
    anywhere = pl.BlockSpec(memory_space=pl.ANY)
    smem = pl.BlockSpec(memory_space=pltpu.SMEM)
    vmem = pl.BlockSpec(memory_space=pltpu.VMEM)
    hbm = lambda *arrays: [pltpu.with_memory_space_constraint(array, pltpu.HBM) for array in arrays]
    near = lambda *arrays: [pltpu.with_memory_space_constraint(array, pltpu.VMEM) for array in arrays]

    modes_scratch = pltpu.VMEM((groups * order, LANES), F32)
    skip_gain = skip_gain.reshape(1, channels)
    apart = pltpu.VMEM((groups * pitch, LANES), F32)
    tall = [pltpu.VMEM((channels // LANES * tokens, LANES), dtype) for dtype in (BF16, BF16)]
    table = pltpu.VMEM((steps * 2 * order * groups, LANES), F32)
    taps_v, modes_v = pltpu.VMEM((3, 3, channels), F32), pltpu.VMEM((order, channels), F32)

    info = pl.pallas_call(
        functools.partial(ends_kernel, width),
        in_specs=[smem] + [anywhere] * 5,
        out_specs=anywhere,
        out_shape=pltpu.HBM((chunks, INFO, wide), BF16),
        scratch_shapes=[
            pltpu.VMEM((2, 2 * ROWS, channels), BF16),
            pltpu.VMEM((tokens, channels), BF16),
            pltpu.VMEM((tokens, channels), BF16),
            taps_v,
            modes_v,
            pltpu.VMEM((chunks, INFO, wide), BF16),
            apart,
            apart,
            modes_scratch,
            pltpu.VMEM((9 * groups, LANES), F32),
            pltpu.SemaphoreType.DMA((7, steps)),
        ],
        compiler_params=params,
        name="block_ends",
    )(*hbm(doc_ids, query, keyed, valued, short_taps, rates))

    if wide != own:
        info = info.transpose(1, 0, 2).reshape(INFO, n_ctx, own).transpose(1, 0, 2)
    info = lax.all_to_all(info, "ctx", split_axis=0, concat_axis=0, tiled=True)

    def local_scan(first, count, filled):
        return pl.pallas_call(
            functools.partial(local_kernel, width, first, count),
            in_specs=[smem] + [anywhere] * 7 + [vmem] * len(filled),
            out_specs=[vmem] * 3,
            out_shape=[*tall, table],
            input_output_aliases={8 + i: i for i in range(len(filled))},
            scratch_shapes=[
                pltpu.VMEM((tokens, channels), BF16),
                pltpu.VMEM((tokens, channels), BF16),
                pltpu.VMEM((tokens, channels), BF16),
                taps_v,
                modes_v,
                modes_v,
                pltpu.VMEM((1, channels), F32),
                apart,
                apart,
                apart,
                modes_scratch,
                pltpu.VMEM((10 * groups, LANES), F32),
                pltpu.SemaphoreType.DMA((7, steps)),
            ],
            compiler_params=params,
            cost_estimate=pl.CostEstimate(
                flops=count * tokens * width * 64, bytes_accessed=count * tokens * width * 14, transcendentals=0
            ),
            name="local_scan",
        )(
            *hbm(doc_ids, query, keyed, valued, short_taps, rates, residues, skip_gain), *near(*filled),
        )

    half = steps // 2 or steps
    filled = local_scan(0, half, [])
    info, *filled = lax.optimization_barrier((info, *filled))
    at = lax.axis_index("ctx") * own
    own_taps = lax.dynamic_slice_in_dim(short_taps, at, own, 2)
    own_modes = [lax.dynamic_slice_in_dim(value, at, own, 1) for value in (rates, residues, skip_gain)]
    state = pl.pallas_call(
        functools.partial(carry_kernel, tokens=tokens),
        out_shape=pltpu.HBM((n_ctx, TOLD, own), BF16),
        compiler_params=params,
        name="block_carry",
    )(*near(info, own_taps, *own_modes))
    state, *filled = lax.optimization_barrier((state, *filled))
    state = lax.all_to_all(state, "ctx", split_axis=0, concat_axis=0, tiled=True)
    if half < steps:
        filled = local_scan(half, steps - half, filled)
    if wide != own:
        state = state.transpose(1, 0, 2).reshape(TOLD, chunks, wide).transpose(1, 0, 2)

    return pl.pallas_call(
        functools.partial(finish_kernel, width),
        in_specs=[vmem] * 4,
        out_specs=anywhere,
        out_shape=pltpu.HBM((tokens, channels), BF16),
        scratch_shapes=[
            pltpu.VMEM((tokens, channels), BF16),
            pltpu.VMEM((groups * pitch, LANES), F32),
            pltpu.VMEM((2 * groups * order, LANES), F32),
            pltpu.SemaphoreType.DMA((steps,)),
        ],
        compiler_params=params,
        name="add_carry",
    )(*near(state, *filled))


def solution(mesh):
    return jax.shard_map(
        on_device,
        mesh=mesh,
        in_specs=(
            P("ctx", "tp"),
            P("ctx", "tp"),
            P("ctx", "tp"),
            P(None, None, "tp"),
            P(None, "tp"),
            P(None, "tp"),
            P("tp"),
            P("ctx"),
        ),
        out_specs=P("ctx", "tp"),
        check_vma=False,
    )
```

```python
import functools

import jax
import jax.numpy as jnp
from jax import lax
from jax.experimental import pallas as pl
from jax.experimental.pallas import tpu as pltpu
from jax.sharding import PartitionSpec as P

LANES = 128
ROWS = 8
CHUNK = 16
INFO = 32
TOLD = 24
F32 = jnp.float32
BF16 = jnp.bfloat16


def rounded(value):
    return value.astype(BF16).astype(F32)


def row_index(rows=ROWS):
    return lax.broadcasted_iota(jnp.int32, (rows, LANES), 0)


def block_at(index, size):
    start = index * size
    return pl.ds(start if isinstance(start, int) else pl.multiple_of(start, size), size)


def lanes_at(index, size, group):
    start = index * size + group * LANES
    return pl.ds(start if isinstance(start, int) else pl.multiple_of(start, LANES), LANES)


def columns(source, target, sems, width):
    return lambda i: pltpu.make_async_copy(
        source.at[..., block_at(i, width)], target.at[..., block_at(i, width)], sems.at[i]
    )


def across(scratch, rows_of):
    rows = scratch.shape[0] // rows_of.groups
    for group in range(rows_of.groups):
        scratch[pl.ds(group * rows, rows)] = rows_of(group)
    return [scratch[pl.ds(n, rows_of.groups, stride=rows)] for n in range(rows)]


class Rows:
    def __init__(self, ref, step, width):
        self.ref, self.step, self.width, self.groups = ref, step, width, width // LANES

    def __call__(self, group):
        return self.ref[..., lanes_at(self.step, self.width, group)]


def across_taps(scratch, rows_of, streams):
    groups = rows_of.groups
    for group in range(groups):
        taps = rows_of(group)
        for s in streams:
            for j in range(3):
                scratch[pl.ds((s * 3 + j) * groups + group, 1)] = taps[s, j : j + 1]
    return [[scratch[pl.ds((s * 3 + j) * groups, groups)] for j in range(3)] for s in streams]


def fill_group(scratch, base, pitch, rows_of, at, group):
    lanes = lanes_at(rows_of.step, rows_of.width, group)
    scratch[pl.ds(base + group * pitch + at, CHUNK)] = rows_of.ref[pl.ds(at, CHUNK), lanes].astype(F32)


def fills(scratches, refs, base, pitch, step, width, at):
    return [
        functools.partial(fill_group, scratch, base, pitch, Rows(ref, step, width), at, group)
        for scratch, ref in zip(scratches, refs)
        for group in range(width // LANES)
    ]


def share(calls, j):
    for call in calls[len(calls) * j // CHUNK : len(calls) * (j + 1) // CHUNK]:
        call()


def first_of_last(ids_ref):
    tokens = ids_ref.shape[0]
    low, high = jnp.int32(0), jnp.int32(tokens - 1)
    last = ids_ref[tokens - 1]
    for _ in range((tokens - 1).bit_length()):
        middle = (low + high) // 2
        same = ids_ref[middle] == last
        low, high = jnp.where(same, low, middle + 1), jnp.where(same, middle, high)
    return high


def summed(terms):
    while len(terms) > 1:
        terms = [sum(terms[i : i + 2]) for i in range(0, len(terms), 2)]
    return terms[0]


def ends_kernel(
    width, ids_ref, q_hbm, k_hbm, v_hbm, taps_hbm, rates_hbm,
    info_hbm,
    q_v, k_v, v_v, taps_v, rates_v, info_v, k_s, v_s, modes_s, taps_s, sems,
):
    tokens, channels = k_v.shape
    steps = channels // width
    groups = width // LANES
    chunks = tokens // CHUNK
    pitch = k_s.shape[0] // (2 * groups)
    wide = info_v.shape[2]
    per_step = width // wide
    order = rates_v.shape[0]
    k_in, v_in = (
        columns(source, target, sems.at[pl.ds(i * steps, steps)], width)
        for i, (source, target) in enumerate(((k_hbm, k_v), (v_hbm, v_v)))
    )
    others = [
        pltpu.make_async_copy(source, target, sems.at[3 * steps + i])
        for i, (source, target) in enumerate(
            (
                (rates_hbm, rates_v),
                (taps_hbm, taps_v),
                (q_hbm.at[pl.ds(0, CHUNK)], q_v.at[0]),
                (q_hbm.at[pl.ds(tokens - CHUNK, CHUNK)], q_v.at[1]),
            )
        )
    ]
    going = lambda i: pltpu.make_async_copy(
        info_v.at[block_at(i, per_step)], info_hbm.at[block_at(i, per_step)], sems.at[2 * steps + i]
    )
    k_in(0).start()
    v_in(0).start()
    for copy in others:
        copy.start()
    for i in range(1, steps):
        k_in(i).start()
        v_in(i).start()
    begin = first_of_last(ids_ref)
    chunk0 = begin // CHUNK
    row = row_index()
    marks = jnp.zeros((ROWS, LANES), F32)
    for i, t in enumerate((0, 1, tokens - 2, tokens - 1)):
        marks = jnp.where(row == i + 4, ids_ref[t].astype(F32), marks)

    def base_of(i):
        return (i % 2) * (groups * pitch)

    def fills_of(i, at):
        return fills((k_s, v_s), (k_v, v_v), base_of(i), pitch, i, width, at)

    def arrive(i):
        k_in(i).wait()
        v_in(i).wait()

    arrive(0)

    def first_fill(c, _):
        for call in fills_of(0, pl.multiple_of(c * CHUNK, CHUNK)):
            call()
        return 0

    lax.fori_loop(chunk0, chunks, first_fill, 0)
    for copy in others:
        copy.wait()

    def step(i):
        after = min(i + 1, steps - 1)
        if i + 1 < steps:
            arrive(i + 1)

        base = base_of(i)
        decay = [jnp.exp(-rate) for rate in across(modes_s, Rows(rates_v, i, width))]
        taps = across_taps(taps_s, Rows(taps_v, i, width), (1, 2))

        def chunk(masked, c, carry):
            at = pl.multiple_of(c * CHUNK, CHUNK)
            back1, back2, ends = carry
            coming = fills_of(after, at)
            for j in range(CHUNK):
                t = at + j
                share(coming, j)
                here = [ref[pl.ds(base + t, groups, stride=pitch)] for ref in (k_s, v_s)]
                if masked:
                    live = (t >= begin).astype(F32)
                    here = [value * live for value in here]
                conv = [taps[s][0] * here[s] + taps[s][1] * back1[s] + taps[s][2] * back2[s] for s in range(2)]
                gated = rounded(conv[0] * conv[1])
                if masked and j < 2:
                    gated = gated * (t >= 2).astype(F32)
                ends = [ends[n] * decay[n] + gated for n in range(order)]
                back1, back2 = here, back1
            return back1, back2, ends

        zero = jnp.zeros((groups, LANES), F32)
        carry = chunk(True, chunk0, ([zero] * 2, [zero] * 2, [zero] * order))
        ends = lax.fori_loop(chunk0 + 1, chunks, functools.partial(chunk, False), carry)[2]
        for n in range(order):
            modes_s[pl.ds(n, groups, stride=order)] = ends[n]

        for group in range(groups):
            lanes = lanes_at(i, width, group)
            state = modes_s[pl.ds(group * order, order)]
            high = rounded(state)
            heads = [ref[pl.ds(0, CHUNK), lanes].astype(F32)[:ROWS] for ref in (k_v, v_v)]
            tails = [ref[pl.ds(tokens - CHUNK, CHUNK), lanes].astype(F32)[ROWS:] for ref in (k_v, v_v)]
            edge = jnp.where(row < 2, heads[0], pltpu.roll(heads[1], 2, 0))
            edge = jnp.where(row < 4, edge, pltpu.roll(tails[0], ROWS - 2, 0))
            edge = jnp.where(row < 6, edge, tails[1])
            at = i * per_step + (group * LANES) // wide
            inner = pl.ds((group * LANES) % wide, LANES)
            info_v[at, pl.ds(0, 16), inner] = jnp.concatenate([high, state - high], axis=0).astype(BF16)
            q_head, q_tail = (q_v[j, :, lanes].astype(F32) for j in range(2))
            more = jnp.where(row < 2, q_head[:ROWS], pltpu.roll(q_tail[ROWS:], 4, 0))
            more = jnp.where(row < 4, more, marks)
            info_v[at, pl.ds(16, 16), inner] = jnp.concatenate([edge, more], axis=0).astype(BF16)
        going(i).start()

    for i in range(steps):
        step(i)
    for i in range(steps):
        going(i).wait()


def carry_kernel(info_ref, taps_ref, rates_ref, resid_ref, skip_ref, out_ref, *, tokens):
    rates, resid, skip = rates_ref[...], resid_ref[...], skip_ref[...]
    order, wide = rates.shape
    decay = jnp.exp(-rates)
    rest = jnp.exp(-float(tokens - 2) * rates)
    taps = [[taps_ref[s, j : j + 1] for j in range(3)] for s in (1, 2, 0)]
    nothing = jnp.zeros((1, wide), F32)
    state = jnp.zeros((order, wide), F32)
    tails, prev0, prev1 = [[nothing, nothing]] * 3, nothing - 1.0, nothing - 1.0
    for block in range(out_ref.shape[0]):
        info = info_ref[block].astype(F32)
        ends = info[0:8] + info[8:16]
        line = lambda i: info[i : i + 1]
        heads = [[line(16), line(17)], [line(18), line(19)], [line(24), line(25)]]
        first0, first1, last0, last1 = (line(28 + i) for i in range(4))
        conv0, conv1 = [], []
        for s in range(3):
            (head0, head1), (tail0, tail1) = heads[s], tails[s]
            conv0.append(
                taps[s][0] * head0
                + taps[s][1] * jnp.where(prev1 == first0, tail1, 0.0)
                + taps[s][2] * jnp.where(prev0 == first0, tail0, 0.0)
            )
            conv1.append(
                taps[s][0] * head1
                + taps[s][1] * jnp.where(first0 == first1, head0, 0.0)
                + taps[s][2] * jnp.where(prev1 == first1, tail1, 0.0)
            )
        gated0, gated1 = rounded(conv0[0] * conv0[1]), rounded(conv1[0] * conv1[1])
        state0 = decay * (state * (prev1 == first0).astype(F32)) + gated0
        state1 = decay * (state0 * (first0 == first1).astype(F32)) + gated1
        long0 = jnp.sum(resid * state0, axis=0, keepdims=True)
        long1 = jnp.sum(resid * state1, axis=0, keepdims=True)
        row = lax.broadcasted_iota(jnp.int32, (order, wide), 0)
        mixed = jnp.where(row == 0, conv0[2] * (long0 + skip * gated0), conv1[2] * (long1 + skip * gated1))
        high = rounded(state1)
        out_ref[block, pl.ds(0, 16)] = jnp.concatenate([high, state1 - high], axis=0).astype(BF16)
        out_ref[block, pl.ds(16, 8)] = mixed.astype(BF16)
        state = ends + rest * (state1 * (first1 == last1).astype(F32))
        tails = [[line(20), line(21)], [line(22), line(23)], [line(26), line(27)]]
        prev0, prev1 = last0, last1


def local_kernel(
    width, first_step, count, filled, ids_ref, q_hbm, k_hbm, v_hbm, taps_hbm, rates_hbm, resid_hbm, skip_hbm, *rest
):
    (
        q_v, k_v, v_v, taps_v, rates_v, resid_v, skip_v, q_s, k_s, v_s, modes_s, taps_s, sems,
    ) = rest[-13:]
    part_ref, query_ref, table_ref, *own_refs = rest[filled:-13]
    tokens, channels = q_v.shape
    owned = []
    if own_refs:
        mine = own_refs[0].shape[-1]
        lanes = pl.ds(pl.multiple_of(lax.axis_index("ctx") * mine, mine), mine)
        owned = [
            (source.at[..., lanes], target)
            for source, target in zip((taps_hbm, rates_hbm, resid_hbm, skip_hbm), own_refs)
        ]
    groups = width // LANES
    pitch = q_s.shape[0] // (2 * groups)
    order = rates_v.shape[0]
    end_step = first_step + count
    scratches = (q_s, k_s, v_s)
    streams = [
        lambda i, s=s, source=source, target=target: pltpu.make_async_copy(
            source.at[:, block_at(i, width)], target.at[:, block_at(i, width)], sems.at[s * count + i - first_step]
        )
        for s, (source, target) in enumerate(((q_hbm, q_v), (k_hbm, k_v), (v_hbm, v_v)))
    ]
    part = pl.ds(first_step * width, count * width)
    own = [pltpu.make_async_copy(source, target, sems.at[3 * count + 4 + i]) for i, (source, target) in enumerate(owned)]
    others = [
        pltpu.make_async_copy(source.at[..., part], target.at[..., part], sems.at[3 * count + i])
        for i, (source, target) in enumerate(
            ((taps_hbm, taps_v), (rates_hbm, rates_v), (resid_hbm, resid_v), (skip_hbm, skip_v))
        )
    ]
    for i in range(first_step, end_step):
        for copy in streams:
            copy(i).start()
        if i == first_step:
            for copy in others + own:
                copy.start()

    def arrive(i):
        for copy in streams:
            copy(i).wait()

    def base_of(i):
        return pl.multiple_of((i % 2) * (groups * pitch), ROWS)

    def fills_of(i, at):
        return fills(scratches, (q_v, k_v, v_v), base_of(i), pitch, i, width, at)

    arrive(first_step)

    def first_fill(c, _):
        for call in fills_of(first_step, pl.multiple_of(c * CHUNK, CHUNK)):
            call()
        return 0

    lax.fori_loop(0, tokens // CHUNK, first_fill, 0)
    for copy in others:
        copy.wait()

    def step(i, _):
        following = jnp.minimum(i + 1, end_step - 1)

        @pl.when(i + 1 < end_step)
        def _():
            arrive(i + 1)

        base = base_of(i)
        for group in range(groups):
            taps_s[pl.ds(9 * groups + group, 1)] = skip_v[:, lanes_at(i, width, group)]
        decay = [jnp.exp(-rate) for rate in across(modes_s, Rows(rates_v, i, width))]
        resid = across(modes_s, Rows(resid_v, i, width))
        taps = across_taps(taps_s, Rows(taps_v, i, width), (0, 1, 2))
        skip = taps_s[pl.ds(9 * groups, groups)]
        for n in range(order):
            at = i * (2 * order) + n
            table_ref[block_at(at, groups)] = decay[n]
            table_ref[block_at(at + order, groups)] = resid[n]

        def row_of(ref, t):
            return ref[pl.ds(base + t, groups, stride=pitch)]

        def token(t, carry, masked):
            back1, back2, states = carry
            now = [row_of(ref, t) for ref in scratches]
            if masked:
                same = (ids_ref[t] == ids_ref[t - 1]).astype(F32)
                back1 = [value * same for value in back1]
                back2 = [value * same for value in back2]
                states = [value * same for value in states]
            conv = [taps[s][0] * now[s] + taps[s][1] * back1[s] + taps[s][2] * back2[s] for s in range(3)]
            gated = rounded(conv[1] * conv[2])
            states = [states[n] * decay[n] + gated for n in range(order)]
            total = summed([states[n] * resid[n] for n in range(order)])
            live = (ids_ref[t] == ids_ref[1]).astype(F32)
            return (now, back1, states), conv[0] * (total + skip * gated), conv[0] * live

        def chunk(masked, skipped, at, carry):
            coming = fills_of(following, at)
            for j in range(skipped):
                share(coming, j)
            for j in range(skipped, CHUNK, 2):
                share(coming, j)
                carry, part0, query0 = token(at + j, carry, masked)
                share(coming, j + 1)
                carry, part1, query1 = token(at + j + 1, carry, masked)
                pair = pl.ds(pl.multiple_of((i * tokens + at + j) * groups, 2 * groups), 2 * groups)
                part_ref[pair] = jnp.concatenate([part0, part1], axis=0).astype(BF16)
                query_ref[pair] = jnp.concatenate([query0, query1], axis=0).astype(BF16)
            return carry

        def any_chunk(c, carry):
            at = pl.multiple_of(c * CHUNK, CHUNK)
            return lax.cond(
                ids_ref[at - 1] == ids_ref[at + CHUNK - 1],
                functools.partial(chunk, False, 0, at),
                functools.partial(chunk, True, 0, at),
                carry,
            )

        back1, back2 = ([row_of(ref, t) for ref in scratches] for t in (1, 0))
        same = (ids_ref[1] == ids_ref[0]).astype(F32)
        carry = (back1, [value * same for value in back2], [jnp.zeros((groups, LANES), F32)] * order)
        carry = chunk(True, 2, 0, carry)
        lax.fori_loop(1, tokens // CHUNK, any_chunk, carry)
        return 0

    lax.fori_loop(first_step, end_step, step, 0)
    for copy in own:
        copy.wait()


def finish_kernel(width, state_ref, part_ref, query_ref, table_ref, out_hbm, out_v, out_s, modes_s, sems):
    tokens, channels = out_v.shape
    steps = channels // width
    groups = width // LANES
    pitch = out_s.shape[0] // groups
    wide = state_ref.shape[2]
    order = table_ref.shape[0] // (2 * groups * steps)
    going = columns(out_v, out_hbm, sems, width)

    def step(i, _):
        at = i * (2 * order)
        decay = [table_ref[block_at(at + n, groups)] for n in range(order)]
        for group in range(groups):
            chunk_at = i * (width // wide) + (group * LANES) // wide
            told = state_ref[chunk_at, :, pl.ds((group * LANES) % wide, LANES)].astype(F32)
            modes_s[pl.ds(group * 2 * order, order)] = told[0:order] + told[order : 2 * order]
            modes_s[pl.ds(group * 2 * order + order, order)] = told[2 * order :]
        weights = [
            modes_s[pl.ds(n, groups, stride=2 * order)] * table_ref[block_at(at + order + n, groups)] for n in range(order)
        ]

        def pair(t, weights):
            at = pl.ds(pl.multiple_of((i * tokens + t) * groups, 2 * groups), 2 * groups)
            part, live_query = part_ref[at].astype(F32), query_ref[at].astype(F32)
            for k in range(2):
                weights = [weights[n] * decay[n] for n in range(order)]
                rows = slice(k * groups, (k + 1) * groups)
                out_s[pl.ds(t + k, groups, stride=pitch)] = part[rows] + live_query[rows] * summed(weights)
            return weights

        def give(at, group):
            out_v[pl.ds(at, CHUNK), lanes_at(i, width, group)] = out_s[pl.ds(group * pitch + at, CHUNK)].astype(BF16)

        def gives(at):
            return [functools.partial(give, at, group) for group in range(groups)]

        def chunk(c, weights):
            at = pl.multiple_of(c * CHUNK, CHUNK)
            done = gives(at - CHUNK)
            for j in range(0, CHUNK, 2):
                share(done, j)
                share(done, j + 1)
                weights = pair(at + j, weights)
            return weights

        for t in range(2):
            out_s[pl.ds(t, groups, stride=pitch)] = modes_s[pl.ds(order + t, groups, stride=2 * order)]
        for t in range(2, CHUNK, 2):
            weights = pair(t, weights)
        lax.fori_loop(1, tokens // CHUNK, chunk, weights)
        for call in gives(tokens - CHUNK):
            call()
        going(i).start()
        return 0

    lax.fori_loop(0, steps, step, 0)
    for i in range(steps):
        going(i).wait()


def on_device(query, keyed, valued, short_taps, rates, residues, skip_gain, doc_ids):
    tokens, channels = query.shape
    order = rates.shape[0]
    n_ctx = lax.axis_size("ctx")
    own = channels // n_ctx
    wide = own if own % LANES == 0 else LANES
    chunks = channels // wide
    width = min(channels, 8 * LANES)
    steps = channels // width
    groups = width // LANES
    pitch = tokens + ROWS
    params = pltpu.CompilerParams(vmem_limit_bytes=24 * 1024 * 1024)
    anywhere = pl.BlockSpec(memory_space=pl.ANY)
    smem = pl.BlockSpec(memory_space=pltpu.SMEM)
    vmem = pl.BlockSpec(memory_space=pltpu.VMEM)
    hbm = lambda *arrays: [pltpu.with_memory_space_constraint(array, pltpu.HBM) for array in arrays]
    near = lambda *arrays: [pltpu.with_memory_space_constraint(array, pltpu.VMEM) for array in arrays]

    modes_scratch = pltpu.VMEM((groups * order, LANES), F32)
    skip_gain = skip_gain.reshape(1, channels)
    tall = [pltpu.VMEM((channels // LANES * tokens, LANES), dtype) for dtype in (BF16, BF16)]
    table = pltpu.VMEM((steps * 2 * order * groups, LANES), F32)
    taps_v, modes_v = pltpu.VMEM((3, 3, channels), F32), pltpu.VMEM((order, channels), F32)

    info = pl.pallas_call(
        functools.partial(ends_kernel, width),
        in_specs=[smem] + [anywhere] * 5,
        out_specs=anywhere,
        out_shape=pltpu.HBM((chunks, INFO, wide), BF16),
        scratch_shapes=[
            pltpu.VMEM((2, 2 * ROWS, channels), BF16),
            pltpu.VMEM((tokens, channels), BF16),
            pltpu.VMEM((tokens, channels), BF16),
            taps_v,
            modes_v,
            pltpu.VMEM((chunks, INFO, wide), BF16),
            pltpu.VMEM((2 * groups * pitch, LANES), F32),
            pltpu.VMEM((2 * groups * pitch, LANES), F32),
            modes_scratch,
            pltpu.VMEM((9 * groups, LANES), F32),
            pltpu.SemaphoreType.DMA((3 * steps + 4,)),
        ],
        compiler_params=params,
        name="block_ends",
    )(*hbm(doc_ids, query, keyed, valued, short_taps, rates))

    if wide != own:
        info = info.transpose(1, 0, 2).reshape(INFO, n_ctx, own).transpose(1, 0, 2)
    info = lax.all_to_all(info, "ctx", split_axis=0, concat_axis=0, tiled=True)

    def local_scan(first, count, filled, owned=()):
        return pl.pallas_call(
            functools.partial(local_kernel, width, first, count, len(filled)),
            in_specs=[smem] + [anywhere] * 7 + [vmem] * len(filled),
            out_specs=[vmem] * (3 + len(owned)),
            out_shape=[*tall, table, *owned],
            input_output_aliases={8 + i: i for i in range(len(filled))},
            scratch_shapes=[
                pltpu.VMEM((tokens, channels), BF16),
                pltpu.VMEM((tokens, channels), BF16),
                pltpu.VMEM((tokens, channels), BF16),
                taps_v,
                modes_v,
                modes_v,
                pltpu.VMEM((1, channels), F32),
                *[pltpu.VMEM((2 * groups * pitch, LANES), F32)] * 3,
                modes_scratch,
                pltpu.VMEM((10 * groups, LANES), F32),
                pltpu.SemaphoreType.DMA((3 * count + 4 + len(owned),)),
            ],
            compiler_params=params,
            cost_estimate=pl.CostEstimate(
                flops=count * tokens * width * 64, bytes_accessed=count * tokens * width * 14, transcendentals=0
            ),
            name="local_scan",
        )(
            *hbm(doc_ids, query, keyed, valued, short_taps, rates, residues, skip_gain), *near(*filled),
        )

    half = steps // 2 or steps
    if own % LANES == 0:
        owned = [pltpu.VMEM(value.shape[:-1] + (own,), F32) for value in (short_taps, rates, residues, skip_gain)]
        *filled, own_taps, own_rates, own_resid, own_skip = local_scan(0, half, [], owned)
        own_params = [own_taps, own_rates, own_resid, own_skip]
    else:
        filled = local_scan(0, half, [])
        at = lax.axis_index("ctx") * own
        own_params = [
            lax.dynamic_slice_in_dim(value, at, own, value.ndim - 1)
            for value in (short_taps, rates, residues, skip_gain)
        ]
    info, *filled = lax.optimization_barrier((info, *filled))
    state = pl.pallas_call(
        functools.partial(carry_kernel, tokens=tokens),
        out_shape=pltpu.HBM((n_ctx, TOLD, own), BF16),
        compiler_params=params,
        name="block_carry",
    )(*near(info, *own_params))
    state, *filled = lax.optimization_barrier((state, *filled))
    state = lax.all_to_all(state, "ctx", split_axis=0, concat_axis=0, tiled=True)
    if half < steps:
        filled = local_scan(half, steps - half, filled)
    if wide != own:
        state = state.transpose(1, 0, 2).reshape(TOLD, chunks, wide).transpose(1, 0, 2)

    return pl.pallas_call(
        functools.partial(finish_kernel, width),
        in_specs=[vmem] * 4,
        out_specs=anywhere,
        out_shape=pltpu.HBM((tokens, channels), BF16),
        scratch_shapes=[
            pltpu.VMEM((tokens, channels), BF16),
            pltpu.VMEM((groups * pitch, LANES), F32),
            pltpu.VMEM((2 * groups * order, LANES), F32),
            pltpu.SemaphoreType.DMA((steps,)),
        ],
        compiler_params=params,
        name="add_carry",
    )(*near(state, *filled))


def solution(mesh):
    return jax.shard_map(
        on_device,
        mesh=mesh,
        in_specs=(
            P("ctx", "tp"),
            P("ctx", "tp"),
            P("ctx", "tp"),
            P(None, None, "tp"),
            P(None, "tp"),
            P(None, "tp"),
            P("tp"),
            P("ctx"),
        ),
        out_specs=P("ctx", "tp"),
        check_vma=False,
    )
```

```python
import functools

import jax
import jax.numpy as jnp
from jax import lax
from jax.experimental import pallas as pl
from jax.experimental.pallas import tpu as pltpu
from jax.sharding import PartitionSpec as P

LANES = 128
ROWS = 8
CHUNK = 16
INFO = 24
TOLD = 16
F32 = jnp.float32
BF16 = jnp.bfloat16


def rounded(value):
    return value.astype(BF16).astype(F32)


def row_index(rows=ROWS):
    return lax.broadcasted_iota(jnp.int32, (rows, LANES), 0)


def block_at(index, size):
    start = index * size
    return pl.ds(start if isinstance(start, int) else pl.multiple_of(start, size), size)


def lanes_at(index, size, group):
    start = index * size + group * LANES
    return pl.ds(start if isinstance(start, int) else pl.multiple_of(start, LANES), LANES)


def columns(source, target, sems, width):
    return lambda i: pltpu.make_async_copy(
        source.at[..., block_at(i, width)], target.at[..., block_at(i, width)], sems.at[i]
    )


def across(scratch, rows_of):
    rows = scratch.shape[0] // rows_of.groups
    for group in range(rows_of.groups):
        scratch[pl.ds(group * rows, rows)] = rows_of(group)
    return [scratch[pl.ds(n, rows_of.groups, stride=rows)] for n in range(rows)]


class Rows:
    def __init__(self, ref, step, width):
        self.ref, self.step, self.width, self.groups = ref, step, width, width // LANES

    def __call__(self, group):
        return self.ref[..., lanes_at(self.step, self.width, group)]


def across_taps(scratch, rows_of, streams):
    groups = rows_of.groups
    for group in range(groups):
        taps = rows_of(group)
        for s in streams:
            for j in range(3):
                scratch[pl.ds((s * 3 + j) * groups + group, 1)] = taps[s, j : j + 1]
    return [[scratch[pl.ds((s * 3 + j) * groups, groups)] for j in range(3)] for s in streams]


def fill_group(scratch, base, pitch, rows_of, at, group):
    lanes = lanes_at(rows_of.step, rows_of.width, group)
    scratch[pl.ds(base + group * pitch + at, CHUNK)] = rows_of.ref[pl.ds(at, CHUNK), lanes].astype(F32)


def fills(scratches, refs, base, pitch, step, width, at):
    return [
        functools.partial(fill_group, scratch, base, pitch, Rows(ref, step, width), at, group)
        for scratch, ref in zip(scratches, refs)
        for group in range(width // LANES)
    ]


def share(calls, j):
    for call in calls[len(calls) * j // CHUNK : len(calls) * (j + 1) // CHUNK]:
        call()


def first_of_last(ids_ref):
    tokens = ids_ref.shape[0]
    low, high = jnp.int32(0), jnp.int32(tokens - 1)
    last = ids_ref[tokens - 1]
    for _ in range((tokens - 1).bit_length()):
        middle = (low + high) // 2
        same = ids_ref[middle] == last
        low, high = jnp.where(same, low, middle + 1), jnp.where(same, middle, high)
    return high


def by_rate(rates, resid):
    rates, resid = list(rates), list(resid)
    for turn in range(len(rates)):
        for i in range(turn % 2, len(rates) - 1, 2):
            low, high = rates[i], rates[i + 1]
            swap = low > high
            rates[i], rates[i + 1] = jnp.minimum(low, high), jnp.maximum(low, high)
            resid[i], resid[i + 1] = jnp.where(swap, resid[i + 1], resid[i]), jnp.where(swap, resid[i], resid[i + 1])
    return rates, resid


def summed(terms):
    while len(terms) > 1:
        terms = [sum(terms[i : i + 2]) for i in range(0, len(terms), 2)]
    return terms[0]


def ends_kernel(
    width, ids_ref, q_hbm, k_hbm, v_hbm, taps_hbm, rates_hbm, resid_hbm,
    info_hbm,
    q_v, k_v, v_v, taps_v, rates_v, resid_v, info_v, k_s, v_s, modes_s, taps_s, sems,
):
    tokens, channels = k_v.shape
    steps = channels // width
    groups = width // LANES
    chunks = tokens // CHUNK
    pitch = k_s.shape[0] // (2 * groups)
    wide = info_v.shape[2]
    per_step = width // wide
    order = rates_v.shape[0]
    k_in, v_in = (
        columns(source, target, sems.at[pl.ds(i * steps, steps)], width)
        for i, (source, target) in enumerate(((k_hbm, k_v), (v_hbm, v_v)))
    )
    others = [
        pltpu.make_async_copy(source, target, sems.at[3 * steps + i])
        for i, (source, target) in enumerate(
            (
                (rates_hbm, rates_v),
                (resid_hbm, resid_v),
                (taps_hbm, taps_v),
                (q_hbm.at[pl.ds(0, CHUNK)], q_v.at[0]),
                (q_hbm.at[pl.ds(tokens - CHUNK, CHUNK)], q_v.at[1]),
            )
        )
    ]
    going = lambda i: pltpu.make_async_copy(
        info_v.at[block_at(i, per_step)], info_hbm.at[block_at(i, per_step)], sems.at[2 * steps + i]
    )
    k_in(0).start()
    v_in(0).start()
    for copy in others:
        copy.start()
    for i in range(1, steps):
        k_in(i).start()
        v_in(i).start()
    begin = first_of_last(ids_ref)
    chunk0 = begin // CHUNK
    row = row_index()
    marks = jnp.zeros((ROWS, LANES), F32)
    for i, t in enumerate((0, 1, tokens - 2, tokens - 1)):
        marks = jnp.where(row == i + 4, ids_ref[t].astype(F32), marks)

    def base_of(i):
        return (i % 2) * (groups * pitch)

    def fills_of(i, at):
        return fills((k_s, v_s), (k_v, v_v), base_of(i), pitch, i, width, at)

    def arrive(i):
        k_in(i).wait()
        v_in(i).wait()

    arrive(0)

    def first_fill(c, _):
        for call in fills_of(0, pl.multiple_of(c * CHUNK, CHUNK)):
            call()
        return 0

    lax.fori_loop(chunk0, chunks, first_fill, 0)
    for copy in others:
        copy.wait()

    def step(i):
        after = min(i + 1, steps - 1)
        if i + 1 < steps:
            arrive(i + 1)

        base = base_of(i)
        rates, resid = by_rate(across(modes_s, Rows(rates_v, i, width)), across(modes_s, Rows(resid_v, i, width)))
        decay = [jnp.exp(-rate) for rate in rates]
        taps = across_taps(taps_s, Rows(taps_v, i, width), (1, 2))

        def chunk(masked, c, carry):
            at = pl.multiple_of(c * CHUNK, CHUNK)
            back1, back2, ends = carry
            coming = fills_of(after, at)
            for j in range(CHUNK):
                t = at + j
                share(coming, j)
                here = [ref[pl.ds(base + t, groups, stride=pitch)] for ref in (k_s, v_s)]
                if masked:
                    live = (t >= begin).astype(F32)
                    here = [value * live for value in here]
                conv = [taps[s][0] * here[s] + taps[s][1] * back1[s] + taps[s][2] * back2[s] for s in range(2)]
                gated = rounded(conv[0] * conv[1])
                if masked and j < 2:
                    gated = gated * (t >= 2).astype(F32)
                ends = [ends[n] * decay[n] + gated for n in range(order)]
                back1, back2 = here, back1
            return back1, back2, ends

        zero = jnp.zeros((groups, LANES), F32)
        carry = chunk(True, chunk0, ([zero] * 2, [zero] * 2, [zero] * order))
        ends = lax.fori_loop(chunk0 + 1, chunks, functools.partial(chunk, False), carry)[2]
        running = zero
        for n in range(order):
            running = running + resid[n] * ends[n]
            modes_s[pl.ds(n, groups, stride=order)] = running

        for group in range(groups):
            lanes = lanes_at(i, width, group)
            state = modes_s[pl.ds(group * order, order)]
            heads = [ref[pl.ds(0, CHUNK), lanes].astype(F32)[:ROWS] for ref in (k_v, v_v)]
            tails = [ref[pl.ds(tokens - CHUNK, CHUNK), lanes].astype(F32)[ROWS:] for ref in (k_v, v_v)]
            edge = jnp.where(row < 2, heads[0], pltpu.roll(heads[1], 2, 0))
            edge = jnp.where(row < 4, edge, pltpu.roll(tails[0], ROWS - 2, 0))
            edge = jnp.where(row < 6, edge, tails[1])
            at = i * per_step + (group * LANES) // wide
            inner = pl.ds((group * LANES) % wide, LANES)
            info_v[at, pl.ds(0, 16), inner] = jnp.concatenate([state, edge], axis=0).astype(BF16)
            q_head, q_tail = (q_v[j, :, lanes].astype(F32) for j in range(2))
            more = jnp.where(row < 2, q_head[:ROWS], pltpu.roll(q_tail[ROWS:], 4, 0))
            more = jnp.where(row < 4, more, marks)
            info_v[at, pl.ds(16, 8), inner] = more.astype(BF16)
        going(i).start()

    for i in range(steps):
        step(i)
    for i in range(steps):
        going(i).wait()


def carry_kernel(info_ref, taps_ref, rates_ref, resid_ref, skip_ref, out_ref, *, tokens):
    order, wide = rates_ref.shape
    skip = skip_ref[...]
    rows = lambda ref: [ref[n : n + 1] for n in range(order)]
    rates, resid = (jnp.concatenate(modes, axis=0) for modes in by_rate(rows(rates_ref), rows(resid_ref)))
    decay = jnp.exp(-rates)
    rest = jnp.exp(-float(tokens - 2) * rates)
    row = lax.broadcasted_iota(jnp.int32, (order, wide), 0)

    def down(value, steps):
        if wide % LANES:
            moved = jnp.concatenate([value[order - steps :], value[: order - steps]], axis=0)
        else:
            moved = pltpu.roll(value, steps, 0)
        return jnp.where(row < steps, 0.0, moved)

    taps = [[taps_ref[s, j : j + 1] for j in range(3)] for s in (1, 2, 0)]
    nothing = jnp.zeros((1, wide), F32)
    state = jnp.zeros((order, wide), F32)
    tails, prev0, prev1 = [[nothing, nothing]] * 3, nothing - 1.0, nothing - 1.0
    for block in range(out_ref.shape[0]):
        info = info_ref[block].astype(F32)
        line = lambda i: info[order + i : order + i + 1]
        ends = info[:order] - down(info[:order], 1)
        heads = [[line(0), line(1)], [line(2), line(3)], [line(8), line(9)]]
        first0, first1, last0, last1 = (line(12 + i) for i in range(4))
        conv0, conv1 = [], []
        for s in range(3):
            (head0, head1), (tail0, tail1) = heads[s], tails[s]
            conv0.append(
                taps[s][0] * head0
                + taps[s][1] * jnp.where(prev1 == first0, tail1, 0.0)
                + taps[s][2] * jnp.where(prev0 == first0, tail0, 0.0)
            )
            conv1.append(
                taps[s][0] * head1
                + taps[s][1] * jnp.where(first0 == first1, head0, 0.0)
                + taps[s][2] * jnp.where(prev1 == first1, tail1, 0.0)
            )
        gated0, gated1 = rounded(conv0[0] * conv0[1]), rounded(conv1[0] * conv1[1])
        state0 = decay * (state * (prev1 == first0).astype(F32)) + resid * gated0
        state1 = decay * (state0 * (first0 == first1).astype(F32)) + resid * gated1
        long0 = jnp.sum(state0, axis=0, keepdims=True)
        long1 = jnp.sum(state1, axis=0, keepdims=True)
        mixed = jnp.where(row == 0, conv0[2] * (long0 + skip * gated0), conv1[2] * (long1 + skip * gated1))
        running = state1
        for steps in (1, 2, 4):
            running = running + down(running, steps)
        out_ref[block] = jnp.concatenate([running, mixed], axis=0).astype(BF16)
        state = ends + rest * (state1 * (first1 == last1).astype(F32))
        tails = [[line(4), line(5)], [line(6), line(7)], [line(10), line(11)]]
        prev0, prev1 = last0, last1


def local_kernel(
    width, first_step, count, filled, ids_ref, q_hbm, k_hbm, v_hbm, taps_hbm, rates_hbm, resid_hbm, skip_hbm, *rest
):
    (
        q_v, k_v, v_v, taps_v, rates_v, resid_v, skip_v, q_s, k_s, v_s, modes_s, taps_s, sems,
    ) = rest[-13:]
    part_ref, query_ref, table_ref, *own_refs = rest[filled:-13]
    tokens, channels = q_v.shape
    owned = []
    if own_refs:
        mine = own_refs[0].shape[-1]
        lanes = pl.ds(pl.multiple_of(lax.axis_index("ctx") * mine, mine), mine)
        owned = [
            (source.at[..., lanes], target)
            for source, target in zip((taps_hbm, rates_hbm, resid_hbm, skip_hbm), own_refs)
        ]
    groups = width // LANES
    pitch = q_s.shape[0] // (2 * groups)
    order = rates_v.shape[0]
    end_step = first_step + count
    scratches = (q_s, k_s, v_s)
    streams = [
        lambda i, s=s, source=source, target=target: pltpu.make_async_copy(
            source.at[:, block_at(i, width)], target.at[:, block_at(i, width)], sems.at[s * count + i - first_step]
        )
        for s, (source, target) in enumerate(((q_hbm, q_v), (k_hbm, k_v), (v_hbm, v_v)))
    ]
    part = pl.ds(first_step * width, count * width)
    own = [pltpu.make_async_copy(source, target, sems.at[3 * count + 4 + i]) for i, (source, target) in enumerate(owned)]
    others = [
        pltpu.make_async_copy(source.at[..., part], target.at[..., part], sems.at[3 * count + i])
        for i, (source, target) in enumerate(
            ((taps_hbm, taps_v), (rates_hbm, rates_v), (resid_hbm, resid_v), (skip_hbm, skip_v))
        )
    ]
    for i in range(first_step, end_step):
        for copy in streams:
            copy(i).start()
        if i == first_step:
            for copy in others + own:
                copy.start()

    def arrive(i):
        for copy in streams:
            copy(i).wait()

    def base_of(i):
        return pl.multiple_of((i % 2) * (groups * pitch), ROWS)

    def fills_of(i, at):
        return fills(scratches, (q_v, k_v, v_v), base_of(i), pitch, i, width, at)

    arrive(first_step)

    def first_fill(c, _):
        for call in fills_of(first_step, pl.multiple_of(c * CHUNK, CHUNK)):
            call()
        return 0

    lax.fori_loop(0, tokens // CHUNK, first_fill, 0)
    for copy in others:
        copy.wait()

    def step(i, _):
        following = jnp.minimum(i + 1, end_step - 1)

        @pl.when(i + 1 < end_step)
        def _():
            arrive(i + 1)

        base = base_of(i)
        for group in range(groups):
            taps_s[pl.ds(9 * groups + group, 1)] = skip_v[:, lanes_at(i, width, group)]
        rates, resid = by_rate(across(modes_s, Rows(rates_v, i, width)), across(modes_s, Rows(resid_v, i, width)))
        decay = [jnp.exp(-rate) for rate in rates]
        taps = across_taps(taps_s, Rows(taps_v, i, width), (0, 1, 2))
        skip = taps_s[pl.ds(9 * groups, groups)]
        for n in range(order):
            table_ref[block_at(i * order + n, groups)] = decay[n]

        def row_of(ref, t):
            return ref[pl.ds(base + t, groups, stride=pitch)]

        def token(t, carry, masked):
            back1, back2, states = carry
            now = [row_of(ref, t) for ref in scratches]
            if masked:
                same = (ids_ref[t] == ids_ref[t - 1]).astype(F32)
                back1 = [value * same for value in back1]
                back2 = [value * same for value in back2]
                states = [value * same for value in states]
            conv = [taps[s][0] * now[s] + taps[s][1] * back1[s] + taps[s][2] * back2[s] for s in range(3)]
            gated = rounded(conv[1] * conv[2])
            states = [states[n] * decay[n] + gated for n in range(order)]
            total = summed([states[n] * resid[n] for n in range(order)])
            live = (ids_ref[t] == ids_ref[1]).astype(F32)
            return (now, back1, states), conv[0] * (total + skip * gated), conv[0] * live

        def chunk(masked, skipped, at, carry):
            coming = fills_of(following, at)
            for j in range(skipped):
                share(coming, j)
            for j in range(skipped, CHUNK, 2):
                share(coming, j)
                carry, part0, query0 = token(at + j, carry, masked)
                share(coming, j + 1)
                carry, part1, query1 = token(at + j + 1, carry, masked)
                pair = pl.ds(pl.multiple_of((i * tokens + at + j) * groups, 2 * groups), 2 * groups)
                part_ref[pair] = jnp.concatenate([part0, part1], axis=0).astype(BF16)
                query_ref[pair] = jnp.concatenate([query0, query1], axis=0).astype(BF16)
            return carry

        def any_chunk(c, carry):
            at = pl.multiple_of(c * CHUNK, CHUNK)
            return lax.cond(
                ids_ref[at - 1] == ids_ref[at + CHUNK - 1],
                functools.partial(chunk, False, 0, at),
                functools.partial(chunk, True, 0, at),
                carry,
            )

        back1, back2 = ([row_of(ref, t) for ref in scratches] for t in (1, 0))
        same = (ids_ref[1] == ids_ref[0]).astype(F32)
        carry = (back1, [value * same for value in back2], [jnp.zeros((groups, LANES), F32)] * order)
        carry = chunk(True, 2, 0, carry)
        lax.fori_loop(1, tokens // CHUNK, any_chunk, carry)
        return 0

    lax.fori_loop(first_step, end_step, step, 0)
    for copy in own:
        copy.wait()


def finish_kernel(width, state_ref, part_ref, query_ref, table_ref, out_hbm, out_v, out_s, modes_s, sems):
    tokens, channels = out_v.shape
    steps = channels // width
    groups = width // LANES
    pitch = out_s.shape[0] // groups
    wide = state_ref.shape[2]
    order = table_ref.shape[0] // (groups * steps)
    going = columns(out_v, out_hbm, sems, width)

    def step(i, _):
        decay = [table_ref[block_at(i * order + n, groups)] for n in range(order)]
        for group in range(groups):
            chunk_at = i * (width // wide) + (group * LANES) // wide
            modes_s[pl.ds(group * TOLD, TOLD)] = state_ref[chunk_at, :, pl.ds((group * LANES) % wide, LANES)].astype(F32)
        running = [modes_s[pl.ds(n, groups, stride=TOLD)] for n in range(order)]
        weights = [running[0]] + [running[n] - running[n - 1] for n in range(1, order)]

        def pair(t, weights):
            at = pl.ds(pl.multiple_of((i * tokens + t) * groups, 2 * groups), 2 * groups)
            part, live_query = part_ref[at].astype(F32), query_ref[at].astype(F32)
            for k in range(2):
                weights = [weights[n] * decay[n] for n in range(order)]
                rows = slice(k * groups, (k + 1) * groups)
                out_s[pl.ds(t + k, groups, stride=pitch)] = part[rows] + live_query[rows] * summed(weights)
            return weights

        def give(at, group):
            out_v[pl.ds(at, CHUNK), lanes_at(i, width, group)] = out_s[pl.ds(group * pitch + at, CHUNK)].astype(BF16)

        def gives(at):
            return [functools.partial(give, at, group) for group in range(groups)]

        def chunk(c, weights):
            at = pl.multiple_of(c * CHUNK, CHUNK)
            done = gives(at - CHUNK)
            for j in range(0, CHUNK, 2):
                share(done, j)
                share(done, j + 1)
                weights = pair(at + j, weights)
            return weights

        for t in range(2):
            out_s[pl.ds(t, groups, stride=pitch)] = modes_s[pl.ds(order + t, groups, stride=TOLD)]
        for t in range(2, CHUNK, 2):
            weights = pair(t, weights)
        lax.fori_loop(1, tokens // CHUNK, chunk, weights)
        for call in gives(tokens - CHUNK):
            call()
        going(i).start()
        return 0

    lax.fori_loop(0, steps, step, 0)
    for i in range(steps):
        going(i).wait()


def on_device(query, keyed, valued, short_taps, rates, residues, skip_gain, doc_ids):
    tokens, channels = query.shape
    order = rates.shape[0]
    n_ctx = lax.axis_size("ctx")
    own = channels // n_ctx
    wide = own if own % LANES == 0 else LANES
    chunks = channels // wide
    width = min(channels, 8 * LANES)
    steps = channels // width
    groups = width // LANES
    pitch = tokens + ROWS
    params = pltpu.CompilerParams(vmem_limit_bytes=24 * 1024 * 1024)
    anywhere = pl.BlockSpec(memory_space=pl.ANY)
    smem = pl.BlockSpec(memory_space=pltpu.SMEM)
    vmem = pl.BlockSpec(memory_space=pltpu.VMEM)
    hbm = lambda *arrays: [pltpu.with_memory_space_constraint(array, pltpu.HBM) for array in arrays]
    near = lambda *arrays: [pltpu.with_memory_space_constraint(array, pltpu.VMEM) for array in arrays]

    modes_scratch = pltpu.VMEM((groups * order, LANES), F32)
    skip_gain = skip_gain.reshape(1, channels)
    tall = [pltpu.VMEM((channels // LANES * tokens, LANES), dtype) for dtype in (BF16, BF16)]
    table = pltpu.VMEM((steps * order * groups, LANES), F32)
    taps_v, modes_v = pltpu.VMEM((3, 3, channels), F32), pltpu.VMEM((order, channels), F32)

    info = pl.pallas_call(
        functools.partial(ends_kernel, width),
        in_specs=[smem] + [anywhere] * 6,
        out_specs=anywhere,
        out_shape=pltpu.HBM((chunks, INFO, wide), BF16),
        scratch_shapes=[
            pltpu.VMEM((2, 2 * ROWS, channels), BF16),
            pltpu.VMEM((tokens, channels), BF16),
            pltpu.VMEM((tokens, channels), BF16),
            taps_v,
            modes_v,
            modes_v,
            pltpu.VMEM((chunks, INFO, wide), BF16),
            pltpu.VMEM((2 * groups * pitch, LANES), F32),
            pltpu.VMEM((2 * groups * pitch, LANES), F32),
            modes_scratch,
            pltpu.VMEM((9 * groups, LANES), F32),
            pltpu.SemaphoreType.DMA((3 * steps + 5,)),
        ],
        compiler_params=params,
        name="block_ends",
    )(*hbm(doc_ids, query, keyed, valued, short_taps, rates, residues))

    if wide != own:
        info = info.transpose(1, 0, 2).reshape(INFO, n_ctx, own).transpose(1, 0, 2)
    info = lax.all_to_all(info, "ctx", split_axis=0, concat_axis=0, tiled=True)

    def local_scan(first, count, filled, owned=()):
        return pl.pallas_call(
            functools.partial(local_kernel, width, first, count, len(filled)),
            in_specs=[smem] + [anywhere] * 7 + [vmem] * len(filled),
            out_specs=[vmem] * (3 + len(owned)),
            out_shape=[*tall, table, *owned],
            input_output_aliases={8 + i: i for i in range(len(filled))},
            scratch_shapes=[
                pltpu.VMEM((tokens, channels), BF16),
                pltpu.VMEM((tokens, channels), BF16),
                pltpu.VMEM((tokens, channels), BF16),
                taps_v,
                modes_v,
                modes_v,
                pltpu.VMEM((1, channels), F32),
                *[pltpu.VMEM((2 * groups * pitch, LANES), F32)] * 3,
                modes_scratch,
                pltpu.VMEM((10 * groups, LANES), F32),
                pltpu.SemaphoreType.DMA((3 * count + 4 + len(owned),)),
            ],
            compiler_params=params,
            cost_estimate=pl.CostEstimate(
                flops=count * tokens * width * 64, bytes_accessed=count * tokens * width * 14, transcendentals=0
            ),
            name="local_scan",
        )(
            *hbm(doc_ids, query, keyed, valued, short_taps, rates, residues, skip_gain), *near(*filled),
        )

    half = steps // 2 or steps
    if own % LANES == 0:
        owned = [pltpu.VMEM(value.shape[:-1] + (own,), F32) for value in (short_taps, rates, residues, skip_gain)]
        *filled, own_taps, own_rates, own_resid, own_skip = local_scan(0, half, [], owned)
        own_params = [own_taps, own_rates, own_resid, own_skip]
    else:
        filled = local_scan(0, half, [])
        at = lax.axis_index("ctx") * own
        own_params = [
            lax.dynamic_slice_in_dim(value, at, own, value.ndim - 1)
            for value in (short_taps, rates, residues, skip_gain)
        ]
    info, *filled = lax.optimization_barrier((info, *filled))
    state = pl.pallas_call(
        functools.partial(carry_kernel, tokens=tokens),
        out_shape=pltpu.HBM((n_ctx, TOLD, own), BF16),
        compiler_params=params,
        name="block_carry",
    )(*near(info, *own_params))
    state, *filled = lax.optimization_barrier((state, *filled))
    state = lax.all_to_all(state, "ctx", split_axis=0, concat_axis=0, tiled=True)
    if half < steps:
        filled = local_scan(half, steps - half, filled)
    if wide != own:
        state = state.transpose(1, 0, 2).reshape(TOLD, chunks, wide).transpose(1, 0, 2)

    return pl.pallas_call(
        functools.partial(finish_kernel, width),
        in_specs=[vmem] * 4,
        out_specs=anywhere,
        out_shape=pltpu.HBM((tokens, channels), BF16),
        scratch_shapes=[
            pltpu.VMEM((tokens, channels), BF16),
            pltpu.VMEM((groups * pitch, LANES), F32),
            pltpu.VMEM((groups * TOLD, LANES), F32),
            pltpu.SemaphoreType.DMA((steps,)),
        ],
        compiler_params=params,
        name="add_carry",
    )(*near(state, *filled))


def solution(mesh):
    return jax.shard_map(
        on_device,
        mesh=mesh,
        in_specs=(
            P("ctx", "tp"),
            P("ctx", "tp"),
            P("ctx", "tp"),
            P(None, None, "tp"),
            P(None, "tp"),
            P(None, "tp"),
            P("tp"),
            P("ctx"),
        ),
        out_specs=P("ctx", "tp"),
        check_vma=False,
    )
```

```python
import functools

import jax
import jax.numpy as jnp
from jax import lax
from jax.experimental import pallas as pl
from jax.experimental.pallas import tpu as pltpu
from jax.sharding import PartitionSpec as P

LANES = 128
ROWS = 8
CHUNK = 16
INFO = 24
TOLD = 16
F32 = jnp.float32
BF16 = jnp.bfloat16


def meeting_order(count):
    place = lambda i: (i % 2, i // 2 % 2, i // 4)
    root = place(count // 2 - 1)
    return sorted(range(count), key=lambda i: sum(abs(a - b) for a, b in zip(place(i), root)))


def place_in(turn):
    me = lax.axis_index("ctx")
    place = jnp.int32(0)
    for i, at in enumerate(turn):
        place = jnp.where(me == i, at, place)
    return place


def rounded(value):
    return value.astype(BF16).astype(F32)


def row_index(rows=ROWS):
    return lax.broadcasted_iota(jnp.int32, (rows, LANES), 0)


def block_at(index, size):
    start = index * size
    return pl.ds(start if isinstance(start, int) else pl.multiple_of(start, size), size)


def lanes_at(index, size, group):
    start = index * size + group * LANES
    return pl.ds(start if isinstance(start, int) else pl.multiple_of(start, LANES), LANES)


def columns(source, target, sems, width):
    return lambda i: pltpu.make_async_copy(
        source.at[..., block_at(i, width)], target.at[..., block_at(i, width)], sems.at[i]
    )


def across(scratch, rows_of):
    rows = scratch.shape[0] // rows_of.groups
    for group in range(rows_of.groups):
        scratch[pl.ds(group * rows, rows)] = rows_of(group)
    return [scratch[pl.ds(n, rows_of.groups, stride=rows)] for n in range(rows)]


class Rows:
    def __init__(self, ref, step, width):
        self.ref, self.step, self.width, self.groups = ref, step, width, width // LANES

    def __call__(self, group):
        return self.ref[..., lanes_at(self.step, self.width, group)]


def across_taps(scratch, rows_of, streams):
    groups = rows_of.groups
    for group in range(groups):
        taps = rows_of(group)
        for s in streams:
            for j in range(3):
                scratch[pl.ds((s * 3 + j) * groups + group, 1)] = taps[s, j : j + 1]
    return [[scratch[pl.ds((s * 3 + j) * groups, groups)] for j in range(3)] for s in streams]


def fill_group(scratch, base, pitch, rows_of, at, group):
    lanes = lanes_at(rows_of.step, rows_of.width, group)
    scratch[pl.ds(base + group * pitch + at, CHUNK)] = rows_of.ref[pl.ds(at, CHUNK), lanes].astype(F32)


def fills(scratches, refs, base, pitch, step, width, at):
    return [
        functools.partial(fill_group, scratch, base, pitch, Rows(ref, step, width), at, group)
        for scratch, ref in zip(scratches, refs)
        for group in range(width // LANES)
    ]


def share(calls, j):
    for call in calls[len(calls) * j // CHUNK : len(calls) * (j + 1) // CHUNK]:
        call()


def first_of_last(ids_ref):
    tokens = ids_ref.shape[0]
    low, high = jnp.int32(0), jnp.int32(tokens - 1)
    last = ids_ref[tokens - 1]
    for _ in range((tokens - 1).bit_length()):
        middle = (low + high) // 2
        same = ids_ref[middle] == last
        low, high = jnp.where(same, low, middle + 1), jnp.where(same, middle, high)
    return high


def by_rate(rates, resid):
    rates, resid = list(rates), list(resid)
    for turn in range(len(rates)):
        for i in range(turn % 2, len(rates) - 1, 2):
            low, high = rates[i], rates[i + 1]
            swap = low > high
            rates[i], rates[i + 1] = jnp.minimum(low, high), jnp.maximum(low, high)
            resid[i], resid[i + 1] = jnp.where(swap, resid[i + 1], resid[i]), jnp.where(swap, resid[i], resid[i + 1])
    return rates, resid


def summed(terms):
    while len(terms) > 1:
        terms = [sum(terms[i : i + 2]) for i in range(0, len(terms), 2)]
    return terms[0]


def ends_kernel(
    width, ids_ref, q_hbm, k_hbm, v_hbm, taps_hbm, rates_hbm, resid_hbm,
    info_hbm,
    q_v, k_v, v_v, taps_v, rates_v, resid_v, info_v, k_s, v_s, modes_s, taps_s, held_s, sems,
):
    tokens, channels = k_v.shape
    steps = channels // width
    groups = width // LANES
    chunks = tokens // CHUNK
    pitch = k_s.shape[0] // (2 * groups)
    wide = info_v.shape[2]
    per_step = width // wide
    order = rates_v.shape[0]
    k_in, v_in = (
        columns(source, target, sems.at[pl.ds(i * steps, steps)], width)
        for i, (source, target) in enumerate(((k_hbm, k_v), (v_hbm, v_v)))
    )
    others = [
        pltpu.make_async_copy(source, target, sems.at[3 * steps + i])
        for i, (source, target) in enumerate(
            (
                (rates_hbm, rates_v),
                (resid_hbm, resid_v),
                (taps_hbm, taps_v),
                (q_hbm.at[pl.ds(0, CHUNK)], q_v.at[0]),
                (q_hbm.at[pl.ds(tokens - CHUNK, CHUNK)], q_v.at[1]),
            )
        )
    ]
    going = lambda i: pltpu.make_async_copy(
        info_v.at[block_at(i, per_step)], info_hbm.at[block_at(i, per_step)], sems.at[2 * steps + i]
    )
    for copy in others[:3]:
        copy.start()
    for i in range(steps):
        k_in(i).start()
        v_in(i).start()
        if i == 0:
            for copy in others[3:]:
                copy.start()
    begin = first_of_last(ids_ref)
    chunk0 = begin // CHUNK
    row = row_index()
    marks = jnp.zeros((ROWS, LANES), F32)
    for i, t in enumerate((0, 1, tokens - 2, tokens - 1)):
        marks = jnp.where(row == i + 4, ids_ref[t].astype(F32), marks)

    def base_of(i):
        return (i % 2) * (groups * pitch)

    def fills_of(i, at):
        return fills((k_s, v_s), (k_v, v_v), base_of(i), pitch, i, width, at)

    def arrive(i):
        k_in(i).wait()
        v_in(i).wait()

    for copy in others[:3]:
        copy.wait()
    held = 2 * order + 6

    def hold(i, _):
        rates, resid = by_rate(across(modes_s, Rows(rates_v, i, width)), across(modes_s, Rows(resid_v, i, width)))
        taps = across_taps(taps_s, Rows(taps_v, i, width), (1, 2))
        for n, value in enumerate([jnp.exp(-rate) for rate in rates] + resid + taps[0] + taps[1]):
            held_s[block_at(i * held + n, groups)] = value
        return 0

    lax.fori_loop(0, steps, hold, 0)
    arrive(0)

    def first_fill(c, _):
        for call in fills_of(0, pl.multiple_of(c * CHUNK, CHUNK)):
            call()
        return 0

    lax.fori_loop(chunk0, chunks, first_fill, 0)
    for copy in others[3:]:
        copy.wait()

    def step(i):
        after = min(i + 1, steps - 1)
        if i + 1 < steps:
            arrive(i + 1)

        base = base_of(i)
        values = [held_s[block_at(i * held + n, groups)] for n in range(held)]
        decay, resid = values[:order], values[order : 2 * order]
        taps = [values[2 * order : 2 * order + 3], values[2 * order + 3 :]]

        def chunk(masked, c, carry):
            at = pl.multiple_of(c * CHUNK, CHUNK)
            back1, back2, ends = carry
            coming = fills_of(after, at)
            for j in range(CHUNK):
                t = at + j
                share(coming, j)
                here = [ref[pl.ds(base + t, groups, stride=pitch)] for ref in (k_s, v_s)]
                if masked:
                    live = (t >= begin).astype(F32)
                    here = [value * live for value in here]
                conv = [taps[s][0] * here[s] + taps[s][1] * back1[s] + taps[s][2] * back2[s] for s in range(2)]
                gated = rounded(conv[0] * conv[1])
                if masked and j < 2:
                    gated = gated * (t >= 2).astype(F32)
                ends = [ends[n] * decay[n] + gated for n in range(order)]
                back1, back2 = here, back1
            return back1, back2, ends

        zero = jnp.zeros((groups, LANES), F32)
        carry = chunk(True, chunk0, ([zero] * 2, [zero] * 2, [zero] * order))
        ends = lax.fori_loop(chunk0 + 1, chunks, functools.partial(chunk, False), carry)[2]
        running = zero
        for n in range(order):
            running = running + resid[n] * ends[n]
            modes_s[pl.ds(n, groups, stride=order)] = running

        for group in range(groups):
            lanes = lanes_at(i, width, group)
            state = modes_s[pl.ds(group * order, order)]
            heads = [ref[pl.ds(0, CHUNK), lanes].astype(F32)[:ROWS] for ref in (k_v, v_v)]
            tails = [ref[pl.ds(tokens - CHUNK, CHUNK), lanes].astype(F32)[ROWS:] for ref in (k_v, v_v)]
            edge = jnp.where(row < 2, heads[0], pltpu.roll(heads[1], 2, 0))
            edge = jnp.where(row < 4, edge, pltpu.roll(tails[0], ROWS - 2, 0))
            edge = jnp.where(row < 6, edge, tails[1])
            at = i * per_step + (group * LANES) // wide
            inner = pl.ds((group * LANES) % wide, LANES)
            info_v[at, pl.ds(0, 16), inner] = jnp.concatenate([state, edge], axis=0).astype(BF16)
            q_head, q_tail = (q_v[j, :, lanes].astype(F32) for j in range(2))
            more = jnp.where(row < 2, q_head[:ROWS], pltpu.roll(q_tail[ROWS:], 4, 0))
            more = jnp.where(row < 4, more, marks)
            info_v[at, pl.ds(16, 8), inner] = more.astype(BF16)
        going(i).start()

    for i in range(steps):
        step(i)
    for i in range(steps):
        going(i).wait()


def carry_kernel(turn, tokens, info_ref, taps_ref, rates_ref, resid_ref, skip_ref, out_ref):
    order, wide = rates_ref.shape
    skip = skip_ref[...]
    rows = lambda ref: [ref[n : n + 1] for n in range(order)]
    rates, resid = (jnp.concatenate(modes, axis=0) for modes in by_rate(rows(rates_ref), rows(resid_ref)))
    decay = jnp.exp(-rates)
    rest = jnp.exp(-float(tokens - 2) * rates)
    row = lax.broadcasted_iota(jnp.int32, (order, wide), 0)

    def down(value, steps):
        if wide % LANES:
            moved = jnp.concatenate([value[order - steps :], value[: order - steps]], axis=0)
        else:
            moved = pltpu.roll(value, steps, 0)
        return jnp.where(row < steps, 0.0, moved)

    taps = [[taps_ref[s, j : j + 1] for j in range(3)] for s in (1, 2, 0)]
    nothing = jnp.zeros((1, wide), F32)
    state = jnp.zeros((order, wide), F32)
    tails, prev0, prev1 = [[nothing, nothing]] * 3, nothing - 1.0, nothing - 1.0
    for block in turn:
        info = info_ref[block].astype(F32)
        line = lambda i: info[order + i : order + i + 1]
        ends = info[:order] - down(info[:order], 1)
        heads = [[line(0), line(1)], [line(2), line(3)], [line(8), line(9)]]
        first0, first1, last0, last1 = (line(12 + i) for i in range(4))
        conv0, conv1 = [], []
        for s in range(3):
            (head0, head1), (tail0, tail1) = heads[s], tails[s]
            conv0.append(
                taps[s][0] * head0
                + taps[s][1] * jnp.where(prev1 == first0, tail1, 0.0)
                + taps[s][2] * jnp.where(prev0 == first0, tail0, 0.0)
            )
            conv1.append(
                taps[s][0] * head1
                + taps[s][1] * jnp.where(first0 == first1, head0, 0.0)
                + taps[s][2] * jnp.where(prev1 == first1, tail1, 0.0)
            )
        gated0, gated1 = rounded(conv0[0] * conv0[1]), rounded(conv1[0] * conv1[1])
        state0 = decay * (state * (prev1 == first0).astype(F32)) + resid * gated0
        state1 = decay * (state0 * (first0 == first1).astype(F32)) + resid * gated1
        long0 = jnp.sum(state0, axis=0, keepdims=True)
        long1 = jnp.sum(state1, axis=0, keepdims=True)
        mixed = jnp.where(row == 0, conv0[2] * (long0 + skip * gated0), conv1[2] * (long1 + skip * gated1))
        running = state1
        for steps in (1, 2, 4):
            running = running + down(running, steps)
        out_ref[block] = jnp.concatenate([running, mixed], axis=0).astype(BF16)
        state = ends + rest * (state1 * (first1 == last1).astype(F32))
        tails = [[line(4), line(5)], [line(6), line(7)], [line(10), line(11)]]
        prev0, prev1 = last0, last1


def local_kernel(
    width, first_step, count, filled, turn, ids_ref, q_hbm, k_hbm, v_hbm, taps_hbm, rates_hbm, resid_hbm, skip_hbm, *rest
):
    (
        q_v, k_v, v_v, taps_v, rates_v, resid_v, skip_v, q_s, k_s, v_s, modes_s, taps_s, sems,
    ) = rest[-13:]
    part_ref, query_ref, table_ref, *own_refs = rest[filled:-13]
    tokens, channels = q_v.shape
    owned = []
    if own_refs:
        mine = own_refs[0].shape[-1]
        lanes = pl.ds(pl.multiple_of(place_in(turn) * mine, mine), mine)
        owned = [
            (source.at[..., lanes], target)
            for source, target in zip((taps_hbm, rates_hbm, resid_hbm, skip_hbm), own_refs)
        ]
    groups = width // LANES
    pitch = q_s.shape[0] // (2 * groups)
    order = rates_v.shape[0]
    end_step = first_step + count
    scratches = (q_s, k_s, v_s)
    streams = [
        lambda i, s=s, source=source, target=target: pltpu.make_async_copy(
            source.at[:, block_at(i, width)], target.at[:, block_at(i, width)], sems.at[s * count + i - first_step]
        )
        for s, (source, target) in enumerate(((q_hbm, q_v), (k_hbm, k_v), (v_hbm, v_v)))
    ]
    part = pl.ds(first_step * width, count * width)
    own = [pltpu.make_async_copy(source, target, sems.at[3 * count + 4 + i]) for i, (source, target) in enumerate(owned)]
    others = [
        pltpu.make_async_copy(source.at[..., part], target.at[..., part], sems.at[3 * count + i])
        for i, (source, target) in enumerate(
            ((taps_hbm, taps_v), (rates_hbm, rates_v), (resid_hbm, resid_v), (skip_hbm, skip_v))
        )
    ]
    for i in range(first_step, end_step):
        for copy in streams:
            copy(i).start()
        if i == first_step:
            for copy in others + own:
                copy.start()

    def arrive(i):
        for copy in streams:
            copy(i).wait()

    def base_of(i):
        return pl.multiple_of((i % 2) * (groups * pitch), ROWS)

    def fills_of(i, at):
        return fills(scratches, (q_v, k_v, v_v), base_of(i), pitch, i, width, at)

    arrive(first_step)

    def first_fill(c, _):
        for call in fills_of(first_step, pl.multiple_of(c * CHUNK, CHUNK)):
            call()
        return 0

    lax.fori_loop(0, tokens // CHUNK, first_fill, 0)
    for copy in others:
        copy.wait()

    def step(i, _):
        following = jnp.minimum(i + 1, end_step - 1)

        @pl.when(i + 1 < end_step)
        def _():
            arrive(i + 1)

        base = base_of(i)
        for group in range(groups):
            taps_s[pl.ds(9 * groups + group, 1)] = skip_v[:, lanes_at(i, width, group)]
        rates, resid = by_rate(across(modes_s, Rows(rates_v, i, width)), across(modes_s, Rows(resid_v, i, width)))
        decay = [jnp.exp(-rate) for rate in rates]
        taps = across_taps(taps_s, Rows(taps_v, i, width), (0, 1, 2))
        skip = taps_s[pl.ds(9 * groups, groups)]
        for n in range(order):
            table_ref[block_at(i * order + n, groups)] = decay[n]

        def row_of(ref, t):
            return ref[pl.ds(base + t, groups, stride=pitch)]

        def token(t, carry, masked):
            back1, back2, states = carry
            now = [row_of(ref, t) for ref in scratches]
            if masked:
                same = (ids_ref[t] == ids_ref[t - 1]).astype(F32)
                back1 = [value * same for value in back1]
                back2 = [value * same for value in back2]
                states = [value * same for value in states]
            conv = [taps[s][0] * now[s] + taps[s][1] * back1[s] + taps[s][2] * back2[s] for s in range(3)]
            gated = rounded(conv[1] * conv[2])
            states = [states[n] * decay[n] + gated for n in range(order)]
            total = summed([states[n] * resid[n] for n in range(order)])
            live = (ids_ref[t] == ids_ref[1]).astype(F32)
            return (now, back1, states), conv[0] * (total + skip * gated), conv[0] * live

        def chunk(masked, skipped, at, carry):
            coming = fills_of(following, at)
            for j in range(skipped):
                share(coming, j)
            for j in range(skipped, CHUNK, 2):
                share(coming, j)
                carry, part0, query0 = token(at + j, carry, masked)
                share(coming, j + 1)
                carry, part1, query1 = token(at + j + 1, carry, masked)
                pair = pl.ds(pl.multiple_of((i * tokens + at + j) * groups, 2 * groups), 2 * groups)
                part_ref[pair] = jnp.concatenate([part0, part1], axis=0).astype(BF16)
                query_ref[pair] = jnp.concatenate([query0, query1], axis=0).astype(BF16)
            return carry

        def any_chunk(c, carry):
            at = pl.multiple_of(c * CHUNK, CHUNK)
            return lax.cond(
                ids_ref[at - 1] == ids_ref[at + CHUNK - 1],
                functools.partial(chunk, False, 0, at),
                functools.partial(chunk, True, 0, at),
                carry,
            )

        back1, back2 = ([row_of(ref, t) for ref in scratches] for t in (1, 0))
        same = (ids_ref[1] == ids_ref[0]).astype(F32)
        carry = (back1, [value * same for value in back2], [jnp.zeros((groups, LANES), F32)] * order)
        carry = chunk(True, 2, 0, carry)
        lax.fori_loop(1, tokens // CHUNK, any_chunk, carry)
        return 0

    lax.fori_loop(first_step, end_step, step, 0)
    for copy in own:
        copy.wait()


def finish_kernel(width, state_ref, part_ref, query_ref, table_ref, out_hbm, out_v, out_s, modes_s, sems):
    tokens, channels = out_v.shape
    steps = channels // width
    groups = width // LANES
    pitch = out_s.shape[0] // groups
    wide = state_ref.shape[2]
    order = table_ref.shape[0] // (groups * steps)
    going = columns(out_v, out_hbm, sems, width)

    def step(i, _):
        decay = [table_ref[block_at(i * order + n, groups)] for n in range(order)]
        for group in range(groups):
            chunk_at = i * (width // wide) + (group * LANES) // wide
            modes_s[pl.ds(group * TOLD, TOLD)] = state_ref[chunk_at, :, pl.ds((group * LANES) % wide, LANES)].astype(F32)
        running = [modes_s[pl.ds(n, groups, stride=TOLD)] for n in range(order)]
        weights = [running[0]] + [running[n] - running[n - 1] for n in range(1, order)]

        def pair(t, weights):
            at = pl.ds(pl.multiple_of((i * tokens + t) * groups, 2 * groups), 2 * groups)
            part, live_query = part_ref[at].astype(F32), query_ref[at].astype(F32)
            for k in range(2):
                weights = [weights[n] * decay[n] for n in range(order)]
                rows = slice(k * groups, (k + 1) * groups)
                out_s[pl.ds(t + k, groups, stride=pitch)] = part[rows] + live_query[rows] * summed(weights)
            return weights

        def give(at, group):
            out_v[pl.ds(at, CHUNK), lanes_at(i, width, group)] = out_s[pl.ds(group * pitch + at, CHUNK)].astype(BF16)

        def gives(at):
            return [functools.partial(give, at, group) for group in range(groups)]

        def chunk(c, weights):
            at = pl.multiple_of(c * CHUNK, CHUNK)
            done = gives(at - CHUNK)
            for j in range(0, CHUNK, 2):
                share(done, j)
                share(done, j + 1)
                weights = pair(at + j, weights)
            return weights

        for t in range(2):
            out_s[pl.ds(t, groups, stride=pitch)] = modes_s[pl.ds(order + t, groups, stride=TOLD)]
        for t in range(2, CHUNK, 2):
            weights = pair(t, weights)
        lax.fori_loop(1, tokens // CHUNK, chunk, weights)
        for call in gives(tokens - CHUNK):
            call()
        going(i).start()
        return 0

    lax.fori_loop(0, steps, step, 0)
    for i in range(steps):
        going(i).wait()


def on_device(query, keyed, valued, short_taps, rates, residues, skip_gain, doc_ids):
    tokens, channels = query.shape
    order = rates.shape[0]
    n_ctx = lax.axis_size("ctx")
    meeting = meeting_order(n_ctx)
    turn = [meeting.index(i) for i in range(n_ctx)]
    exchange = lambda value: lax.all_to_all(
        value, "ctx", split_axis=0, concat_axis=0, tiled=True, axis_index_groups=[meeting]
    )
    own = channels // n_ctx
    wide = own if own % LANES == 0 else LANES
    chunks = channels // wide
    width = min(channels, 8 * LANES)
    steps = channels // width
    groups = width // LANES
    pitch = tokens + ROWS
    params = pltpu.CompilerParams(vmem_limit_bytes=24 * 1024 * 1024)
    anywhere = pl.BlockSpec(memory_space=pl.ANY)
    smem = pl.BlockSpec(memory_space=pltpu.SMEM)
    vmem = pl.BlockSpec(memory_space=pltpu.VMEM)
    hbm = lambda *arrays: [pltpu.with_memory_space_constraint(array, pltpu.HBM) for array in arrays]
    near = lambda *arrays: [pltpu.with_memory_space_constraint(array, pltpu.VMEM) for array in arrays]

    modes_scratch = pltpu.VMEM((groups * order, LANES), F32)
    skip_gain = skip_gain.reshape(1, channels)
    tall = [pltpu.VMEM((channels // LANES * tokens, LANES), dtype) for dtype in (BF16, BF16)]
    table = pltpu.VMEM((steps * order * groups, LANES), F32)
    taps_v, modes_v = pltpu.VMEM((3, 3, channels), F32), pltpu.VMEM((order, channels), F32)

    info = pl.pallas_call(
        functools.partial(ends_kernel, width),
        in_specs=[smem] + [anywhere] * 6,
        out_specs=anywhere,
        out_shape=pltpu.HBM((chunks, INFO, wide), BF16),
        scratch_shapes=[
            pltpu.VMEM((2, 2 * ROWS, channels), BF16),
            pltpu.VMEM((tokens, channels), BF16),
            pltpu.VMEM((tokens, channels), BF16),
            taps_v,
            modes_v,
            modes_v,
            pltpu.VMEM((chunks, INFO, wide), BF16),
            pltpu.VMEM((2 * groups * pitch, LANES), F32),
            pltpu.VMEM((2 * groups * pitch, LANES), F32),
            modes_scratch,
            pltpu.VMEM((9 * groups, LANES), F32),
            pltpu.VMEM((steps * (2 * order + 6) * groups, LANES), F32),
            pltpu.SemaphoreType.DMA((3 * steps + 5,)),
        ],
        compiler_params=params,
        name="block_ends",
    )(*hbm(doc_ids, query, keyed, valued, short_taps, rates, residues))

    if wide != own:
        info = info.transpose(1, 0, 2).reshape(INFO, n_ctx, own).transpose(1, 0, 2)
    info = exchange(info)

    def local_scan(first, count, filled, owned=()):
        return pl.pallas_call(
            functools.partial(local_kernel, width, first, count, len(filled), turn),
            in_specs=[smem] + [anywhere] * 7 + [vmem] * len(filled),
            out_specs=[vmem] * (3 + len(owned)),
            out_shape=[*tall, table, *owned],
            input_output_aliases={8 + i: i for i in range(len(filled))},
            scratch_shapes=[
                pltpu.VMEM((tokens, channels), BF16),
                pltpu.VMEM((tokens, channels), BF16),
                pltpu.VMEM((tokens, channels), BF16),
                taps_v,
                modes_v,
                modes_v,
                pltpu.VMEM((1, channels), F32),
                *[pltpu.VMEM((2 * groups * pitch, LANES), F32)] * 3,
                modes_scratch,
                pltpu.VMEM((10 * groups, LANES), F32),
                pltpu.SemaphoreType.DMA((3 * count + 4 + len(owned),)),
            ],
            compiler_params=params,
            cost_estimate=pl.CostEstimate(
                flops=count * tokens * width * 64, bytes_accessed=count * tokens * width * 14, transcendentals=0
            ),
            name="local_scan",
        )(
            *hbm(doc_ids, query, keyed, valued, short_taps, rates, residues, skip_gain), *near(*filled),
        )

    half = steps // 2 or steps
    if own % LANES == 0:
        owned = [pltpu.VMEM(value.shape[:-1] + (own,), F32) for value in (short_taps, rates, residues, skip_gain)]
        *filled, own_taps, own_rates, own_resid, own_skip = local_scan(0, half, [], owned)
        own_params = [own_taps, own_rates, own_resid, own_skip]
    else:
        filled = local_scan(0, half, [])
        at = place_in(turn) * own
        own_params = [
            lax.dynamic_slice_in_dim(value, at, own, value.ndim - 1)
            for value in (short_taps, rates, residues, skip_gain)
        ]
    info, *filled = lax.optimization_barrier((info, *filled))
    state = pl.pallas_call(
        functools.partial(carry_kernel, turn, tokens),
        out_shape=pltpu.HBM((n_ctx, TOLD, own), BF16),
        compiler_params=params,
        name="block_carry",
    )(*near(info, *own_params))
    state, *filled = lax.optimization_barrier((state, *filled))
    state = exchange(state)
    if half < steps:
        filled = local_scan(half, steps - half, filled)
    if wide != own:
        state = state.transpose(1, 0, 2).reshape(TOLD, chunks, wide).transpose(1, 0, 2)

    return pl.pallas_call(
        functools.partial(finish_kernel, width),
        in_specs=[vmem] * 4,
        out_specs=anywhere,
        out_shape=pltpu.HBM((tokens, channels), BF16),
        scratch_shapes=[
            pltpu.VMEM((tokens, channels), BF16),
            pltpu.VMEM((groups * pitch, LANES), F32),
            pltpu.VMEM((groups * TOLD, LANES), F32),
            pltpu.SemaphoreType.DMA((steps,)),
        ],
        compiler_params=params,
        name="add_carry",
    )(*near(state, *filled))


def solution(mesh):
    return jax.shard_map(
        on_device,
        mesh=mesh,
        in_specs=(
            P("ctx", "tp"),
            P("ctx", "tp"),
            P("ctx", "tp"),
            P(None, None, "tp"),
            P(None, "tp"),
            P(None, "tp"),
            P("tp"),
            P("ctx"),
        ),
        out_specs=P("ctx", "tp"),
        check_vma=False,
    )
```

```python
import functools

import jax
import jax.numpy as jnp
from jax import lax
from jax.experimental import pallas as pl
from jax.experimental.pallas import tpu as pltpu
from jax.sharding import PartitionSpec as P

LANES = 128
ROWS = 8
CHUNK = 16
INFO = 24
TOLD = 16
F32 = jnp.float32
BF16 = jnp.bfloat16


def meeting_order(count):
    first = 5 * count // 8
    return [(first + i) % count for i in range(count)]


def place_in(turn):
    me = lax.axis_index("ctx")
    place = jnp.int32(0)
    for i, at in enumerate(turn):
        place = jnp.where(me == i, at, place)
    return place


def rounded(value):
    return value.astype(BF16).astype(F32)


def row_index(rows=ROWS):
    return lax.broadcasted_iota(jnp.int32, (rows, LANES), 0)


def block_at(index, size):
    start = index * size
    return pl.ds(start if isinstance(start, int) else pl.multiple_of(start, size), size)


def lanes_at(index, size, group):
    start = index * size + group * LANES
    return pl.ds(start if isinstance(start, int) else pl.multiple_of(start, LANES), LANES)


def columns(source, target, sems, width):
    return lambda i: pltpu.make_async_copy(
        source.at[..., block_at(i, width)], target.at[..., block_at(i, width)], sems.at[i]
    )


def across(scratch, rows_of):
    rows = scratch.shape[0] // rows_of.groups
    for group in range(rows_of.groups):
        scratch[pl.ds(group * rows, rows)] = rows_of(group)
    return [scratch[pl.ds(n, rows_of.groups, stride=rows)] for n in range(rows)]


class Rows:
    def __init__(self, ref, step, width):
        self.ref, self.step, self.width, self.groups = ref, step, width, width // LANES

    def __call__(self, group):
        return self.ref[..., lanes_at(self.step, self.width, group)]


def across_taps(scratch, rows_of, streams):
    groups = rows_of.groups
    for group in range(groups):
        taps = rows_of(group)
        for s in streams:
            for j in range(3):
                scratch[pl.ds((s * 3 + j) * groups + group, 1)] = taps[s, j : j + 1]
    return [[scratch[pl.ds((s * 3 + j) * groups, groups)] for j in range(3)] for s in streams]


def fill_group(scratch, base, pitch, rows_of, at, group):
    lanes = lanes_at(rows_of.step, rows_of.width, group)
    scratch[pl.ds(base + group * pitch + at, CHUNK)] = rows_of.ref[pl.ds(at, CHUNK), lanes].astype(F32)


def fills(scratches, refs, base, pitch, step, width, at):
    return [
        functools.partial(fill_group, scratch, base, pitch, Rows(ref, step, width), at, group)
        for scratch, ref in zip(scratches, refs)
        for group in range(width // LANES)
    ]


def share(calls, j):
    for call in calls[len(calls) * j // CHUNK : len(calls) * (j + 1) // CHUNK]:
        call()


def first_of_last(ids_ref):
    tokens = ids_ref.shape[0]
    low, high = jnp.int32(0), jnp.int32(tokens - 1)
    last = ids_ref[tokens - 1]
    for _ in range((tokens - 1).bit_length()):
        middle = (low + high) // 2
        same = ids_ref[middle] == last
        low, high = jnp.where(same, low, middle + 1), jnp.where(same, middle, high)
    return high


def by_rate(rates, resid):
    rates, resid = list(rates), list(resid)
    for turn in range(len(rates)):
        for i in range(turn % 2, len(rates) - 1, 2):
            low, high = rates[i], rates[i + 1]
            swap = low > high
            rates[i], rates[i + 1] = jnp.minimum(low, high), jnp.maximum(low, high)
            resid[i], resid[i + 1] = jnp.where(swap, resid[i + 1], resid[i]), jnp.where(swap, resid[i], resid[i + 1])
    return rates, resid


def summed(terms):
    while len(terms) > 1:
        terms = [sum(terms[i : i + 2]) for i in range(0, len(terms), 2)]
    return terms[0]


def ends_kernel(
    width, ids_ref, q_hbm, k_hbm, v_hbm, taps_hbm, rates_hbm, resid_hbm,
    info_hbm,
    q_v, k_v, v_v, taps_v, rates_v, resid_v, info_v, k_s, v_s, modes_s, taps_s, held_s, sems,
):
    tokens, channels = k_v.shape
    steps = channels // width
    groups = width // LANES
    chunks = tokens // CHUNK
    pitch = k_s.shape[0] // (2 * groups)
    wide = info_v.shape[2]
    per_step = width // wide
    order = rates_v.shape[0]
    k_in, v_in = (
        columns(source, target, sems.at[pl.ds(i * steps, steps)], width)
        for i, (source, target) in enumerate(((k_hbm, k_v), (v_hbm, v_v)))
    )
    others = [
        pltpu.make_async_copy(source, target, sems.at[3 * steps + i])
        for i, (source, target) in enumerate(
            (
                (rates_hbm, rates_v),
                (resid_hbm, resid_v),
                (taps_hbm, taps_v),
                (q_hbm.at[pl.ds(0, CHUNK)], q_v.at[0]),
                (q_hbm.at[pl.ds(tokens - CHUNK, CHUNK)], q_v.at[1]),
            )
        )
    ]
    going = lambda i: pltpu.make_async_copy(
        info_v.at[block_at(i, per_step)], info_hbm.at[block_at(i, per_step)], sems.at[2 * steps + i]
    )
    for copy in others[:3]:
        copy.start()
    for i in range(steps):
        k_in(i).start()
        v_in(i).start()
        if i == 0:
            for copy in others[3:]:
                copy.start()
    begin = first_of_last(ids_ref)
    chunk0 = begin // CHUNK
    row = row_index()
    marks = jnp.zeros((ROWS, LANES), F32)
    for i, t in enumerate((0, 1, tokens - 2, tokens - 1)):
        marks = jnp.where(row == i + 4, ids_ref[t].astype(F32), marks)

    def base_of(i):
        return pl.multiple_of(jnp.bitwise_and(i, 1) * (groups * pitch), ROWS)

    def fills_of(i, at):
        return fills((k_s, v_s), (k_v, v_v), base_of(i), pitch, i, width, at)

    def arrive(i):
        k_in(i).wait()
        v_in(i).wait()

    for copy in others[:3]:
        copy.wait()
    held = 2 * order + 6

    def hold(i, _):
        rates, resid = by_rate(across(modes_s, Rows(rates_v, i, width)), across(modes_s, Rows(resid_v, i, width)))
        taps = across_taps(taps_s, Rows(taps_v, i, width), (1, 2))
        for n, value in enumerate([jnp.exp(-rate) for rate in rates] + resid + taps[0] + taps[1]):
            held_s[block_at(i * held + n, groups)] = value
        return 0

    lax.fori_loop(0, steps, hold, 0)
    arrive(0)
    for call in fills_of(0, pl.multiple_of(chunk0 * CHUNK, CHUNK)):
        call()
    for copy in others[3:]:
        copy.wait()

    def step(i):

        base = base_of(i)
        values = [held_s[block_at(i * held + n, groups)] for n in range(held)]
        decay, resid = values[:order], values[order : 2 * order]
        taps = [values[2 * order : 2 * order + 3], values[2 * order + 3 :]]

        def chunk(masked, c, carry):
            at = pl.multiple_of(c * CHUNK, CHUNK)
            back1, back2, ends = carry
            ends_here = c == chunks - 1
            if i + 1 < steps:
                pl.when(ends_here)(functools.partial(arrive, i + 1))
            later = jnp.where(ends_here, min(i + 1, steps - 1), i)
            later_at = pl.multiple_of(jnp.where(ends_here, chunk0, c + 1) * CHUNK, CHUNK)
            coming = fills_of(later, later_at)
            for j in range(CHUNK):
                t = at + j
                share(coming, j)
                here = [ref[pl.ds(base + t, groups, stride=pitch)] for ref in (k_s, v_s)]
                if masked:
                    live = (t >= begin).astype(F32)
                    here = [value * live for value in here]
                conv = [taps[s][0] * here[s] + taps[s][1] * back1[s] + taps[s][2] * back2[s] for s in range(2)]
                gated = rounded(conv[0] * conv[1])
                if masked and j < 2:
                    gated = gated * (t >= 2).astype(F32)
                ends = [ends[n] * decay[n] + gated for n in range(order)]
                back1, back2 = here, back1
            return back1, back2, ends

        zero = jnp.zeros((groups, LANES), F32)
        carry = chunk(True, chunk0, ([zero] * 2, [zero] * 2, [zero] * order))
        ends = lax.fori_loop(chunk0 + 1, chunks, functools.partial(chunk, False), carry)[2]
        running = zero
        for n in range(order):
            running = running + resid[n] * ends[n]
            modes_s[pl.ds(n, groups, stride=order)] = running

        for group in range(groups):
            lanes = lanes_at(i, width, group)
            state = modes_s[pl.ds(group * order, order)]
            heads = [ref[pl.ds(0, CHUNK), lanes].astype(F32)[:ROWS] for ref in (k_v, v_v)]
            tails = [ref[pl.ds(tokens - CHUNK, CHUNK), lanes].astype(F32)[ROWS:] for ref in (k_v, v_v)]
            edge = jnp.where(row < 2, heads[0], pltpu.roll(heads[1], 2, 0))
            edge = jnp.where(row < 4, edge, pltpu.roll(tails[0], ROWS - 2, 0))
            edge = jnp.where(row < 6, edge, tails[1])
            at = i * per_step + (group * LANES) // wide
            inner = pl.ds((group * LANES) % wide, LANES)
            info_v[at, pl.ds(0, 16), inner] = jnp.concatenate([state, edge], axis=0).astype(BF16)
            q_head, q_tail = (q_v[j, :, lanes].astype(F32) for j in range(2))
            more = jnp.where(row < 2, q_head[:ROWS], pltpu.roll(q_tail[ROWS:], 4, 0))
            more = jnp.where(row < 4, more, marks)
            info_v[at, pl.ds(16, 8), inner] = more.astype(BF16)
        going(i).start()

    for i in range(steps):
        step(i)
    for i in range(steps):
        going(i).wait()


def carry_kernel(turn, tokens, info_ref, taps_ref, rates_ref, resid_ref, skip_ref, out_ref):
    order, wide = rates_ref.shape
    skip = skip_ref[...]
    rows = lambda ref: [ref[n : n + 1] for n in range(order)]
    rates, resid = (jnp.concatenate(modes, axis=0) for modes in by_rate(rows(rates_ref), rows(resid_ref)))
    decay = jnp.exp(-rates)
    rest = jnp.exp(-float(tokens - 2) * rates)
    row = lax.broadcasted_iota(jnp.int32, (order, wide), 0)

    def down(value, steps):
        if wide % LANES:
            moved = jnp.concatenate([value[order - steps :], value[: order - steps]], axis=0)
        else:
            moved = pltpu.roll(value, steps, 0)
        return jnp.where(row < steps, 0.0, moved)

    taps = [[taps_ref[s, j : j + 1] for j in range(3)] for s in (1, 2, 0)]
    nothing = jnp.zeros((1, wide), F32)
    state = jnp.zeros((order, wide), F32)
    tails, prev0, prev1 = [[nothing, nothing]] * 3, nothing - 1.0, nothing - 1.0
    for block in turn:
        info = info_ref[block].astype(F32)
        line = lambda i: info[order + i : order + i + 1]
        ends = info[:order] - down(info[:order], 1)
        heads = [[line(0), line(1)], [line(2), line(3)], [line(8), line(9)]]
        first0, first1, last0, last1 = (line(12 + i) for i in range(4))
        conv0, conv1 = [], []
        for s in range(3):
            (head0, head1), (tail0, tail1) = heads[s], tails[s]
            conv0.append(
                taps[s][0] * head0
                + taps[s][1] * jnp.where(prev1 == first0, tail1, 0.0)
                + taps[s][2] * jnp.where(prev0 == first0, tail0, 0.0)
            )
            conv1.append(
                taps[s][0] * head1
                + taps[s][1] * jnp.where(first0 == first1, head0, 0.0)
                + taps[s][2] * jnp.where(prev1 == first1, tail1, 0.0)
            )
        gated0, gated1 = rounded(conv0[0] * conv0[1]), rounded(conv1[0] * conv1[1])
        state0 = decay * (state * (prev1 == first0).astype(F32)) + resid * gated0
        state1 = decay * (state0 * (first0 == first1).astype(F32)) + resid * gated1
        long0 = jnp.sum(state0, axis=0, keepdims=True)
        long1 = jnp.sum(state1, axis=0, keepdims=True)
        mixed = jnp.where(row == 0, conv0[2] * (long0 + skip * gated0), conv1[2] * (long1 + skip * gated1))
        running = state1
        for steps in (1, 2, 4):
            running = running + down(running, steps)
        out_ref[block] = jnp.concatenate([running, mixed], axis=0).astype(BF16)
        state = ends + rest * (state1 * (first1 == last1).astype(F32))
        tails = [[line(4), line(5)], [line(6), line(7)], [line(10), line(11)]]
        prev0, prev1 = last0, last1


def local_kernel(
    width, first_step, count, filled, turn, ids_ref, q_hbm, k_hbm, v_hbm, taps_hbm, rates_hbm, resid_hbm, skip_hbm, *rest
):
    (
        q_v, k_v, v_v, taps_v, rates_v, resid_v, skip_v, q_s, k_s, v_s, modes_s, taps_s, held_s, sems,
    ) = rest[-14:]
    part_ref, query_ref, table_ref, *own_refs = rest[filled:-14]
    tokens, channels = q_v.shape
    owned = []
    if own_refs:
        mine = own_refs[0].shape[-1]
        lanes = pl.ds(pl.multiple_of(place_in(turn) * mine, mine), mine)
        owned = [
            (source.at[..., lanes], target)
            for source, target in zip((taps_hbm, rates_hbm, resid_hbm, skip_hbm), own_refs)
        ]
    groups = width // LANES
    pitch = q_s.shape[0] // groups
    chunks = tokens // CHUNK
    order = rates_v.shape[0]
    end_step = first_step + count
    scratches = (q_s, k_s, v_s)
    streams = [
        lambda i, s=s, source=source, target=target: pltpu.make_async_copy(
            source.at[:, block_at(i, width)], target.at[:, block_at(i, width)], sems.at[s * count + i - first_step]
        )
        for s, (source, target) in enumerate(((q_hbm, q_v), (k_hbm, k_v), (v_hbm, v_v)))
    ]
    part = pl.ds(first_step * width, count * width)
    own = [pltpu.make_async_copy(source, target, sems.at[3 * count + 4 + i]) for i, (source, target) in enumerate(owned)]
    others = [
        pltpu.make_async_copy(source.at[..., part], target.at[..., part], sems.at[3 * count + i])
        for i, (source, target) in enumerate(
            ((taps_hbm, taps_v), (rates_hbm, rates_v), (resid_hbm, resid_v), (skip_hbm, skip_v))
        )
    ]
    for copy in others:
        copy.start()
    for i in range(first_step, end_step):
        for copy in streams:
            copy(i).start()
    for copy in own:
        copy.start()

    def arrive(i):
        for copy in streams:
            copy(i).wait()

    def fills_of(i, at):
        return fills(scratches, (q_v, k_v, v_v), 0, pitch, i, width, at)

    for copy in others:
        copy.wait()
    held = 2 * order + 10

    def hold(i, _):
        for group in range(groups):
            taps_s[pl.ds(9 * groups + group, 1)] = skip_v[:, lanes_at(i, width, group)]
        rates, resid = by_rate(across(modes_s, Rows(rates_v, i, width)), across(modes_s, Rows(resid_v, i, width)))
        decay = [jnp.exp(-rate) for rate in rates]
        taps = across_taps(taps_s, Rows(taps_v, i, width), (0, 1, 2))
        skip = taps_s[pl.ds(9 * groups, groups)]
        for n, value in enumerate(decay + resid + taps[0] + taps[1] + taps[2] + [skip]):
            held_s[block_at((i - first_step) * held + n, groups)] = value
        for n in range(order):
            table_ref[block_at(i * order + n, groups)] = decay[n]
        return 0

    lax.fori_loop(first_step, end_step, hold, 0)
    arrive(first_step)
    for call in fills_of(first_step, 0):
        call()

    def step(i, _):
        values = [held_s[block_at((i - first_step) * held + n, groups)] for n in range(held)]
        decay, resid, skip = values[:order], values[order : 2 * order], values[-1]
        taps = [values[2 * order + 3 * s : 2 * order + 3 * s + 3] for s in range(3)]

        def row_of(ref, t):
            return ref[pl.ds(t, groups, stride=pitch)]

        def token(t, carry, masked):
            back1, back2, states = carry
            now = [row_of(ref, t) for ref in scratches]
            if masked:
                same = (ids_ref[t] == ids_ref[t - 1]).astype(F32)
                back1 = [value * same for value in back1]
                back2 = [value * same for value in back2]
                states = [value * same for value in states]
            conv = [taps[s][0] * now[s] + taps[s][1] * back1[s] + taps[s][2] * back2[s] for s in range(3)]
            gated = rounded(conv[1] * conv[2])
            states = [states[n] * decay[n] + gated for n in range(order)]
            total = summed([states[n] * resid[n] for n in range(order)])
            live = (ids_ref[t] == ids_ref[1]).astype(F32)
            return (now, back1, states), conv[0] * (total + skip * gated), conv[0] * live

        def chunk(masked, skipped, at, later, later_at, carry):
            coming = fills_of(later, later_at)
            for j in range(skipped):
                share(coming, j)
            for j in range(skipped, CHUNK, 2):
                share(coming, j)
                carry, part0, query0 = token(at + j, carry, masked)
                share(coming, j + 1)
                carry, part1, query1 = token(at + j + 1, carry, masked)
                pair = pl.ds(pl.multiple_of((i * tokens + at + j) * groups, 2 * groups), 2 * groups)
                part_ref[pair] = jnp.concatenate([part0, part1], axis=0).astype(BF16)
                query_ref[pair] = jnp.concatenate([query0, query1], axis=0).astype(BF16)
            return carry

        def any_chunk(c, carry):
            at = pl.multiple_of(c * CHUNK, CHUNK)
            ends_here = c == chunks - 1
            pl.when(ends_here & (i + 1 < end_step))(functools.partial(arrive, i + 1))
            later = jnp.where(ends_here, jnp.minimum(i + 1, end_step - 1), i)
            later_at = pl.multiple_of(jnp.where(ends_here, 0, at + CHUNK), CHUNK)
            return lax.cond(
                ids_ref[at - 1] == ids_ref[at + CHUNK - 1],
                functools.partial(chunk, False, 0, at, later, later_at),
                functools.partial(chunk, True, 0, at, later, later_at),
                carry,
            )

        back1, back2 = ([row_of(ref, t) for ref in scratches] for t in (1, 0))
        same = (ids_ref[1] == ids_ref[0]).astype(F32)
        carry = (back1, [value * same for value in back2], [jnp.zeros((groups, LANES), F32)] * order)
        carry = chunk(True, 2, 0, i, CHUNK, carry)
        lax.fori_loop(1, chunks, any_chunk, carry)
        return 0

    lax.fori_loop(first_step, end_step, step, 0)
    for copy in own:
        copy.wait()


def finish_kernel(width, state_ref, part_ref, query_ref, table_ref, out_hbm, out_v, out_s, modes_s, sems):
    tokens, channels = out_v.shape
    steps = channels // width
    groups = width // LANES
    pitch = out_s.shape[0] // groups
    wide = state_ref.shape[2]
    order = table_ref.shape[0] // (groups * steps)
    going = columns(out_v, out_hbm, sems, width)

    def step(i, _):
        decay = [table_ref[block_at(i * order + n, groups)] for n in range(order)]
        for group in range(groups):
            chunk_at = i * (width // wide) + (group * LANES) // wide
            modes_s[pl.ds(group * TOLD, TOLD)] = state_ref[chunk_at, :, pl.ds((group * LANES) % wide, LANES)].astype(F32)
        running = [modes_s[pl.ds(n, groups, stride=TOLD)] for n in range(order)]
        weights = [running[0]] + [running[n] - running[n - 1] for n in range(1, order)]

        def pair(t, weights):
            at = pl.ds(pl.multiple_of((i * tokens + t) * groups, 2 * groups), 2 * groups)
            part, live_query = part_ref[at].astype(F32), query_ref[at].astype(F32)
            for k in range(2):
                weights = [weights[n] * decay[n] for n in range(order)]
                rows = slice(k * groups, (k + 1) * groups)
                out_s[pl.ds(t + k, groups, stride=pitch)] = part[rows] + live_query[rows] * summed(weights)
            return weights

        def give(at, group):
            out_v[pl.ds(at, CHUNK), lanes_at(i, width, group)] = out_s[pl.ds(group * pitch + at, CHUNK)].astype(BF16)

        def gives(at):
            return [functools.partial(give, at, group) for group in range(groups)]

        def chunk(c, weights):
            at = pl.multiple_of(c * CHUNK, CHUNK)
            done = gives(at - CHUNK)
            for j in range(0, CHUNK, 2):
                share(done, j)
                share(done, j + 1)
                weights = pair(at + j, weights)
            return weights

        for t in range(2):
            out_s[pl.ds(t, groups, stride=pitch)] = modes_s[pl.ds(order + t, groups, stride=TOLD)]
        for t in range(2, CHUNK, 2):
            weights = pair(t, weights)
        lax.fori_loop(1, tokens // CHUNK, chunk, weights)
        for call in gives(tokens - CHUNK):
            call()
        going(i).start()
        return 0

    lax.fori_loop(0, steps, step, 0)
    for i in range(steps):
        going(i).wait()


def on_device(query, keyed, valued, short_taps, rates, residues, skip_gain, doc_ids):
    tokens, channels = query.shape
    order = rates.shape[0]
    n_ctx = lax.axis_size("ctx")
    meeting = meeting_order(n_ctx)
    turn = [meeting.index(i) for i in range(n_ctx)]
    exchange = lambda value: lax.all_to_all(
        value, "ctx", split_axis=0, concat_axis=0, tiled=True, axis_index_groups=[meeting]
    )
    own = channels // n_ctx
    wide = own if own % LANES == 0 else LANES
    chunks = channels // wide
    width = min(channels, 8 * LANES)
    steps = channels // width
    groups = width // LANES
    pitch = tokens + ROWS
    params = pltpu.CompilerParams(vmem_limit_bytes=24 * 1024 * 1024)
    anywhere = pl.BlockSpec(memory_space=pl.ANY)
    smem = pl.BlockSpec(memory_space=pltpu.SMEM)
    vmem = pl.BlockSpec(memory_space=pltpu.VMEM)
    hbm = lambda *arrays: [pltpu.with_memory_space_constraint(array, pltpu.HBM) for array in arrays]
    near = lambda *arrays: [pltpu.with_memory_space_constraint(array, pltpu.VMEM) for array in arrays]

    modes_scratch = pltpu.VMEM((groups * order, LANES), F32)
    skip_gain = skip_gain.reshape(1, channels)
    tall = [pltpu.VMEM((channels // LANES * tokens, LANES), dtype) for dtype in (BF16, BF16)]
    table = pltpu.VMEM((steps * order * groups, LANES), F32)
    taps_v, modes_v = pltpu.VMEM((3, 3, channels), F32), pltpu.VMEM((order, channels), F32)

    info = pl.pallas_call(
        functools.partial(ends_kernel, width),
        in_specs=[smem] + [anywhere] * 6,
        out_specs=anywhere,
        out_shape=pltpu.HBM((chunks, INFO, wide), BF16),
        scratch_shapes=[
            pltpu.VMEM((2, 2 * ROWS, channels), BF16),
            pltpu.VMEM((tokens, channels), BF16),
            pltpu.VMEM((tokens, channels), BF16),
            taps_v,
            modes_v,
            modes_v,
            pltpu.VMEM((chunks, INFO, wide), BF16),
            pltpu.VMEM((2 * groups * pitch, LANES), F32),
            pltpu.VMEM((2 * groups * pitch, LANES), F32),
            modes_scratch,
            pltpu.VMEM((9 * groups, LANES), F32),
            pltpu.VMEM((steps * (2 * order + 6) * groups, LANES), F32),
            pltpu.SemaphoreType.DMA((3 * steps + 5,)),
        ],
        compiler_params=params,
        name="block_ends",
    )(*hbm(doc_ids, query, keyed, valued, short_taps, rates, residues))

    if wide != own:
        info = info.transpose(1, 0, 2).reshape(INFO, n_ctx, own).transpose(1, 0, 2)
    info = exchange(info)

    def local_scan(first, count, filled, owned=()):
        return pl.pallas_call(
            functools.partial(local_kernel, width, first, count, len(filled), turn),
            in_specs=[smem] + [anywhere] * 7 + [vmem] * len(filled),
            out_specs=[vmem] * (3 + len(owned)),
            out_shape=[*tall, table, *owned],
            input_output_aliases={8 + i: i for i in range(len(filled))},
            scratch_shapes=[
                pltpu.VMEM((tokens, channels), BF16),
                pltpu.VMEM((tokens, channels), BF16),
                pltpu.VMEM((tokens, channels), BF16),
                taps_v,
                modes_v,
                modes_v,
                pltpu.VMEM((1, channels), F32),
                *[pltpu.VMEM((groups * pitch, LANES), F32)] * 3,
                modes_scratch,
                pltpu.VMEM((10 * groups, LANES), F32),
                pltpu.VMEM((count * (2 * order + 10) * groups, LANES), F32),
                pltpu.SemaphoreType.DMA((3 * count + 4 + len(owned),)),
            ],
            compiler_params=params,
            cost_estimate=pl.CostEstimate(
                flops=count * tokens * width * 64, bytes_accessed=count * tokens * width * 14, transcendentals=0
            ),
            name="local_scan",
        )(
            *hbm(doc_ids, query, keyed, valued, short_taps, rates, residues, skip_gain), *near(*filled),
        )

    half = steps // 2 or steps
    if own % LANES == 0:
        owned = [pltpu.VMEM(value.shape[:-1] + (own,), F32) for value in (short_taps, rates, residues, skip_gain)]
        *filled, own_taps, own_rates, own_resid, own_skip = local_scan(0, half, [], owned)
        own_params = [own_taps, own_rates, own_resid, own_skip]
    else:
        filled = local_scan(0, half, [])
        at = place_in(turn) * own
        own_params = [
            lax.dynamic_slice_in_dim(value, at, own, value.ndim - 1)
            for value in (short_taps, rates, residues, skip_gain)
        ]
    info, *filled = lax.optimization_barrier((info, *filled))
    state = pl.pallas_call(
        functools.partial(carry_kernel, turn, tokens),
        out_shape=pltpu.HBM((n_ctx, TOLD, own), BF16),
        compiler_params=params,
        name="block_carry",
    )(*near(info, *own_params))
    state, *filled = lax.optimization_barrier((state, *filled))
    state = exchange(state)
    if half < steps:
        filled = local_scan(half, steps - half, filled)
    if wide != own:
        state = state.transpose(1, 0, 2).reshape(TOLD, chunks, wide).transpose(1, 0, 2)

    return pl.pallas_call(
        functools.partial(finish_kernel, width),
        in_specs=[vmem] * 4,
        out_specs=anywhere,
        out_shape=pltpu.HBM((tokens, channels), BF16),
        scratch_shapes=[
            pltpu.VMEM((tokens, channels), BF16),
            pltpu.VMEM((groups * pitch, LANES), F32),
            pltpu.VMEM((groups * TOLD, LANES), F32),
            pltpu.SemaphoreType.DMA((steps,)),
        ],
        compiler_params=params,
        name="add_carry",
    )(*near(state, *filled))


def solution(mesh):
    return jax.shard_map(
        on_device,
        mesh=mesh,
        in_specs=(
            P("ctx", "tp"),
            P("ctx", "tp"),
            P("ctx", "tp"),
            P(None, None, "tp"),
            P(None, "tp"),
            P(None, "tp"),
            P("tp"),
            P("ctx"),
        ),
        out_specs=P("ctx", "tp"),
        check_vma=False,
    )
```

```python
import functools

import jax
import jax.numpy as jnp
from jax import lax
from jax.experimental import pallas as pl
from jax.experimental.pallas import tpu as pltpu
from jax.sharding import PartitionSpec as P

LANES = 128
ROWS = 8
CHUNK = 16
INFO = 24
TOLD = 16
F32 = jnp.float32
BF16 = jnp.bfloat16


def meeting_order(count):
    first = 5 * count // 8
    return [(first + i) % count for i in range(count)]


def place_in(turn):
    me = lax.axis_index("ctx")
    place = jnp.int32(0)
    for i, at in enumerate(turn):
        place = jnp.where(me == i, at, place)
    return place


def rounded(value):
    return value.astype(BF16).astype(F32)


def row_index(rows=ROWS):
    return lax.broadcasted_iota(jnp.int32, (rows, LANES), 0)


def block_at(index, size):
    start = index * size
    return pl.ds(start if isinstance(start, int) else pl.multiple_of(start, size), size)


def lanes_at(index, size, group):
    start = index * size + group * LANES
    return pl.ds(start if isinstance(start, int) else pl.multiple_of(start, LANES), LANES)


def columns(source, target, sems, width):
    return lambda i: pltpu.make_async_copy(
        source.at[..., block_at(i, width)], target.at[..., block_at(i, width)], sems.at[i]
    )


def across(scratch, rows_of):
    rows = scratch.shape[0] // rows_of.groups
    for group in range(rows_of.groups):
        scratch[pl.ds(group * rows, rows)] = rows_of(group)
    return [scratch[pl.ds(n, rows_of.groups, stride=rows)] for n in range(rows)]


class Rows:
    def __init__(self, ref, step, width):
        self.ref, self.step, self.width, self.groups = ref, step, width, width // LANES

    def __call__(self, group):
        return self.ref[..., lanes_at(self.step, self.width, group)]


def across_taps(scratch, rows_of, streams):
    groups = rows_of.groups
    for group in range(groups):
        taps = rows_of(group)
        for s in streams:
            for j in range(3):
                scratch[pl.ds((s * 3 + j) * groups + group, 1)] = taps[s, j : j + 1]
    return [[scratch[pl.ds((s * 3 + j) * groups, groups)] for j in range(3)] for s in streams]


def fill_group(scratch, base, pitch, rows_of, at, group):
    lanes = lanes_at(rows_of.step, rows_of.width, group)
    scratch[pl.ds(base + group * pitch + at, CHUNK)] = rows_of.ref[pl.ds(at, CHUNK), lanes].astype(F32)


def fills(scratches, refs, base, pitch, step, width, at):
    return [
        functools.partial(fill_group, scratch, base, pitch, Rows(ref, step, width), at, group)
        for scratch, ref in zip(scratches, refs)
        for group in range(width // LANES)
    ]


def share(calls, j):
    for call in calls[len(calls) * j // CHUNK : len(calls) * (j + 1) // CHUNK]:
        call()


def first_of_last(ids_ref):
    tokens = ids_ref.shape[0]
    low, high = jnp.int32(0), jnp.int32(tokens - 1)
    last = ids_ref[tokens - 1]
    for _ in range((tokens - 1).bit_length()):
        middle = (low + high) // 2
        same = ids_ref[middle] == last
        low, high = jnp.where(same, low, middle + 1), jnp.where(same, middle, high)
    return high


def by_rate(rates, resid):
    rates, resid = list(rates), list(resid)
    for turn in range(len(rates)):
        for i in range(turn % 2, len(rates) - 1, 2):
            low, high = rates[i], rates[i + 1]
            swap = low > high
            rates[i], rates[i + 1] = jnp.minimum(low, high), jnp.maximum(low, high)
            resid[i], resid[i + 1] = jnp.where(swap, resid[i + 1], resid[i]), jnp.where(swap, resid[i], resid[i + 1])
    return rates, resid


def summed(terms):
    while len(terms) > 1:
        terms = [sum(terms[i : i + 2]) for i in range(0, len(terms), 2)]
    return terms[0]


def ends_kernel(
    width, ids_ref, q_hbm, k_hbm, v_hbm, taps_hbm, rates_hbm, resid_hbm,
    info_hbm,
    q_v, k_v, v_v, taps_v, rates_v, resid_v, info_v, k_s, v_s, modes_s, taps_s, held_s, sems,
):
    tokens, channels = k_v.shape
    steps = channels // width
    groups = width // LANES
    chunks = tokens // CHUNK
    pitch = k_s.shape[0] // (2 * groups)
    wide = info_v.shape[2]
    per_step = width // wide
    order = rates_v.shape[0]
    k_in, v_in = (
        columns(source, target, sems.at[pl.ds(i * steps, steps)], width)
        for i, (source, target) in enumerate(((k_hbm, k_v), (v_hbm, v_v)))
    )
    others = [
        pltpu.make_async_copy(source, target, sems.at[3 * steps + i])
        for i, (source, target) in enumerate(
            (
                (rates_hbm, rates_v),
                (resid_hbm, resid_v),
                (taps_hbm, taps_v),
                (q_hbm.at[pl.ds(0, CHUNK)], q_v.at[0]),
                (q_hbm.at[pl.ds(tokens - CHUNK, CHUNK)], q_v.at[1]),
            )
        )
    ]
    going = lambda i: pltpu.make_async_copy(
        info_v.at[block_at(i, per_step)], info_hbm.at[block_at(i, per_step)], sems.at[2 * steps + i]
    )
    for copy in others[:3]:
        copy.start()
    for i in range(steps):
        k_in(i).start()
        v_in(i).start()
        if i == 0:
            for copy in others[3:]:
                copy.start()
    begin = first_of_last(ids_ref)
    chunk0 = begin // CHUNK
    row = row_index()
    marks = jnp.zeros((ROWS, LANES), F32)
    for i, t in enumerate((0, 1, tokens - 2, tokens - 1)):
        marks = jnp.where(row == i + 4, ids_ref[t].astype(F32), marks)

    def base_of(i):
        return pl.multiple_of(jnp.bitwise_and(i, 1) * (groups * pitch), ROWS)

    def fills_of(i, at):
        return fills((k_s, v_s), (k_v, v_v), base_of(i), pitch, i, width, at)

    def arrive(i):
        k_in(i).wait()
        v_in(i).wait()

    for copy in others[:3]:
        copy.wait()
    held = 2 * order + 6

    def hold(i, _):
        rates, resid = by_rate(across(modes_s, Rows(rates_v, i, width)), across(modes_s, Rows(resid_v, i, width)))
        taps = across_taps(taps_s, Rows(taps_v, i, width), (1, 2))
        for n, value in enumerate([jnp.exp(-rate) for rate in rates] + resid + taps[0] + taps[1]):
            held_s[block_at(i * held + n, groups)] = value
        return 0

    lax.fori_loop(0, steps, hold, 0)
    arrive(0)
    for call in fills_of(0, pl.multiple_of(chunk0 * CHUNK, CHUNK)):
        call()
    for copy in others[3:]:
        copy.wait()

    def step(i):

        base = base_of(i)
        values = [held_s[block_at(i * held + n, groups)] for n in range(held)]
        decay, resid = values[:order], values[order : 2 * order]
        taps = [values[2 * order : 2 * order + 3], values[2 * order + 3 :]]

        def chunk(masked, c, carry):
            at = pl.multiple_of(c * CHUNK, CHUNK)
            back1, back2, ends = carry
            ends_here = c == chunks - 1
            if i + 1 < steps:
                pl.when(ends_here)(functools.partial(arrive, i + 1))
            later = jnp.where(ends_here, min(i + 1, steps - 1), i)
            later_at = pl.multiple_of(jnp.where(ends_here, chunk0, c + 1) * CHUNK, CHUNK)
            coming = fills_of(later, later_at)
            for j in range(CHUNK):
                t = at + j
                share(coming, j)
                here = [ref[pl.ds(base + t, groups, stride=pitch)] for ref in (k_s, v_s)]
                if masked:
                    live = (t >= begin).astype(F32)
                    here = [value * live for value in here]
                conv = [taps[s][0] * here[s] + taps[s][1] * back1[s] + taps[s][2] * back2[s] for s in range(2)]
                gated = rounded(conv[0] * conv[1])
                if masked and j < 2:
                    gated = gated * (t >= 2).astype(F32)
                ends = [ends[n] * decay[n] + gated for n in range(order)]
                back1, back2 = here, back1
            return back1, back2, ends

        zero = jnp.zeros((groups, LANES), F32)
        carry = chunk(True, chunk0, ([zero] * 2, [zero] * 2, [zero] * order))
        ends = lax.fori_loop(chunk0 + 1, chunks, functools.partial(chunk, False), carry)[2]
        running = zero
        for n in range(order):
            running = running + resid[n] * ends[n]
            modes_s[pl.ds(n, groups, stride=order)] = running

        for group in range(groups):
            lanes = lanes_at(i, width, group)
            state = modes_s[pl.ds(group * order, order)]
            heads = [ref[pl.ds(0, CHUNK), lanes].astype(F32)[:ROWS] for ref in (k_v, v_v)]
            tails = [ref[pl.ds(tokens - CHUNK, CHUNK), lanes].astype(F32)[ROWS:] for ref in (k_v, v_v)]
            edge = jnp.where(row < 2, heads[0], pltpu.roll(heads[1], 2, 0))
            edge = jnp.where(row < 4, edge, pltpu.roll(tails[0], ROWS - 2, 0))
            edge = jnp.where(row < 6, edge, tails[1])
            at = i * per_step + (group * LANES) // wide
            inner = pl.ds((group * LANES) % wide, LANES)
            info_v[at, pl.ds(0, 16), inner] = jnp.concatenate([state, edge], axis=0).astype(BF16)
            q_head, q_tail = (q_v[j, :, lanes].astype(F32) for j in range(2))
            more = jnp.where(row < 2, q_head[:ROWS], pltpu.roll(q_tail[ROWS:], 4, 0))
            more = jnp.where(row < 4, more, marks)
            info_v[at, pl.ds(16, 8), inner] = more.astype(BF16)
        going(i).start()

    for i in range(steps):
        step(i)
    for i in range(steps):
        going(i).wait()


def carry_kernel(turn, tokens, info_ref, taps_ref, rates_ref, resid_ref, skip_ref, out_ref):
    order, wide = rates_ref.shape
    skip = skip_ref[...]
    rows = lambda ref: [ref[n : n + 1] for n in range(order)]
    rates, resid = (jnp.concatenate(modes, axis=0) for modes in by_rate(rows(rates_ref), rows(resid_ref)))
    decay = jnp.exp(-rates)
    rest = jnp.exp(-float(tokens - 2) * rates)
    row = lax.broadcasted_iota(jnp.int32, (order, wide), 0)
    even = row % 2 == 0

    def turned(value, steps):
        if wide % LANES:
            return jnp.concatenate([value[order - steps :], value[: order - steps]], axis=0)
        return pltpu.roll(value, steps, 0)

    def down(value, steps):
        return jnp.where(row < steps, 0.0, turned(value, steps))

    def tap(j):
        key, value, query = (jnp.broadcast_to(taps_ref[s, j : j + 1], (order, wide)) for s in (1, 2, 0))
        return jnp.where(row < 2, key, jnp.where(row < 4, value, query))

    taps = [tap(j) for j in range(3)]
    state = jnp.zeros((order, wide), F32)
    tails, prev0, prev1 = state, jnp.full((1, wide), -1.0, F32), jnp.full((1, wide), -1.0, F32)
    for block in turn:
        info = info_ref[block].astype(F32)
        running, edge, more = (info[i * ROWS : (i + 1) * ROWS] for i in range(3))
        ends = running - down(running, 1)
        first0, first1, last0, last1 = (more[4 + i : 5 + i] for i in range(4))
        same = lambda one, other: (one == other).astype(F32)
        entering, inside = same(prev1, first0), same(first0, first1)
        heads = jnp.where(row < 4, edge, turned(more, 4))
        back1 = jnp.where(even, turned(tails, order - 1), turned(heads, 1))
        conv = (
            taps[0] * heads
            + taps[1] * (back1 * jnp.where(even, entering, inside))
            + taps[2] * (tails * jnp.where(even, same(prev0, first0), same(prev1, first1)))
        )
        gated = rounded(conv * turned(conv, order - 2))
        state0 = decay * (state * entering) + resid * gated[0:1]
        state1 = decay * (state0 * inside) + resid * gated[1:2]
        long0 = jnp.sum(state0, axis=0, keepdims=True)
        long1 = jnp.sum(state1, axis=0, keepdims=True)
        mixed = turned(conv, order - 4) * (jnp.where(row == 0, long0, long1) + skip * gated)
        running = state1
        for steps in (1, 2, 4):
            running = running + down(running, steps)
        out_ref[block] = jnp.concatenate([running, mixed], axis=0).astype(BF16)
        state = ends + rest * (state1 * same(first1, last1))
        tails = jnp.where(row < 4, turned(edge, 4), turned(more, 2))
        prev0, prev1 = last0, last1


def local_kernel(
    width, first_step, count, filled, turn, ids_ref, q_hbm, k_hbm, v_hbm, taps_hbm, rates_hbm, resid_hbm, skip_hbm, *rest
):
    (
        q_v, k_v, v_v, taps_v, rates_v, resid_v, skip_v, q_s, k_s, v_s, modes_s, taps_s, held_s, sems,
    ) = rest[-14:]
    part_ref, query_ref, table_ref, *own_refs = rest[filled:-14]
    tokens, channels = q_v.shape
    owned = []
    if own_refs:
        mine = own_refs[0].shape[-1]
        lanes = pl.ds(pl.multiple_of(place_in(turn) * mine, mine), mine)
        owned = [
            (source.at[..., lanes], target)
            for source, target in zip((taps_hbm, rates_hbm, resid_hbm, skip_hbm), own_refs)
        ]
    groups = width // LANES
    pitch = q_s.shape[0] // groups
    chunks = tokens // CHUNK
    order = rates_v.shape[0]
    end_step = first_step + count
    scratches = (q_s, k_s, v_s)
    streams = [
        lambda i, s=s, source=source, target=target: pltpu.make_async_copy(
            source.at[:, block_at(i, width)], target.at[:, block_at(i, width)], sems.at[s * count + i - first_step]
        )
        for s, (source, target) in enumerate(((q_hbm, q_v), (k_hbm, k_v), (v_hbm, v_v)))
    ]
    part = pl.ds(first_step * width, count * width)
    own = [pltpu.make_async_copy(source, target, sems.at[3 * count + 4 + i]) for i, (source, target) in enumerate(owned)]
    others = [
        pltpu.make_async_copy(source.at[..., part], target.at[..., part], sems.at[3 * count + i])
        for i, (source, target) in enumerate(
            ((taps_hbm, taps_v), (rates_hbm, rates_v), (resid_hbm, resid_v), (skip_hbm, skip_v))
        )
    ]
    for copy in others:
        copy.start()
    for i in range(first_step, end_step):
        for copy in streams:
            copy(i).start()
    for copy in own:
        copy.start()

    def arrive(i):
        for copy in streams:
            copy(i).wait()

    def fills_of(i, at):
        return fills(scratches, (q_v, k_v, v_v), 0, pitch, i, width, at)

    for copy in others:
        copy.wait()
    held = 2 * order + 10

    def hold(i, _):
        for group in range(groups):
            taps_s[pl.ds(9 * groups + group, 1)] = skip_v[:, lanes_at(i, width, group)]
        rates, resid = by_rate(across(modes_s, Rows(rates_v, i, width)), across(modes_s, Rows(resid_v, i, width)))
        decay = [jnp.exp(-rate) for rate in rates]
        taps = across_taps(taps_s, Rows(taps_v, i, width), (0, 1, 2))
        skip = taps_s[pl.ds(9 * groups, groups)]
        for n, value in enumerate(decay + resid + taps[0] + taps[1] + taps[2] + [skip]):
            held_s[block_at((i - first_step) * held + n, groups)] = value
        for n in range(order):
            table_ref[block_at(i * order + n, groups)] = decay[n]
        return 0

    lax.fori_loop(first_step, end_step, hold, 0)
    arrive(first_step)
    for call in fills_of(first_step, 0):
        call()

    def step(i, _):
        values = [held_s[block_at((i - first_step) * held + n, groups)] for n in range(held)]
        decay, resid, skip = values[:order], values[order : 2 * order], values[-1]
        taps = [values[2 * order + 3 * s : 2 * order + 3 * s + 3] for s in range(3)]

        def row_of(ref, t):
            return ref[pl.ds(t, groups, stride=pitch)]

        def token(t, carry, masked):
            back1, back2, states = carry
            now = [row_of(ref, t) for ref in scratches]
            if masked:
                same = (ids_ref[t] == ids_ref[t - 1]).astype(F32)
                back1 = [value * same for value in back1]
                back2 = [value * same for value in back2]
                states = [value * same for value in states]
            conv = [taps[s][0] * now[s] + taps[s][1] * back1[s] + taps[s][2] * back2[s] for s in range(3)]
            gated = rounded(conv[1] * conv[2])
            states = [states[n] * decay[n] + gated for n in range(order)]
            total = summed([states[n] * resid[n] for n in range(order)])
            live = (ids_ref[t] == ids_ref[1]).astype(F32)
            return (now, back1, states), conv[0] * (total + skip * gated), conv[0] * live

        def chunk(masked, skipped, at, later, later_at, carry):
            coming = fills_of(later, later_at)
            for j in range(skipped):
                share(coming, j)
            for j in range(skipped, CHUNK, 2):
                share(coming, j)
                carry, part0, query0 = token(at + j, carry, masked)
                share(coming, j + 1)
                carry, part1, query1 = token(at + j + 1, carry, masked)
                pair = pl.ds(pl.multiple_of((i * tokens + at + j) * groups, 2 * groups), 2 * groups)
                part_ref[pair] = jnp.concatenate([part0, part1], axis=0).astype(BF16)
                query_ref[pair] = jnp.concatenate([query0, query1], axis=0).astype(BF16)
            return carry

        def any_chunk(c, carry):
            at = pl.multiple_of(c * CHUNK, CHUNK)
            ends_here = c == chunks - 1
            pl.when(ends_here & (i + 1 < end_step))(functools.partial(arrive, i + 1))
            later = jnp.where(ends_here, jnp.minimum(i + 1, end_step - 1), i)
            later_at = pl.multiple_of(jnp.where(ends_here, 0, at + CHUNK), CHUNK)
            return lax.cond(
                ids_ref[at - 1] == ids_ref[at + CHUNK - 1],
                functools.partial(chunk, False, 0, at, later, later_at),
                functools.partial(chunk, True, 0, at, later, later_at),
                carry,
            )

        back1, back2 = ([row_of(ref, t) for ref in scratches] for t in (1, 0))
        same = (ids_ref[1] == ids_ref[0]).astype(F32)
        carry = (back1, [value * same for value in back2], [jnp.zeros((groups, LANES), F32)] * order)
        carry = chunk(True, 2, 0, i, CHUNK, carry)
        lax.fori_loop(1, chunks, any_chunk, carry)
        return 0

    lax.fori_loop(first_step, end_step, step, 0)
    for copy in own:
        copy.wait()


def finish_kernel(width, state_ref, part_ref, query_ref, table_ref, out_hbm, out_v, out_s, modes_s, sems):
    tokens, channels = out_v.shape
    steps = channels // width
    groups = width // LANES
    pitch = out_s.shape[0] // groups
    wide = state_ref.shape[2]
    order = table_ref.shape[0] // (groups * steps)
    going = columns(out_v, out_hbm, sems, width)

    def step(i, _):
        decay = [table_ref[block_at(i * order + n, groups)] for n in range(order)]
        for group in range(groups):
            chunk_at = i * (width // wide) + (group * LANES) // wide
            modes_s[pl.ds(group * TOLD, TOLD)] = state_ref[chunk_at, :, pl.ds((group * LANES) % wide, LANES)].astype(F32)
        running = [modes_s[pl.ds(n, groups, stride=TOLD)] for n in range(order)]
        weights = [running[0]] + [running[n] - running[n - 1] for n in range(1, order)]

        def pair(t, weights):
            at = pl.ds(pl.multiple_of((i * tokens + t) * groups, 2 * groups), 2 * groups)
            part, live_query = part_ref[at].astype(F32), query_ref[at].astype(F32)
            for k in range(2):
                weights = [weights[n] * decay[n] for n in range(order)]
                rows = slice(k * groups, (k + 1) * groups)
                out_s[pl.ds(t + k, groups, stride=pitch)] = part[rows] + live_query[rows] * summed(weights)
            return weights

        def give(at, group):
            out_v[pl.ds(at, CHUNK), lanes_at(i, width, group)] = out_s[pl.ds(group * pitch + at, CHUNK)].astype(BF16)

        def gives(at):
            return [functools.partial(give, at, group) for group in range(groups)]

        def chunk(c, weights):
            at = pl.multiple_of(c * CHUNK, CHUNK)
            done = gives(at - CHUNK)
            for j in range(0, CHUNK, 2):
                share(done, j)
                share(done, j + 1)
                weights = pair(at + j, weights)
            return weights

        for t in range(2):
            out_s[pl.ds(t, groups, stride=pitch)] = modes_s[pl.ds(order + t, groups, stride=TOLD)]
        for t in range(2, CHUNK, 2):
            weights = pair(t, weights)
        lax.fori_loop(1, tokens // CHUNK, chunk, weights)
        for call in gives(tokens - CHUNK):
            call()
        going(i).start()
        return 0

    lax.fori_loop(0, steps, step, 0)
    for i in range(steps):
        going(i).wait()


def on_device(query, keyed, valued, short_taps, rates, residues, skip_gain, doc_ids):
    tokens, channels = query.shape
    order = rates.shape[0]
    n_ctx = lax.axis_size("ctx")
    meeting = meeting_order(n_ctx)
    turn = [meeting.index(i) for i in range(n_ctx)]
    exchange = lambda value: lax.all_to_all(
        value, "ctx", split_axis=0, concat_axis=0, tiled=True, axis_index_groups=[meeting]
    )
    own = channels // n_ctx
    wide = own if own % LANES == 0 else LANES
    chunks = channels // wide
    width = min(channels, 8 * LANES)
    steps = channels // width
    groups = width // LANES
    pitch = tokens + ROWS
    params = pltpu.CompilerParams(vmem_limit_bytes=24 * 1024 * 1024)
    anywhere = pl.BlockSpec(memory_space=pl.ANY)
    smem = pl.BlockSpec(memory_space=pltpu.SMEM)
    vmem = pl.BlockSpec(memory_space=pltpu.VMEM)
    hbm = lambda *arrays: [pltpu.with_memory_space_constraint(array, pltpu.HBM) for array in arrays]
    near = lambda *arrays: [pltpu.with_memory_space_constraint(array, pltpu.VMEM) for array in arrays]

    modes_scratch = pltpu.VMEM((groups * order, LANES), F32)
    skip_gain = skip_gain.reshape(1, channels)
    tall = [pltpu.VMEM((channels // LANES * tokens, LANES), dtype) for dtype in (BF16, BF16)]
    table = pltpu.VMEM((steps * order * groups, LANES), F32)
    taps_v, modes_v = pltpu.VMEM((3, 3, channels), F32), pltpu.VMEM((order, channels), F32)

    info = pl.pallas_call(
        functools.partial(ends_kernel, width),
        in_specs=[smem] + [anywhere] * 6,
        out_specs=anywhere,
        out_shape=pltpu.HBM((chunks, INFO, wide), BF16),
        scratch_shapes=[
            pltpu.VMEM((2, 2 * ROWS, channels), BF16),
            pltpu.VMEM((tokens, channels), BF16),
            pltpu.VMEM((tokens, channels), BF16),
            taps_v,
            modes_v,
            modes_v,
            pltpu.VMEM((chunks, INFO, wide), BF16),
            pltpu.VMEM((2 * groups * pitch, LANES), F32),
            pltpu.VMEM((2 * groups * pitch, LANES), F32),
            modes_scratch,
            pltpu.VMEM((9 * groups, LANES), F32),
            pltpu.VMEM((steps * (2 * order + 6) * groups, LANES), F32),
            pltpu.SemaphoreType.DMA((3 * steps + 5,)),
        ],
        compiler_params=params,
        name="block_ends",
    )(*hbm(doc_ids, query, keyed, valued, short_taps, rates, residues))

    if wide != own:
        info = info.transpose(1, 0, 2).reshape(INFO, n_ctx, own).transpose(1, 0, 2)
    info = exchange(info)

    def local_scan(first, count, filled, owned=()):
        return pl.pallas_call(
            functools.partial(local_kernel, width, first, count, len(filled), turn),
            in_specs=[smem] + [anywhere] * 7 + [vmem] * len(filled),
            out_specs=[vmem] * (3 + len(owned)),
            out_shape=[*tall, table, *owned],
            input_output_aliases={8 + i: i for i in range(len(filled))},
            scratch_shapes=[
                pltpu.VMEM((tokens, channels), BF16),
                pltpu.VMEM((tokens, channels), BF16),
                pltpu.VMEM((tokens, channels), BF16),
                taps_v,
                modes_v,
                modes_v,
                pltpu.VMEM((1, channels), F32),
                *[pltpu.VMEM((groups * pitch, LANES), F32)] * 3,
                modes_scratch,
                pltpu.VMEM((10 * groups, LANES), F32),
                pltpu.VMEM((count * (2 * order + 10) * groups, LANES), F32),
                pltpu.SemaphoreType.DMA((3 * count + 4 + len(owned),)),
            ],
            compiler_params=params,
            cost_estimate=pl.CostEstimate(
                flops=count * tokens * width * 64, bytes_accessed=count * tokens * width * 14, transcendentals=0
            ),
            name="local_scan",
        )(
            *hbm(doc_ids, query, keyed, valued, short_taps, rates, residues, skip_gain), *near(*filled),
        )

    half = steps // 2 or steps
    if own % LANES == 0:
        owned = [pltpu.VMEM(value.shape[:-1] + (own,), F32) for value in (short_taps, rates, residues, skip_gain)]
        *filled, own_taps, own_rates, own_resid, own_skip = local_scan(0, half, [], owned)
        own_params = [own_taps, own_rates, own_resid, own_skip]
    else:
        filled = local_scan(0, half, [])
        at = place_in(turn) * own
        own_params = [
            lax.dynamic_slice_in_dim(value, at, own, value.ndim - 1)
            for value in (short_taps, rates, residues, skip_gain)
        ]
    info, *filled = lax.optimization_barrier((info, *filled))
    state = pl.pallas_call(
        functools.partial(carry_kernel, turn, tokens),
        out_shape=pltpu.HBM((n_ctx, TOLD, own), BF16),
        compiler_params=params,
        name="block_carry",
    )(*near(info, *own_params))
    state, *filled = lax.optimization_barrier((state, *filled))
    state = exchange(state)
    if half < steps:
        filled = local_scan(half, steps - half, filled)
    if wide != own:
        state = state.transpose(1, 0, 2).reshape(TOLD, chunks, wide).transpose(1, 0, 2)

    return pl.pallas_call(
        functools.partial(finish_kernel, width),
        in_specs=[vmem] * 4,
        out_specs=anywhere,
        out_shape=pltpu.HBM((tokens, channels), BF16),
        scratch_shapes=[
            pltpu.VMEM((tokens, channels), BF16),
            pltpu.VMEM((groups * pitch, LANES), F32),
            pltpu.VMEM((groups * TOLD, LANES), F32),
            pltpu.SemaphoreType.DMA((steps,)),
        ],
        compiler_params=params,
        name="add_carry",
    )(*near(state, *filled))


def solution(mesh):
    return jax.shard_map(
        on_device,
        mesh=mesh,
        in_specs=(
            P("ctx", "tp"),
            P("ctx", "tp"),
            P("ctx", "tp"),
            P(None, None, "tp"),
            P(None, "tp"),
            P(None, "tp"),
            P("tp"),
            P("ctx"),
        ),
        out_specs=P("ctx", "tp"),
        check_vma=False,
    )
```

```python
import functools

import jax
import jax.numpy as jnp
from jax import lax
from jax.experimental import pallas as pl
from jax.experimental.pallas import tpu as pltpu
from jax.sharding import PartitionSpec as P

LANES = 128
ROWS = 8
CHUNK = 16
INFO = 24
TOLD = 16
F32 = jnp.float32
BF16 = jnp.bfloat16


def meeting_order(count):
    first = 5 * count // 8
    return [(first + i) % count for i in range(count)]


def place_in(turn):
    me = lax.axis_index("ctx")
    place = jnp.int32(0)
    for i, at in enumerate(turn):
        place = jnp.where(me == i, at, place)
    return place


def rounded(value):
    return value.astype(BF16).astype(F32)


def row_index(rows=ROWS):
    return lax.broadcasted_iota(jnp.int32, (rows, LANES), 0)


def block_at(index, size):
    start = index * size
    return pl.ds(start if isinstance(start, int) else pl.multiple_of(start, size), size)


def pitch_of(tokens):
    return tokens + ROWS


def lanes_at(index, size, group):
    start = index * size + group * LANES
    return pl.ds(start if isinstance(start, int) else pl.multiple_of(start, LANES), LANES)


def columns(source, target, sems, width):
    return lambda i: pltpu.make_async_copy(
        source.at[..., block_at(i, width)], target.at[..., block_at(i, width)], sems.at[i]
    )


def across(scratch, rows_of):
    rows = rows_of.ref.shape[0]
    for group in range(rows_of.groups):
        scratch[pl.ds(group * rows, rows)] = rows_of(group)
    return [scratch[pl.ds(n, rows_of.groups, stride=rows)] for n in range(rows)]


class Rows:
    def __init__(self, ref, step, width):
        self.ref, self.step, self.width, self.groups = ref, step, width, width // LANES

    def __call__(self, group):
        return self.ref[..., lanes_at(self.step, self.width, group)]


def across_taps(scratch, rows_of, streams):
    groups = rows_of.groups
    for group in range(groups):
        taps = rows_of(group)
        for s in streams:
            for j in range(3):
                scratch[pl.ds((s * 3 + j) * groups + group, 1)] = taps[s, j : j + 1]
    return [[scratch[pl.ds((s * 3 + j) * groups, groups)] for j in range(3)] for s in streams]


def fill_group(scratch, base, pitch, rows_of, at, group):
    lanes = lanes_at(rows_of.step, rows_of.width, group)
    scratch[pl.ds(base + group * pitch + at, CHUNK)] = rows_of.ref[pl.ds(at, CHUNK), lanes].astype(F32)


def fills(scratches, refs, base, pitch, step, width, at):
    return [
        functools.partial(fill_group, scratch, base, pitch, Rows(ref, step, width), at, group)
        for scratch, ref in zip(scratches, refs)
        for group in range(width // LANES)
    ]


def share(calls, j):
    for call in calls[len(calls) * j // CHUNK : len(calls) * (j + 1) // CHUNK]:
        call()


def first_of_last(ids_ref):
    tokens = ids_ref.shape[0]
    low, high = jnp.int32(0), jnp.int32(tokens - 1)
    last = ids_ref[tokens - 1]
    for _ in range((tokens - 1).bit_length()):
        middle = (low + high) // 2
        same = ids_ref[middle] == last
        low, high = jnp.where(same, low, middle + 1), jnp.where(same, middle, high)
    return high


def by_rate(rates, resid):
    rates, resid = list(rates), list(resid)
    for turn in range(len(rates)):
        for i in range(turn % 2, len(rates) - 1, 2):
            low, high = rates[i], rates[i + 1]
            swap = low > high
            rates[i], rates[i + 1] = jnp.minimum(low, high), jnp.maximum(low, high)
            resid[i], resid[i + 1] = jnp.where(swap, resid[i + 1], resid[i]), jnp.where(swap, resid[i], resid[i + 1])
    return rates, resid


def summed(terms):
    while len(terms) > 1:
        terms = [sum(terms[i : i + 2]) for i in range(0, len(terms), 2)]
    return terms[0]


def ends_kernel(
    width, ids_ref, q_hbm, k_hbm, v_hbm, taps_hbm, rates_hbm, resid_hbm,
    info_hbm,
    q_v, k_v, v_v, taps_v, rates_v, resid_v, info_v, k_s, v_s, modes_s, taps_s, held_s, sems,
):
    tokens, channels = k_v.shape
    steps = channels // width
    groups = width // LANES
    chunks = tokens // CHUNK
    pitch = pitch_of(tokens)
    wide = info_v.shape[2]
    per_step = width // wide
    order = rates_v.shape[0]
    k_in, v_in = (
        columns(source, target, sems.at[pl.ds(i * steps, steps)], width)
        for i, (source, target) in enumerate(((k_hbm, k_v), (v_hbm, v_v)))
    )
    others = [
        pltpu.make_async_copy(source, target, sems.at[3 * steps + i])
        for i, (source, target) in enumerate(
            (
                (rates_hbm, rates_v),
                (resid_hbm, resid_v),
                (taps_hbm, taps_v),
                (q_hbm.at[pl.ds(0, CHUNK)], q_v.at[0]),
                (q_hbm.at[pl.ds(tokens - CHUNK, CHUNK)], q_v.at[1]),
            )
        )
    ]
    going = lambda i: pltpu.make_async_copy(
        info_v.at[block_at(i, per_step)], info_hbm.at[block_at(i, per_step)], sems.at[2 * steps + i]
    )
    for copy in others[:3]:
        copy.start()
    for i in range(steps):
        k_in(i).start()
        v_in(i).start()
        if i == 0:
            for copy in others[3:]:
                copy.start()
    begin = first_of_last(ids_ref)
    chunk0 = begin // CHUNK
    row = row_index()
    marks = jnp.zeros((ROWS, LANES), F32)
    for i, t in enumerate((0, 1, tokens - 2, tokens - 1)):
        marks = jnp.where(row == i + 4, ids_ref[t].astype(F32), marks)

    def base_of(i):
        return pl.multiple_of(jnp.bitwise_and(i, 1) * (groups * pitch), ROWS)

    def fills_of(i, at):
        return fills((k_s, v_s), (k_v, v_v), base_of(i), pitch, i, width, at)

    def arrive(i):
        k_in(i).wait()
        v_in(i).wait()

    for copy in others[:3]:
        copy.wait()
    held = 2 * order + 6

    def hold(i, _):
        rates, resid = by_rate(across(modes_s, Rows(rates_v, i, width)), across(modes_s, Rows(resid_v, i, width)))
        taps = across_taps(taps_s, Rows(taps_v, i, width), (1, 2))
        for n, value in enumerate([jnp.exp(-rate) for rate in rates] + resid + taps[0] + taps[1]):
            held_s[block_at(i * held + n, groups)] = value
        return 0

    lax.fori_loop(0, steps, hold, 0)
    arrive(0)
    for call in fills_of(0, pl.multiple_of(chunk0 * CHUNK, CHUNK)):
        call()
    for copy in others[3:]:
        copy.wait()

    def step(i):

        base = base_of(i)
        values = [held_s[block_at(i * held + n, groups)] for n in range(held)]
        decay, resid = values[:order], values[order : 2 * order]
        taps = [values[2 * order : 2 * order + 3], values[2 * order + 3 :]]

        def chunk(masked, c, carry):
            at = pl.multiple_of(c * CHUNK, CHUNK)
            back1, back2, ends = carry
            ends_here = c == chunks - 1
            if i + 1 < steps:
                pl.when(ends_here)(functools.partial(arrive, i + 1))
            later = jnp.where(ends_here, min(i + 1, steps - 1), i)
            later_at = pl.multiple_of(jnp.where(ends_here, chunk0, c + 1) * CHUNK, CHUNK)
            coming = fills_of(later, later_at)
            for j in range(CHUNK):
                t = at + j
                share(coming, j)
                here = [ref[pl.ds(base + t, groups, stride=pitch)] for ref in (k_s, v_s)]
                if masked:
                    live = (t >= begin).astype(F32)
                    here = [value * live for value in here]
                conv = [taps[s][0] * here[s] + taps[s][1] * back1[s] + taps[s][2] * back2[s] for s in range(2)]
                gated = rounded(conv[0] * conv[1])
                if masked and j < 2:
                    gated = gated * (t >= 2).astype(F32)
                ends = [ends[n] * decay[n] + gated for n in range(order)]
                back1, back2 = here, back1
            return back1, back2, ends

        zero = jnp.zeros((groups, LANES), F32)
        carry = chunk(True, chunk0, ([zero] * 2, [zero] * 2, [zero] * order))
        ends = lax.fori_loop(chunk0 + 1, chunks, functools.partial(chunk, False), carry)[2]
        running = zero
        for n in range(order):
            running = running + resid[n] * ends[n]
            modes_s[pl.ds(n, groups, stride=order)] = running

        for group in range(groups):
            lanes = lanes_at(i, width, group)
            state = modes_s[pl.ds(group * order, order)]
            heads = [ref[pl.ds(0, CHUNK), lanes].astype(F32)[:ROWS] for ref in (k_v, v_v)]
            tails = [ref[pl.ds(tokens - CHUNK, CHUNK), lanes].astype(F32)[ROWS:] for ref in (k_v, v_v)]
            edge = jnp.where(row < 2, heads[0], pltpu.roll(heads[1], 2, 0))
            edge = jnp.where(row < 4, edge, pltpu.roll(tails[0], ROWS - 2, 0))
            edge = jnp.where(row < 6, edge, tails[1])
            at = i * per_step + (group * LANES) // wide
            inner = pl.ds((group * LANES) % wide, LANES)
            q_head, q_tail = (q_v[j, :, lanes].astype(F32) for j in range(2))
            more = jnp.where(row < 2, q_head[:ROWS], pltpu.roll(q_tail[ROWS:], 4, 0))
            more = jnp.where(row < 4, more, marks)
            info_v[at, :, inner] = jnp.concatenate([state, edge, more], axis=0).astype(BF16)
        going(i).start()

    for i in range(steps):
        step(i)
    for i in range(steps):
        going(i).wait()


def carry_kernel(turn, tokens, info_ref, taps_ref, rates_ref, resid_ref, skip_ref, out_ref):
    order, wide = rates_ref.shape
    skip = skip_ref[...]
    rows = lambda ref: [ref[n : n + 1] for n in range(order)]
    rates, resid = (jnp.concatenate(modes, axis=0) for modes in by_rate(rows(rates_ref), rows(resid_ref)))
    decay = jnp.exp(-rates)
    rest = jnp.exp(-float(tokens - 2) * rates)
    row = lax.broadcasted_iota(jnp.int32, (order, wide), 0)
    even = row % 2 == 0

    def turned(value, steps):
        if wide % LANES:
            return jnp.concatenate([value[order - steps :], value[: order - steps]], axis=0)
        return pltpu.roll(value, steps, 0)

    def down(value, steps):
        return jnp.where(row < steps, 0.0, turned(value, steps))

    def tap(j):
        key, value, query = (jnp.broadcast_to(taps_ref[s, j : j + 1], (order, wide)) for s in (1, 2, 0))
        return jnp.where(row < 2, key, jnp.where(row < 4, value, query))

    taps = [tap(j) for j in range(3)]
    state = jnp.zeros((order, wide), F32)
    tails, prev0, prev1 = state, jnp.full((1, wide), -1.0, F32), jnp.full((1, wide), -1.0, F32)
    for block in turn:
        info = info_ref[block].astype(F32)
        running, edge, more = (info[i * ROWS : (i + 1) * ROWS] for i in range(3))
        ends = running - down(running, 1)
        first0, first1, last0, last1 = (more[4 + i : 5 + i] for i in range(4))
        same = lambda one, other: (one == other).astype(F32)
        entering, inside = same(prev1, first0), same(first0, first1)
        heads = jnp.where(row < 4, edge, turned(more, 4))
        back1 = jnp.where(even, turned(tails, order - 1), turned(heads, 1))
        conv = (
            taps[0] * heads
            + taps[1] * (back1 * jnp.where(even, entering, inside))
            + taps[2] * (tails * jnp.where(even, same(prev0, first0), same(prev1, first1)))
        )
        gated = rounded(conv * turned(conv, order - 2))
        state0 = decay * (state * entering) + resid * gated[0:1]
        state1 = decay * (state0 * inside) + resid * gated[1:2]
        long0 = jnp.sum(state0, axis=0, keepdims=True)
        long1 = jnp.sum(state1, axis=0, keepdims=True)
        mixed = turned(conv, order - 4) * (jnp.where(row == 0, long0, long1) + skip * gated)
        running = state1
        for steps in (1, 2, 4):
            running = running + down(running, steps)
        out_ref[block] = jnp.concatenate([running, mixed], axis=0).astype(BF16)
        state = ends + rest * (state1 * same(first1, last1))
        tails = jnp.where(row < 4, turned(edge, 4), turned(more, 2))
        prev0, prev1 = last0, last1


def local_kernel(
    width, first_step, count, filled, turn, ids_ref, q_hbm, k_hbm, v_hbm, taps_hbm, rates_hbm, resid_hbm, skip_hbm, *rest
):
    (
        q_v, k_v, v_v, taps_v, rates_v, resid_v, skip_v, q_s, k_s, v_s, modes_s, taps_s, held_s, sems,
    ) = rest[-14:]
    part_ref, query_ref, table_ref, *own_refs = rest[filled:-14]
    tokens, channels = q_v.shape
    owned = []
    if own_refs:
        mine = own_refs[0].shape[-1]
        lanes = pl.ds(pl.multiple_of(place_in(turn) * mine, mine), mine)
        owned = [
            (source.at[..., lanes], target)
            for source, target in zip((taps_hbm, rates_hbm, resid_hbm, skip_hbm), own_refs)
        ]
    groups = width // LANES
    pitch = pitch_of(tokens)
    chunks = tokens // CHUNK
    order = rates_v.shape[0]
    end_step = first_step + count
    scratches = (q_s, k_s, v_s)
    streams = [
        lambda i, s=s, source=source, target=target: pltpu.make_async_copy(
            source.at[:, block_at(i, width)], target.at[:, block_at(i, width)], sems.at[s * count + i - first_step]
        )
        for s, (source, target) in enumerate(((q_hbm, q_v), (k_hbm, k_v), (v_hbm, v_v)))
    ]
    part = pl.ds(first_step * width, count * width)
    own = [pltpu.make_async_copy(source, target, sems.at[3 * count + 4 + i]) for i, (source, target) in enumerate(owned)]
    others = [
        pltpu.make_async_copy(source.at[..., part], target.at[..., part], sems.at[3 * count + i])
        for i, (source, target) in enumerate(
            ((taps_hbm, taps_v), (rates_hbm, rates_v), (resid_hbm, resid_v), (skip_hbm, skip_v))
        )
    ]
    for copy in others:
        copy.start()
    for i in range(first_step, end_step):
        for copy in streams:
            copy(i).start()
    for copy in own:
        copy.start()

    def arrive(i):
        for copy in streams:
            copy(i).wait()

    def fills_of(i, at):
        return fills(scratches, (q_v, k_v, v_v), 0, pitch, i, width, at)

    for copy in others:
        copy.wait()
    held = 2 * order + 10

    def hold(i, _):
        for group in range(groups):
            taps_s[pl.ds(9 * groups + group, 1)] = skip_v[:, lanes_at(i, width, group)]
        rates, resid = by_rate(across(modes_s, Rows(rates_v, i, width)), across(modes_s, Rows(resid_v, i, width)))
        decay = [jnp.exp(-rate) for rate in rates]
        taps = across_taps(taps_s, Rows(taps_v, i, width), (0, 1, 2))
        skip = taps_s[pl.ds(9 * groups, groups)]
        for n, value in enumerate(decay + resid + taps[0] + taps[1] + taps[2] + [skip]):
            held_s[block_at((i - first_step) * held + n, groups)] = value
        for n in range(order):
            table_ref[block_at(i * order + n, groups)] = decay[n]
        return 0

    lax.fori_loop(first_step, end_step, hold, 0)
    arrive(first_step)
    for call in fills_of(first_step, 0):
        call()

    def step(i, _):
        values = [held_s[block_at((i - first_step) * held + n, groups)] for n in range(held)]
        decay, resid, skip = values[:order], values[order : 2 * order], values[-1]
        taps = [values[2 * order + 3 * s : 2 * order + 3 * s + 3] for s in range(3)]

        def row_of(ref, t):
            return ref[pl.ds(t, groups, stride=pitch)]

        def token(t, carry, masked):
            back1, back2, states = carry
            now = [row_of(ref, t) for ref in scratches]
            if masked:
                same = (ids_ref[t] == ids_ref[t - 1]).astype(F32)
                back1 = [value * same for value in back1]
                back2 = [value * same for value in back2]
                states = [value * same for value in states]
            conv = [taps[s][0] * now[s] + taps[s][1] * back1[s] + taps[s][2] * back2[s] for s in range(3)]
            gated = rounded(conv[1] * conv[2])
            states = [states[n] * decay[n] + gated for n in range(order)]
            total = summed([states[n] * resid[n] for n in range(order)])
            live = (ids_ref[t] == ids_ref[1]).astype(F32)
            return (now, back1, states), conv[0] * (total + skip * gated), conv[0] * live

        def chunk(masked, skipped, at, later, later_at, carry):
            coming = fills_of(later, later_at)
            for j in range(skipped):
                share(coming, j)
            for j in range(skipped, CHUNK, 2):
                share(coming, j)
                carry, part0, query0 = token(at + j, carry, masked)
                share(coming, j + 1)
                carry, part1, query1 = token(at + j + 1, carry, masked)
                pair = pl.ds(pl.multiple_of((i * tokens + at + j) * groups, 2 * groups), 2 * groups)
                part_ref[pair] = jnp.concatenate([part0, part1], axis=0).astype(BF16)
                query_ref[pair] = jnp.concatenate([query0, query1], axis=0).astype(BF16)
            return carry

        def any_chunk(c, carry):
            at = pl.multiple_of(c * CHUNK, CHUNK)
            ends_here = c == chunks - 1
            pl.when(ends_here & (i + 1 < end_step))(functools.partial(arrive, i + 1))
            later = jnp.where(ends_here, jnp.minimum(i + 1, end_step - 1), i)
            later_at = pl.multiple_of(jnp.where(ends_here, 0, at + CHUNK), CHUNK)
            return lax.cond(
                ids_ref[at - 1] == ids_ref[at + CHUNK - 1],
                functools.partial(chunk, False, 0, at, later, later_at),
                functools.partial(chunk, True, 0, at, later, later_at),
                carry,
            )

        back1, back2 = ([row_of(ref, t) for ref in scratches] for t in (1, 0))
        same = (ids_ref[1] == ids_ref[0]).astype(F32)
        carry = (back1, [value * same for value in back2], [jnp.zeros((groups, LANES), F32)] * order)
        carry = chunk(True, 2, 0, i, CHUNK, carry)
        lax.fori_loop(1, chunks, any_chunk, carry)
        return 0

    lax.fori_loop(first_step, end_step, step, 0)
    for copy in own:
        copy.wait()


def finish_kernel(width, state_ref, part_ref, query_ref, table_ref, out_hbm, out_v, out_s, modes_s, sems):
    tokens, channels = out_v.shape
    steps = channels // width
    groups = width // LANES
    pitch = pitch_of(tokens)
    wide = state_ref.shape[2]
    order = table_ref.shape[0] // (groups * steps)
    going = columns(out_v, out_hbm, sems, width)

    def step(i, _):
        decay = [table_ref[block_at(i * order + n, groups)] for n in range(order)]
        for group in range(groups):
            chunk_at = i * (width // wide) + (group * LANES) // wide
            modes_s[pl.ds(group * TOLD, TOLD)] = state_ref[chunk_at, :, pl.ds((group * LANES) % wide, LANES)].astype(F32)
        running = [modes_s[pl.ds(n, groups, stride=TOLD)] for n in range(order)]
        weights = [running[0]] + [running[n] - running[n - 1] for n in range(1, order)]

        def pair(t, weights):
            at = pl.ds(pl.multiple_of((i * tokens + t) * groups, 2 * groups), 2 * groups)
            part, live_query = part_ref[at].astype(F32), query_ref[at].astype(F32)
            for k in range(2):
                weights = [weights[n] * decay[n] for n in range(order)]
                rows = slice(k * groups, (k + 1) * groups)
                out_s[pl.ds(t + k, groups, stride=pitch)] = part[rows] + live_query[rows] * summed(weights)
            return weights

        def give(at, group):
            out_v[pl.ds(at, CHUNK), lanes_at(i, width, group)] = out_s[pl.ds(group * pitch + at, CHUNK)].astype(BF16)

        def gives(at):
            return [functools.partial(give, at, group) for group in range(groups)]

        def chunk(c, weights):
            at = pl.multiple_of(c * CHUNK, CHUNK)
            done = gives(at - CHUNK)
            for j in range(0, CHUNK, 2):
                share(done, j)
                share(done, j + 1)
                weights = pair(at + j, weights)
            return weights

        for t in range(2):
            out_s[pl.ds(t, groups, stride=pitch)] = modes_s[pl.ds(order + t, groups, stride=TOLD)]
        for t in range(2, CHUNK, 2):
            weights = pair(t, weights)
        lax.fori_loop(1, tokens // CHUNK, chunk, weights)
        for call in gives(tokens - CHUNK):
            call()
        going(i).start()
        return 0

    lax.fori_loop(0, steps, step, 0)
    for i in range(steps):
        going(i).wait()


def on_device(query, keyed, valued, short_taps, rates, residues, skip_gain, doc_ids):
    tokens, channels = query.shape
    order = rates.shape[0]
    n_ctx = lax.axis_size("ctx")
    meeting = meeting_order(n_ctx)
    turn = [meeting.index(i) for i in range(n_ctx)]
    exchange = lambda value: lax.all_to_all(
        value, "ctx", split_axis=0, concat_axis=0, tiled=True, axis_index_groups=[meeting]
    )
    own = channels // n_ctx
    wide = own if own % LANES == 0 else LANES
    chunks = channels // wide
    width = min(channels, 8 * LANES)
    steps = channels // width
    groups = width // LANES
    pitch = pitch_of(tokens)
    params = pltpu.CompilerParams(vmem_limit_bytes=24 * 1024 * 1024)
    anywhere = pl.BlockSpec(memory_space=pl.ANY)
    smem = pl.BlockSpec(memory_space=pltpu.SMEM)
    vmem = pl.BlockSpec(memory_space=pltpu.VMEM)
    hbm = lambda *arrays: [pltpu.with_memory_space_constraint(array, pltpu.HBM) for array in arrays]
    near = lambda *arrays: [pltpu.with_memory_space_constraint(array, pltpu.VMEM) for array in arrays]

    modes_scratch = pltpu.VMEM(((groups + 1) * order, LANES), F32)
    skip_gain = skip_gain.reshape(1, channels)
    tall = [pltpu.VMEM((channels // LANES * tokens, LANES), dtype) for dtype in (BF16, BF16)]
    table = pltpu.VMEM((steps * order * groups, LANES), F32)
    taps_v, modes_v = pltpu.VMEM((3, 3, channels), F32), pltpu.VMEM((order, channels), F32)

    info = pl.pallas_call(
        functools.partial(ends_kernel, width),
        in_specs=[smem] + [anywhere] * 6,
        out_specs=anywhere,
        out_shape=pltpu.HBM((chunks, INFO, wide), BF16),
        scratch_shapes=[
            pltpu.VMEM((2, 2 * ROWS, channels), BF16),
            pltpu.VMEM((tokens, channels), BF16),
            pltpu.VMEM((tokens, channels), BF16),
            taps_v,
            modes_v,
            modes_v,
            pltpu.VMEM((chunks, INFO, wide), BF16),
            pltpu.VMEM(((2 * groups + 1) * pitch, LANES), F32),
            pltpu.VMEM(((2 * groups + 1) * pitch, LANES), F32),
            modes_scratch,
            pltpu.VMEM((9 * groups, LANES), F32),
            pltpu.VMEM((steps * (2 * order + 6) * groups, LANES), F32),
            pltpu.SemaphoreType.DMA((3 * steps + 5,)),
        ],
        compiler_params=params,
        name="block_ends",
    )(*hbm(doc_ids, query, keyed, valued, short_taps, rates, residues))

    if wide != own:
        info = info.transpose(1, 0, 2).reshape(INFO, n_ctx, own).transpose(1, 0, 2)
    info = exchange(info)

    def local_scan(first, count, filled, owned=()):
        return pl.pallas_call(
            functools.partial(local_kernel, width, first, count, len(filled), turn),
            in_specs=[smem] + [anywhere] * 7 + [vmem] * len(filled),
            out_specs=[vmem] * (3 + len(owned)),
            out_shape=[*tall, table, *owned],
            input_output_aliases={8 + i: i for i in range(len(filled))},
            scratch_shapes=[
                pltpu.VMEM((tokens, channels), BF16),
                pltpu.VMEM((tokens, channels), BF16),
                pltpu.VMEM((tokens, channels), BF16),
                taps_v,
                modes_v,
                modes_v,
                pltpu.VMEM((1, channels), F32),
                *[pltpu.VMEM(((groups + 1) * pitch, LANES), F32)] * 3,
                modes_scratch,
                pltpu.VMEM((10 * groups, LANES), F32),
                pltpu.VMEM((count * (2 * order + 10) * groups, LANES), F32),
                pltpu.SemaphoreType.DMA((3 * count + 4 + len(owned),)),
            ],
            compiler_params=params,
            cost_estimate=pl.CostEstimate(
                flops=count * tokens * width * 64, bytes_accessed=count * tokens * width * 14, transcendentals=0
            ),
            name="local_scan",
        )(
            *hbm(doc_ids, query, keyed, valued, short_taps, rates, residues, skip_gain), *near(*filled),
        )

    half = steps // 2 or steps
    if own % LANES == 0:
        owned = [pltpu.VMEM(value.shape[:-1] + (own,), F32) for value in (short_taps, rates, residues, skip_gain)]
        *filled, own_taps, own_rates, own_resid, own_skip = local_scan(0, half, [], owned)
        own_params = [own_taps, own_rates, own_resid, own_skip]
    else:
        filled = local_scan(0, half, [])
        at = place_in(turn) * own
        own_params = [
            lax.dynamic_slice_in_dim(value, at, own, value.ndim - 1)
            for value in (short_taps, rates, residues, skip_gain)
        ]
    info, *filled = lax.optimization_barrier((info, *filled))
    state = pl.pallas_call(
        functools.partial(carry_kernel, turn, tokens),
        out_shape=pltpu.HBM((n_ctx, TOLD, own), BF16),
        compiler_params=params,
        name="block_carry",
    )(*near(info, *own_params))
    state, *filled = lax.optimization_barrier((state, *filled))
    state = exchange(state)
    if half < steps:
        filled = local_scan(half, steps - half, filled)
    if wide != own:
        state = state.transpose(1, 0, 2).reshape(TOLD, chunks, wide).transpose(1, 0, 2)

    return pl.pallas_call(
        functools.partial(finish_kernel, width),
        in_specs=[vmem] * 4,
        out_specs=anywhere,
        out_shape=pltpu.HBM((tokens, channels), BF16),
        scratch_shapes=[
            pltpu.VMEM((tokens, channels), BF16),
            pltpu.VMEM(((groups + 1) * pitch, LANES), F32),
            pltpu.VMEM(((groups + 1) * TOLD, LANES), F32),
            pltpu.SemaphoreType.DMA((steps,)),
        ],
        compiler_params=params,
        name="add_carry",
    )(*near(state, *filled))


def solution(mesh):
    return jax.shard_map(
        on_device,
        mesh=mesh,
        in_specs=(
            P("ctx", "tp"),
            P("ctx", "tp"),
            P("ctx", "tp"),
            P(None, None, "tp"),
            P(None, "tp"),
            P(None, "tp"),
            P("tp"),
            P("ctx"),
        ),
        out_specs=P("ctx", "tp"),
        check_vma=False,
    )
```

```python
import functools

import jax
import jax.numpy as jnp
from jax import lax
from jax.experimental import pallas as pl
from jax.experimental.pallas import tpu as pltpu
from jax.sharding import PartitionSpec as P

LANES = 128
ROWS = 8
CHUNK = 16
INFO = 24
TOLD = 16
F32 = jnp.float32
BF16 = jnp.bfloat16


def meeting_order(count):
    first = 5 * count // 8
    return [(first + i) % count for i in range(count)]


def place_in(turn):
    me = lax.axis_index("ctx")
    place = jnp.int32(0)
    for i, at in enumerate(turn):
        place = jnp.where(me == i, at, place)
    return place


def rounded(value):
    return value.astype(BF16).astype(F32)


def row_index(rows=ROWS):
    return lax.broadcasted_iota(jnp.int32, (rows, LANES), 0)


def block_at(index, size):
    start = index * size
    return pl.ds(start if isinstance(start, int) else pl.multiple_of(start, size), size)


def pitch_of(tokens):
    return tokens + ROWS


def lanes_at(index, size, group):
    start = index * size + group * LANES
    return pl.ds(start if isinstance(start, int) else pl.multiple_of(start, LANES), LANES)


def columns(source, target, sems, width):
    return lambda i: pltpu.make_async_copy(
        source.at[..., block_at(i, width)], target.at[..., block_at(i, width)], sems.at[i]
    )


def across(scratch, rows_of):
    rows = rows_of.ref.shape[0]
    for group in range(rows_of.groups):
        scratch[pl.ds(group * rows, rows)] = rows_of(group)
    return [scratch[pl.ds(n, rows_of.groups, stride=rows)] for n in range(rows)]


class Rows:
    def __init__(self, ref, step, width):
        self.ref, self.step, self.width, self.groups = ref, step, width, width // LANES

    def __call__(self, group):
        return self.ref[..., lanes_at(self.step, self.width, group)]


def across_taps(scratch, rows_of, streams):
    groups = rows_of.groups
    for group in range(groups):
        taps = rows_of(group)
        for s in streams:
            for j in range(3):
                scratch[pl.ds((s * 3 + j) * groups + group, 1)] = taps[s, j : j + 1]
    return [[scratch[pl.ds((s * 3 + j) * groups, groups)] for j in range(3)] for s in streams]


def fill_group(scratch, base, pitch, rows_of, at, group):
    lanes = lanes_at(rows_of.step, rows_of.width, group)
    scratch[pl.ds(base + group * pitch + at, CHUNK)] = rows_of.ref[pl.ds(at, CHUNK), lanes].astype(F32)


def fills(scratches, refs, base, pitch, step, width, at):
    return [
        functools.partial(fill_group, scratch, base, pitch, Rows(ref, step, width), at, group)
        for scratch, ref in zip(scratches, refs)
        for group in range(width // LANES)
    ]


def share(calls, j):
    for call in calls[len(calls) * j // CHUNK : len(calls) * (j + 1) // CHUNK]:
        call()


def first_of_last(ids_ref):
    tokens = ids_ref.shape[0]
    low, high = jnp.int32(0), jnp.int32(tokens - 1)
    last = ids_ref[tokens - 1]
    for _ in range((tokens - 1).bit_length()):
        middle = (low + high) // 2
        same = ids_ref[middle] == last
        low, high = jnp.where(same, low, middle + 1), jnp.where(same, middle, high)
    return high


def by_rate(rates, resid):
    rates, resid = list(rates), list(resid)
    for turn in range(len(rates)):
        for i in range(turn % 2, len(rates) - 1, 2):
            low, high = rates[i], rates[i + 1]
            swap = low > high
            rates[i], rates[i + 1] = jnp.minimum(low, high), jnp.maximum(low, high)
            resid[i], resid[i + 1] = jnp.where(swap, resid[i + 1], resid[i]), jnp.where(swap, resid[i], resid[i + 1])
    return rates, resid


def summed(terms):
    while len(terms) > 1:
        terms = [sum(terms[i : i + 2]) for i in range(0, len(terms), 2)]
    return terms[0]


def ends_kernel(
    width, ids_ref, q_hbm, k_hbm, v_hbm, taps_hbm, rates_hbm, resid_hbm,
    info_hbm,
    q_v, k_v, v_v, taps_v, rates_v, resid_v, info_v, k_s, v_s, modes_s, taps_s, held_s, sems,
):
    tokens, channels = k_v.shape
    steps = channels // width
    groups = width // LANES
    chunks = tokens // CHUNK
    pitch = pitch_of(tokens)
    wide = info_v.shape[2]
    per_step = width // wide
    order = rates_v.shape[0]
    k_in, v_in = (
        columns(source, target, sems.at[pl.ds(i * steps, steps)], width)
        for i, (source, target) in enumerate(((k_hbm, k_v), (v_hbm, v_v)))
    )
    others = [
        pltpu.make_async_copy(source, target, sems.at[3 * steps + i])
        for i, (source, target) in enumerate(
            (
                (rates_hbm, rates_v),
                (resid_hbm, resid_v),
                (taps_hbm, taps_v),
                (q_hbm.at[pl.ds(0, CHUNK)], q_v.at[0]),
                (q_hbm.at[pl.ds(tokens - CHUNK, CHUNK)], q_v.at[1]),
            )
        )
    ]
    going = lambda i: pltpu.make_async_copy(
        info_v.at[block_at(i, per_step)], info_hbm.at[block_at(i, per_step)], sems.at[2 * steps + i]
    )
    for copy in others[:3]:
        copy.start()
    for i in range(steps):
        k_in(i).start()
        v_in(i).start()
        if i == min(1, steps - 1):
            for copy in others[3:]:
                copy.start()
    begin = first_of_last(ids_ref)
    chunk0 = begin // CHUNK
    row = row_index()
    marks = jnp.zeros((ROWS, LANES), F32)
    for i, t in enumerate((0, 1, tokens - 2, tokens - 1)):
        marks = jnp.where(row == i + 4, ids_ref[t].astype(F32), marks)

    def base_of(i):
        return pl.multiple_of(jnp.bitwise_and(i, 1) * (groups * pitch), ROWS)

    def fills_of(i, at):
        return fills((k_s, v_s), (k_v, v_v), base_of(i), pitch, i, width, at)

    def arrive(i):
        k_in(i).wait()
        v_in(i).wait()

    for copy in others[:3]:
        copy.wait()
    held = 2 * order + 6

    def hold(i, _):
        rates, resid = by_rate(across(modes_s, Rows(rates_v, i, width)), across(modes_s, Rows(resid_v, i, width)))
        taps = across_taps(taps_s, Rows(taps_v, i, width), (1, 2))
        for n, value in enumerate([jnp.exp(-rate) for rate in rates] + resid + taps[0] + taps[1]):
            held_s[block_at(i * held + n, groups)] = value
        return 0

    lax.fori_loop(0, steps, hold, 0)
    arrive(0)
    for call in fills_of(0, pl.multiple_of(chunk0 * CHUNK, CHUNK)):
        call()
    def step(i):

        base = base_of(i)
        values = [held_s[block_at(i * held + n, groups)] for n in range(held)]
        decay, resid = values[:order], values[order : 2 * order]
        taps = [values[2 * order : 2 * order + 3], values[2 * order + 3 :]]

        def chunk(masked, c, carry):
            at = pl.multiple_of(c * CHUNK, CHUNK)
            back1, back2, ends = carry
            ends_here = c == chunks - 1
            if i + 1 < steps:
                pl.when(ends_here)(functools.partial(arrive, i + 1))
            later = jnp.where(ends_here, min(i + 1, steps - 1), i)
            later_at = pl.multiple_of(jnp.where(ends_here, chunk0, c + 1) * CHUNK, CHUNK)
            coming = fills_of(later, later_at)
            for j in range(CHUNK):
                t = at + j
                share(coming, j)
                here = [ref[pl.ds(base + t, groups, stride=pitch)] for ref in (k_s, v_s)]
                if masked:
                    live = (t >= begin).astype(F32)
                    here = [value * live for value in here]
                conv = [taps[s][0] * here[s] + taps[s][1] * back1[s] + taps[s][2] * back2[s] for s in range(2)]
                gated = rounded(conv[0] * conv[1])
                if masked and j < 2:
                    gated = gated * (t >= 2).astype(F32)
                ends = [ends[n] * decay[n] + gated for n in range(order)]
                back1, back2 = here, back1
            return back1, back2, ends

        zero = jnp.zeros((groups, LANES), F32)
        carry = chunk(True, chunk0, ([zero] * 2, [zero] * 2, [zero] * order))
        ends = lax.fori_loop(chunk0 + 1, chunks, functools.partial(chunk, False), carry)[2]
        running = zero
        for n in range(order):
            running = running + resid[n] * ends[n]
            modes_s[pl.ds(n, groups, stride=order)] = running

        if i == 0:
            for copy in others[3:]:
                copy.wait()
        for group in range(groups):
            lanes = lanes_at(i, width, group)
            state = modes_s[pl.ds(group * order, order)]
            heads = [ref[pl.ds(0, CHUNK), lanes].astype(F32)[:ROWS] for ref in (k_v, v_v)]
            tails = [ref[pl.ds(tokens - CHUNK, CHUNK), lanes].astype(F32)[ROWS:] for ref in (k_v, v_v)]
            edge = jnp.where(row < 2, heads[0], pltpu.roll(heads[1], 2, 0))
            edge = jnp.where(row < 4, edge, pltpu.roll(tails[0], ROWS - 2, 0))
            edge = jnp.where(row < 6, edge, tails[1])
            at = i * per_step + (group * LANES) // wide
            inner = pl.ds((group * LANES) % wide, LANES)
            q_head, q_tail = (q_v[j, :, lanes].astype(F32) for j in range(2))
            more = jnp.where(row < 2, q_head[:ROWS], pltpu.roll(q_tail[ROWS:], 4, 0))
            more = jnp.where(row < 4, more, marks)
            info_v[at, :, inner] = jnp.concatenate([state, edge, more], axis=0).astype(BF16)
        going(i).start()

    for i in range(steps):
        step(i)
    for i in range(steps):
        going(i).wait()


def carry_kernel(turn, tokens, info_ref, taps_ref, rates_ref, resid_ref, skip_ref, out_ref):
    order, wide = rates_ref.shape
    skip = skip_ref[...]
    rows = lambda ref: [ref[n : n + 1] for n in range(order)]
    rates, resid = (jnp.concatenate(modes, axis=0) for modes in by_rate(rows(rates_ref), rows(resid_ref)))
    decay = jnp.exp(-rates)
    rest = jnp.exp(-float(tokens - 2) * rates)
    row = lax.broadcasted_iota(jnp.int32, (order, wide), 0)
    even = row % 2 == 0

    def turned(value, steps):
        if wide % LANES:
            return jnp.concatenate([value[order - steps :], value[: order - steps]], axis=0)
        return pltpu.roll(value, steps, 0)

    def down(value, steps):
        return jnp.where(row < steps, 0.0, turned(value, steps))

    def tap(j):
        key, value, query = (jnp.broadcast_to(taps_ref[s, j : j + 1], (order, wide)) for s in (1, 2, 0))
        return jnp.where(row < 2, key, jnp.where(row < 4, value, query))

    taps = [tap(j) for j in range(3)]
    state = jnp.zeros((order, wide), F32)
    tails, prev0, prev1 = state, jnp.full((1, wide), -1.0, F32), jnp.full((1, wide), -1.0, F32)
    for block in turn:
        info = info_ref[block].astype(F32)
        running, edge, more = (info[i * ROWS : (i + 1) * ROWS] for i in range(3))
        ends = running - down(running, 1)
        first0, first1, last0, last1 = (more[4 + i : 5 + i] for i in range(4))
        same = lambda one, other: (one == other).astype(F32)
        entering, inside = same(prev1, first0), same(first0, first1)
        heads = jnp.where(row < 4, edge, turned(more, 4))
        back1 = jnp.where(even, turned(tails, order - 1), turned(heads, 1))
        conv = (
            taps[0] * heads
            + taps[1] * (back1 * jnp.where(even, entering, inside))
            + taps[2] * (tails * jnp.where(even, same(prev0, first0), same(prev1, first1)))
        )
        gated = rounded(conv * turned(conv, order - 2))
        state0 = decay * (state * entering) + resid * gated[0:1]
        state1 = decay * (state0 * inside) + resid * gated[1:2]
        long0 = jnp.sum(state0, axis=0, keepdims=True)
        long1 = jnp.sum(state1, axis=0, keepdims=True)
        mixed = turned(conv, order - 4) * (jnp.where(row == 0, long0, long1) + skip * gated)
        running = state1
        for steps in (1, 2, 4):
            running = running + down(running, steps)
        out_ref[block] = jnp.concatenate([running, mixed], axis=0).astype(BF16)
        state = ends + rest * (state1 * same(first1, last1))
        tails = jnp.where(row < 4, turned(edge, 4), turned(more, 2))
        prev0, prev1 = last0, last1


def local_kernel(
    width, first_step, count, filled, turn, ids_ref, q_hbm, k_hbm, v_hbm, taps_hbm, rates_hbm, resid_hbm, skip_hbm, *rest
):
    (
        q_v, k_v, v_v, taps_v, rates_v, resid_v, skip_v, q_s, k_s, v_s, modes_s, taps_s, held_s, sems,
    ) = rest[-14:]
    part_ref, query_ref, table_ref, *own_refs = rest[filled:-14]
    tokens, channels = q_v.shape
    owned = []
    if own_refs:
        mine = own_refs[0].shape[-1]
        lanes = pl.ds(pl.multiple_of(place_in(turn) * mine, mine), mine)
        owned = [
            (source.at[..., lanes], target)
            for source, target in zip((taps_hbm, rates_hbm, resid_hbm, skip_hbm), own_refs)
        ]
    groups = width // LANES
    pitch = pitch_of(tokens)
    chunks = tokens // CHUNK
    order = rates_v.shape[0]
    end_step = first_step + count
    scratches = (q_s, k_s, v_s)
    streams = [
        lambda i, s=s, source=source, target=target: pltpu.make_async_copy(
            source.at[:, block_at(i, width)], target.at[:, block_at(i, width)], sems.at[s * count + i - first_step]
        )
        for s, (source, target) in enumerate(((q_hbm, q_v), (k_hbm, k_v), (v_hbm, v_v)))
    ]
    part = pl.ds(first_step * width, count * width)
    own = [pltpu.make_async_copy(source, target, sems.at[3 * count + 4 + i]) for i, (source, target) in enumerate(owned)]
    others = [
        pltpu.make_async_copy(source.at[..., part], target.at[..., part], sems.at[3 * count + i])
        for i, (source, target) in enumerate(
            ((taps_hbm, taps_v), (rates_hbm, rates_v), (resid_hbm, resid_v), (skip_hbm, skip_v))
        )
    ]
    for copy in others:
        copy.start()
    for i in range(first_step, end_step):
        for copy in streams:
            copy(i).start()
    for copy in own:
        copy.start()

    def arrive(i):
        for copy in streams:
            copy(i).wait()

    def fills_of(i, at):
        return fills(scratches, (q_v, k_v, v_v), 0, pitch, i, width, at)

    for copy in others:
        copy.wait()
    held = 2 * order + 10

    def hold(i, _):
        for group in range(groups):
            taps_s[pl.ds(9 * groups + group, 1)] = skip_v[:, lanes_at(i, width, group)]
        rates, resid = by_rate(across(modes_s, Rows(rates_v, i, width)), across(modes_s, Rows(resid_v, i, width)))
        decay = [jnp.exp(-rate) for rate in rates]
        taps = across_taps(taps_s, Rows(taps_v, i, width), (0, 1, 2))
        skip = taps_s[pl.ds(9 * groups, groups)]
        for n, value in enumerate(decay + resid + taps[0] + taps[1] + taps[2] + [skip]):
            held_s[block_at((i - first_step) * held + n, groups)] = value
        for n in range(order):
            table_ref[block_at(i * order + n, groups)] = decay[n]
        return 0

    lax.fori_loop(first_step, end_step, hold, 0)
    arrive(first_step)
    for call in fills_of(first_step, 0):
        call()

    def step(i, _):
        values = [held_s[block_at((i - first_step) * held + n, groups)] for n in range(held)]
        decay, resid, skip = values[:order], values[order : 2 * order], values[-1]
        taps = [values[2 * order + 3 * s : 2 * order + 3 * s + 3] for s in range(3)]

        def row_of(ref, t):
            return ref[pl.ds(t, groups, stride=pitch)]

        def token(t, carry, masked):
            back1, back2, states = carry
            now = [row_of(ref, t) for ref in scratches]
            if masked:
                same = (ids_ref[t] == ids_ref[t - 1]).astype(F32)
                back1 = [value * same for value in back1]
                back2 = [value * same for value in back2]
                states = [value * same for value in states]
            conv = [taps[s][0] * now[s] + taps[s][1] * back1[s] + taps[s][2] * back2[s] for s in range(3)]
            gated = rounded(conv[1] * conv[2])
            states = [states[n] * decay[n] + gated for n in range(order)]
            total = summed([states[n] * resid[n] for n in range(order)])
            live = (ids_ref[t] == ids_ref[1]).astype(F32)
            return (now, back1, states), conv[0] * (total + skip * gated), conv[0] * live

        def chunk(masked, skipped, at, later, later_at, carry):
            coming = fills_of(later, later_at)
            for j in range(skipped):
                share(coming, j)
            for j in range(skipped, CHUNK, 2):
                share(coming, j)
                carry, part0, query0 = token(at + j, carry, masked)
                share(coming, j + 1)
                carry, part1, query1 = token(at + j + 1, carry, masked)
                pair = pl.ds(pl.multiple_of((i * tokens + at + j) * groups, 2 * groups), 2 * groups)
                part_ref[pair] = jnp.concatenate([part0, part1], axis=0).astype(BF16)
                query_ref[pair] = jnp.concatenate([query0, query1], axis=0).astype(BF16)
            return carry

        def any_chunk(c, carry):
            at = pl.multiple_of(c * CHUNK, CHUNK)
            ends_here = c == chunks - 1
            pl.when(ends_here & (i + 1 < end_step))(functools.partial(arrive, i + 1))
            later = jnp.where(ends_here, jnp.minimum(i + 1, end_step - 1), i)
            later_at = pl.multiple_of(jnp.where(ends_here, 0, at + CHUNK), CHUNK)
            return lax.cond(
                ids_ref[at - 1] == ids_ref[at + CHUNK - 1],
                functools.partial(chunk, False, 0, at, later, later_at),
                functools.partial(chunk, True, 0, at, later, later_at),
                carry,
            )

        back1, back2 = ([row_of(ref, t) for ref in scratches] for t in (1, 0))
        same = (ids_ref[1] == ids_ref[0]).astype(F32)
        carry = (back1, [value * same for value in back2], [jnp.zeros((groups, LANES), F32)] * order)
        carry = chunk(True, 2, 0, i, CHUNK, carry)
        lax.fori_loop(1, chunks, any_chunk, carry)
        return 0

    lax.fori_loop(first_step, end_step, step, 0)
    for copy in own:
        copy.wait()


def finish_kernel(width, state_ref, part_ref, query_ref, table_ref, out_hbm, out_v, out_s, modes_s, sems):
    tokens, channels = out_v.shape
    steps = channels // width
    groups = width // LANES
    pitch = pitch_of(tokens)
    wide = state_ref.shape[2]
    order = table_ref.shape[0] // (groups * steps)
    going = columns(out_v, out_hbm, sems, width)

    def step(i, _):
        decay = [table_ref[block_at(i * order + n, groups)] for n in range(order)]
        for group in range(groups):
            chunk_at = i * (width // wide) + (group * LANES) // wide
            modes_s[pl.ds(group * TOLD, TOLD)] = state_ref[chunk_at, :, pl.ds((group * LANES) % wide, LANES)].astype(F32)
        running = [modes_s[pl.ds(n, groups, stride=TOLD)] for n in range(order)]
        weights = [running[0]] + [running[n] - running[n - 1] for n in range(1, order)]

        def pair(t, weights):
            at = pl.ds(pl.multiple_of((i * tokens + t) * groups, 2 * groups), 2 * groups)
            part, live_query = part_ref[at].astype(F32), query_ref[at].astype(F32)
            for k in range(2):
                weights = [weights[n] * decay[n] for n in range(order)]
                rows = slice(k * groups, (k + 1) * groups)
                out_s[pl.ds(t + k, groups, stride=pitch)] = part[rows] + live_query[rows] * summed(weights)
            return weights

        def give(at, group):
            out_v[pl.ds(at, CHUNK), lanes_at(i, width, group)] = out_s[pl.ds(group * pitch + at, CHUNK)].astype(BF16)

        def gives(at):
            return [functools.partial(give, at, group) for group in range(groups)]

        def chunk(c, weights):
            at = pl.multiple_of(c * CHUNK, CHUNK)
            done = gives(at - CHUNK)
            for j in range(0, CHUNK, 2):
                share(done, j)
                share(done, j + 1)
                weights = pair(at + j, weights)
            return weights

        for t in range(2):
            out_s[pl.ds(t, groups, stride=pitch)] = modes_s[pl.ds(order + t, groups, stride=TOLD)]
        for t in range(2, CHUNK, 2):
            weights = pair(t, weights)
        lax.fori_loop(1, tokens // CHUNK, chunk, weights)
        for call in gives(tokens - CHUNK):
            call()
        going(i).start()
        return 0

    lax.fori_loop(0, steps, step, 0)
    for i in range(steps):
        going(i).wait()


def on_device(query, keyed, valued, short_taps, rates, residues, skip_gain, doc_ids):
    tokens, channels = query.shape
    order = rates.shape[0]
    n_ctx = lax.axis_size("ctx")
    meeting = meeting_order(n_ctx)
    turn = [meeting.index(i) for i in range(n_ctx)]
    exchange = lambda value: lax.all_to_all(
        value, "ctx", split_axis=0, concat_axis=0, tiled=True, axis_index_groups=[meeting]
    )
    own = channels // n_ctx
    wide = own if own % LANES == 0 else LANES
    chunks = channels // wide
    width = min(channels, 8 * LANES)
    steps = channels // width
    groups = width // LANES
    pitch = pitch_of(tokens)
    params = pltpu.CompilerParams(vmem_limit_bytes=24 * 1024 * 1024)
    anywhere = pl.BlockSpec(memory_space=pl.ANY)
    smem = pl.BlockSpec(memory_space=pltpu.SMEM)
    vmem = pl.BlockSpec(memory_space=pltpu.VMEM)
    hbm = lambda *arrays: [pltpu.with_memory_space_constraint(array, pltpu.HBM) for array in arrays]
    near = lambda *arrays: [pltpu.with_memory_space_constraint(array, pltpu.VMEM) for array in arrays]

    modes_scratch = pltpu.VMEM(((groups + 1) * order, LANES), F32)
    skip_gain = skip_gain.reshape(1, channels)
    tall = [pltpu.VMEM((channels // LANES * tokens, LANES), dtype) for dtype in (BF16, BF16)]
    table = pltpu.VMEM((steps * order * groups, LANES), F32)
    taps_v, modes_v = pltpu.VMEM((3, 3, channels), F32), pltpu.VMEM((order, channels), F32)

    info = pl.pallas_call(
        functools.partial(ends_kernel, width),
        in_specs=[smem] + [anywhere] * 6,
        out_specs=anywhere,
        out_shape=pltpu.HBM((chunks, INFO, wide), BF16),
        scratch_shapes=[
            pltpu.VMEM((2, 2 * ROWS, channels), BF16),
            pltpu.VMEM((tokens, channels), BF16),
            pltpu.VMEM((tokens, channels), BF16),
            taps_v,
            modes_v,
            modes_v,
            pltpu.VMEM((chunks, INFO, wide), BF16),
            pltpu.VMEM(((2 * groups + 1) * pitch, LANES), F32),
            pltpu.VMEM(((2 * groups + 1) * pitch, LANES), F32),
            modes_scratch,
            pltpu.VMEM((9 * groups, LANES), F32),
            pltpu.VMEM((steps * (2 * order + 6) * groups, LANES), F32),
            pltpu.SemaphoreType.DMA((3 * steps + 5,)),
        ],
        compiler_params=params,
        name="block_ends",
    )(*hbm(doc_ids, query, keyed, valued, short_taps, rates, residues))

    if wide != own:
        info = info.transpose(1, 0, 2).reshape(INFO, n_ctx, own).transpose(1, 0, 2)
    info = exchange(info)

    def local_scan(first, count, filled, owned=()):
        return pl.pallas_call(
            functools.partial(local_kernel, width, first, count, len(filled), turn),
            in_specs=[smem] + [anywhere] * 7 + [vmem] * len(filled),
            out_specs=[vmem] * (3 + len(owned)),
            out_shape=[*tall, table, *owned],
            input_output_aliases={8 + i: i for i in range(len(filled))},
            scratch_shapes=[
                pltpu.VMEM((tokens, channels), BF16),
                pltpu.VMEM((tokens, channels), BF16),
                pltpu.VMEM((tokens, channels), BF16),
                taps_v,
                modes_v,
                modes_v,
                pltpu.VMEM((1, channels), F32),
                *[pltpu.VMEM(((groups + 1) * pitch, LANES), F32)] * 3,
                modes_scratch,
                pltpu.VMEM((10 * groups, LANES), F32),
                pltpu.VMEM((count * (2 * order + 10) * groups, LANES), F32),
                pltpu.SemaphoreType.DMA((3 * count + 4 + len(owned),)),
            ],
            compiler_params=params,
            cost_estimate=pl.CostEstimate(
                flops=count * tokens * width * 64, bytes_accessed=count * tokens * width * 14, transcendentals=0
            ),
            name="local_scan",
        )(
            *hbm(doc_ids, query, keyed, valued, short_taps, rates, residues, skip_gain), *near(*filled),
        )

    half = steps // 2 or steps
    if own % LANES == 0:
        owned = [pltpu.VMEM(value.shape[:-1] + (own,), F32) for value in (short_taps, rates, residues, skip_gain)]
        *filled, own_taps, own_rates, own_resid, own_skip = local_scan(0, half, [], owned)
        own_params = [own_taps, own_rates, own_resid, own_skip]
    else:
        filled = local_scan(0, half, [])
        at = place_in(turn) * own
        own_params = [
            lax.dynamic_slice_in_dim(value, at, own, value.ndim - 1)
            for value in (short_taps, rates, residues, skip_gain)
        ]
    info, *filled = lax.optimization_barrier((info, *filled))
    state = pl.pallas_call(
        functools.partial(carry_kernel, turn, tokens),
        out_shape=pltpu.HBM((n_ctx, TOLD, own), BF16),
        compiler_params=params,
        name="block_carry",
    )(*near(info, *own_params))
    state, *filled = lax.optimization_barrier((state, *filled))
    state = exchange(state)
    if half < steps:
        filled = local_scan(half, steps - half, filled)
    if wide != own:
        state = state.transpose(1, 0, 2).reshape(TOLD, chunks, wide).transpose(1, 0, 2)

    return pl.pallas_call(
        functools.partial(finish_kernel, width),
        in_specs=[vmem] * 4,
        out_specs=anywhere,
        out_shape=pltpu.HBM((tokens, channels), BF16),
        scratch_shapes=[
            pltpu.VMEM((tokens, channels), BF16),
            pltpu.VMEM(((groups + 1) * pitch, LANES), F32),
            pltpu.VMEM(((groups + 1) * TOLD, LANES), F32),
            pltpu.SemaphoreType.DMA((steps,)),
        ],
        compiler_params=params,
        name="add_carry",
    )(*near(state, *filled))


def solution(mesh):
    return jax.shard_map(
        on_device,
        mesh=mesh,
        in_specs=(
            P("ctx", "tp"),
            P("ctx", "tp"),
            P("ctx", "tp"),
            P(None, None, "tp"),
            P(None, "tp"),
            P(None, "tp"),
            P("tp"),
            P("ctx"),
        ),
        out_specs=P("ctx", "tp"),
        check_vma=False,
    )
```

```python
import functools

import jax
import jax.numpy as jnp
from jax import lax
from jax.experimental import pallas as pl
from jax.experimental.pallas import tpu as pltpu
from jax.sharding import PartitionSpec as P

LANES = 128
ROWS = 8
CHUNK = 16
INFO = 24
TOLD = 16
F32 = jnp.float32
BF16 = jnp.bfloat16


def meeting_order(count):
    place = lambda i: (i % 2, i // 2 % 2, i // 4)
    root = place(5 * count // 8)
    return sorted(range(count), key=lambda i: (sum(abs(a - b) for a, b in zip(place(i), root)), -i))


def place_in(turn):
    me = lax.axis_index("ctx")
    place = jnp.int32(0)
    for i, at in enumerate(turn):
        place = jnp.where(me == i, at, place)
    return place


def rounded(value):
    return value.astype(BF16).astype(F32)


def row_index(rows=ROWS):
    return lax.broadcasted_iota(jnp.int32, (rows, LANES), 0)


def block_at(index, size):
    start = index * size
    return pl.ds(start if isinstance(start, int) else pl.multiple_of(start, size), size)


def pitch_of(tokens):
    return tokens + ROWS


def lanes_at(index, size, group):
    start = index * size + group * LANES
    return pl.ds(start if isinstance(start, int) else pl.multiple_of(start, LANES), LANES)


def columns(source, target, sems, width):
    return lambda i: pltpu.make_async_copy(
        source.at[..., block_at(i, width)], target.at[..., block_at(i, width)], sems.at[i]
    )


def across(scratch, rows_of):
    rows = rows_of.ref.shape[0]
    for group in range(rows_of.groups):
        scratch[pl.ds(group * rows, rows)] = rows_of(group)
    return [scratch[pl.ds(n, rows_of.groups, stride=rows)] for n in range(rows)]


class Rows:
    def __init__(self, ref, step, width):
        self.ref, self.step, self.width, self.groups = ref, step, width, width // LANES

    def __call__(self, group):
        return self.ref[..., lanes_at(self.step, self.width, group)]


def across_taps(scratch, rows_of, streams):
    groups = rows_of.groups
    for group in range(groups):
        taps = rows_of(group)
        for s in streams:
            for j in range(3):
                scratch[pl.ds((s * 3 + j) * groups + group, 1)] = taps[s, j : j + 1]
    return [[scratch[pl.ds((s * 3 + j) * groups, groups)] for j in range(3)] for s in streams]


def fill_group(scratch, base, pitch, rows_of, at, group):
    lanes = lanes_at(rows_of.step, rows_of.width, group)
    scratch[pl.ds(base + group * pitch + at, CHUNK)] = rows_of.ref[pl.ds(at, CHUNK), lanes].astype(F32)


def fills(scratches, refs, base, pitch, step, width, at):
    return [
        functools.partial(fill_group, scratch, base, pitch, Rows(ref, step, width), at, group)
        for scratch, ref in zip(scratches, refs)
        for group in range(width // LANES)
    ]


def share(calls, j):
    for call in calls[len(calls) * j // CHUNK : len(calls) * (j + 1) // CHUNK]:
        call()


def first_of_last(ids_ref):
    tokens = ids_ref.shape[0]
    low, high = jnp.int32(0), jnp.int32(tokens - 1)
    last = ids_ref[tokens - 1]
    for _ in range((tokens - 1).bit_length()):
        middle = (low + high) // 2
        same = ids_ref[middle] == last
        low, high = jnp.where(same, low, middle + 1), jnp.where(same, middle, high)
    return high


def by_rate(rates, resid):
    rates, resid = list(rates), list(resid)
    for turn in range(len(rates)):
        for i in range(turn % 2, len(rates) - 1, 2):
            low, high = rates[i], rates[i + 1]
            swap = low > high
            rates[i], rates[i + 1] = jnp.minimum(low, high), jnp.maximum(low, high)
            resid[i], resid[i + 1] = jnp.where(swap, resid[i + 1], resid[i]), jnp.where(swap, resid[i], resid[i + 1])
    return rates, resid


def summed(terms):
    while len(terms) > 1:
        terms = [sum(terms[i : i + 2]) for i in range(0, len(terms), 2)]
    return terms[0]


def ends_kernel(
    width, ids_ref, q_hbm, k_hbm, v_hbm, taps_hbm, rates_hbm, resid_hbm,
    info_hbm,
    q_v, k_v, v_v, taps_v, rates_v, resid_v, info_v, k_s, v_s, modes_s, taps_s, held_s, sems,
):
    tokens, channels = k_v.shape
    steps = channels // width
    groups = width // LANES
    chunks = tokens // CHUNK
    pitch = pitch_of(tokens)
    wide = info_v.shape[2]
    per_step = width // wide
    order = rates_v.shape[0]
    k_in, v_in = (
        columns(source, target, sems.at[pl.ds(i * steps, steps)], width)
        for i, (source, target) in enumerate(((k_hbm, k_v), (v_hbm, v_v)))
    )
    others = [
        pltpu.make_async_copy(source, target, sems.at[3 * steps + i])
        for i, (source, target) in enumerate(
            (
                (rates_hbm, rates_v),
                (resid_hbm, resid_v),
                (taps_hbm, taps_v),
                (q_hbm.at[pl.ds(0, CHUNK)], q_v.at[0]),
                (q_hbm.at[pl.ds(tokens - CHUNK, CHUNK)], q_v.at[1]),
            )
        )
    ]
    going = lambda i: pltpu.make_async_copy(
        info_v.at[block_at(i, per_step)], info_hbm.at[block_at(i, per_step)], sems.at[2 * steps + i]
    )
    for copy in others[:3]:
        copy.start()
    for i in range(steps):
        k_in(i).start()
        v_in(i).start()
        if i == 0:
            for copy in others[3:]:
                copy.start()
    begin = first_of_last(ids_ref)
    chunk0 = begin // CHUNK
    row = row_index()
    marks = jnp.zeros((ROWS, LANES), F32)
    for i, t in enumerate((0, 1, tokens - 2, tokens - 1)):
        marks = jnp.where(row == i + 4, ids_ref[t].astype(F32), marks)

    def base_of(i):
        return pl.multiple_of(jnp.bitwise_and(i, 1) * (groups * pitch), ROWS)

    def fills_of(i, at):
        return fills((k_s, v_s), (k_v, v_v), base_of(i), pitch, i, width, at)

    def arrive(i):
        k_in(i).wait()
        v_in(i).wait()

    for copy in others[:3]:
        copy.wait()
    held = 2 * order + 6

    def hold(i, _):
        rates, resid = by_rate(across(modes_s, Rows(rates_v, i, width)), across(modes_s, Rows(resid_v, i, width)))
        taps = across_taps(taps_s, Rows(taps_v, i, width), (1, 2))
        for n, value in enumerate([jnp.exp(-rate) for rate in rates] + resid + taps[0] + taps[1]):
            held_s[block_at(i * held + n, groups)] = value
        return 0

    lax.fori_loop(0, steps, hold, 0)
    arrive(0)
    for call in fills_of(0, pl.multiple_of(chunk0 * CHUNK, CHUNK)):
        call()
    for copy in others[3:]:
        copy.wait()

    def step(i):

        base = base_of(i)
        values = [held_s[block_at(i * held + n, groups)] for n in range(held)]
        decay, resid = values[:order], values[order : 2 * order]
        taps = [values[2 * order : 2 * order + 3], values[2 * order + 3 :]]

        def chunk(masked, c, carry):
            at = pl.multiple_of(c * CHUNK, CHUNK)
            back1, back2, ends = carry
            ends_here = c == chunks - 1
            if i + 1 < steps:
                pl.when(ends_here)(functools.partial(arrive, i + 1))
            later = jnp.where(ends_here, min(i + 1, steps - 1), i)
            later_at = pl.multiple_of(jnp.where(ends_here, chunk0, c + 1) * CHUNK, CHUNK)
            coming = fills_of(later, later_at)
            for j in range(CHUNK):
                t = at + j
                share(coming, j)
                here = [ref[pl.ds(base + t, groups, stride=pitch)] for ref in (k_s, v_s)]
                if masked:
                    live = (t >= begin).astype(F32)
                    here = [value * live for value in here]
                conv = [taps[s][0] * here[s] + taps[s][1] * back1[s] + taps[s][2] * back2[s] for s in range(2)]
                gated = rounded(conv[0] * conv[1])
                if masked and j < 2:
                    gated = gated * (t >= 2).astype(F32)
                ends = [ends[n] * decay[n] + gated for n in range(order)]
                back1, back2 = here, back1
            return back1, back2, ends

        zero = jnp.zeros((groups, LANES), F32)
        carry = chunk(True, chunk0, ([zero] * 2, [zero] * 2, [zero] * order))
        ends = lax.fori_loop(chunk0 + 1, chunks, functools.partial(chunk, False), carry)[2]
        running = zero
        for n in range(order):
            running = running + resid[n] * ends[n]
            modes_s[pl.ds(n, groups, stride=order)] = running

        for group in range(groups):
            lanes = lanes_at(i, width, group)
            state = modes_s[pl.ds(group * order, order)]
            heads = [ref[pl.ds(0, CHUNK), lanes].astype(F32)[:ROWS] for ref in (k_v, v_v)]
            tails = [ref[pl.ds(tokens - CHUNK, CHUNK), lanes].astype(F32)[ROWS:] for ref in (k_v, v_v)]
            edge = jnp.where(row < 2, heads[0], pltpu.roll(heads[1], 2, 0))
            edge = jnp.where(row < 4, edge, pltpu.roll(tails[0], ROWS - 2, 0))
            edge = jnp.where(row < 6, edge, tails[1])
            at = i * per_step + (group * LANES) // wide
            inner = pl.ds((group * LANES) % wide, LANES)
            q_head, q_tail = (q_v[j, :, lanes].astype(F32) for j in range(2))
            more = jnp.where(row < 2, q_head[:ROWS], pltpu.roll(q_tail[ROWS:], 4, 0))
            more = jnp.where(row < 4, more, marks)
            info_v[at, :, inner] = jnp.concatenate([state, edge, more], axis=0).astype(BF16)
        going(i).start()

    for i in range(steps):
        step(i)
    for i in range(steps):
        going(i).wait()


def carry_kernel(turn, tokens, info_ref, taps_ref, rates_ref, resid_ref, skip_ref, out_ref):
    order, wide = rates_ref.shape
    skip = skip_ref[...]
    rows = lambda ref: [ref[n : n + 1] for n in range(order)]
    rates, resid = (jnp.concatenate(modes, axis=0) for modes in by_rate(rows(rates_ref), rows(resid_ref)))
    decay = jnp.exp(-rates)
    rest = jnp.exp(-float(tokens - 2) * rates)
    row = lax.broadcasted_iota(jnp.int32, (order, wide), 0)
    even = row % 2 == 0

    def turned(value, steps):
        if wide % LANES:
            return jnp.concatenate([value[order - steps :], value[: order - steps]], axis=0)
        return pltpu.roll(value, steps, 0)

    def down(value, steps):
        return jnp.where(row < steps, 0.0, turned(value, steps))

    def tap(j):
        key, value, query = (jnp.broadcast_to(taps_ref[s, j : j + 1], (order, wide)) for s in (1, 2, 0))
        return jnp.where(row < 2, key, jnp.where(row < 4, value, query))

    taps = [tap(j) for j in range(3)]
    state = jnp.zeros((order, wide), F32)
    tails, prev0, prev1 = state, jnp.full((1, wide), -1.0, F32), jnp.full((1, wide), -1.0, F32)
    for block in turn:
        info = info_ref[block].astype(F32)
        running, edge, more = (info[i * ROWS : (i + 1) * ROWS] for i in range(3))
        ends = running - down(running, 1)
        first0, first1, last0, last1 = (more[4 + i : 5 + i] for i in range(4))
        same = lambda one, other: (one == other).astype(F32)
        entering, inside = same(prev1, first0), same(first0, first1)
        heads = jnp.where(row < 4, edge, turned(more, 4))
        back1 = jnp.where(even, turned(tails, order - 1), turned(heads, 1))
        conv = (
            taps[0] * heads
            + taps[1] * (back1 * jnp.where(even, entering, inside))
            + taps[2] * (tails * jnp.where(even, same(prev0, first0), same(prev1, first1)))
        )
        gated = rounded(conv * turned(conv, order - 2))
        state0 = decay * (state * entering) + resid * gated[0:1]
        state1 = decay * (state0 * inside) + resid * gated[1:2]
        long0 = jnp.sum(state0, axis=0, keepdims=True)
        long1 = jnp.sum(state1, axis=0, keepdims=True)
        mixed = turned(conv, order - 4) * (jnp.where(row == 0, long0, long1) + skip * gated)
        running = state1
        for steps in (1, 2, 4):
            running = running + down(running, steps)
        out_ref[block] = jnp.concatenate([running, mixed], axis=0).astype(BF16)
        state = ends + rest * (state1 * same(first1, last1))
        tails = jnp.where(row < 4, turned(edge, 4), turned(more, 2))
        prev0, prev1 = last0, last1


def local_kernel(
    width, first_step, count, filled, turn, ids_ref, q_hbm, k_hbm, v_hbm, taps_hbm, rates_hbm, resid_hbm, skip_hbm, *rest
):
    (
        q_v, k_v, v_v, taps_v, rates_v, resid_v, skip_v, q_s, k_s, v_s, modes_s, taps_s, held_s, sems,
    ) = rest[-14:]
    part_ref, query_ref, table_ref, *own_refs = rest[filled:-14]
    tokens, channels = q_v.shape
    owned = []
    if own_refs:
        mine = own_refs[0].shape[-1]
        lanes = pl.ds(pl.multiple_of(place_in(turn) * mine, mine), mine)
        owned = [
            (source.at[..., lanes], target)
            for source, target in zip((taps_hbm, rates_hbm, resid_hbm, skip_hbm), own_refs)
        ]
    groups = width // LANES
    pitch = pitch_of(tokens)
    chunks = tokens // CHUNK
    order = rates_v.shape[0]
    end_step = first_step + count
    scratches = (q_s, k_s, v_s)
    streams = [
        lambda i, s=s, source=source, target=target: pltpu.make_async_copy(
            source.at[:, block_at(i, width)], target.at[:, block_at(i, width)], sems.at[s * count + i - first_step]
        )
        for s, (source, target) in enumerate(((q_hbm, q_v), (k_hbm, k_v), (v_hbm, v_v)))
    ]
    part = pl.ds(first_step * width, count * width)
    own = [pltpu.make_async_copy(source, target, sems.at[3 * count + 4 + i]) for i, (source, target) in enumerate(owned)]
    others = [
        pltpu.make_async_copy(source.at[..., part], target.at[..., part], sems.at[3 * count + i])
        for i, (source, target) in enumerate(
            ((taps_hbm, taps_v), (rates_hbm, rates_v), (resid_hbm, resid_v), (skip_hbm, skip_v))
        )
    ]
    for copy in others:
        copy.start()
    for i in range(first_step, end_step):
        for copy in streams:
            copy(i).start()
    for copy in own:
        copy.start()

    def arrive(i):
        for copy in streams:
            copy(i).wait()

    def fills_of(i, at):
        return fills(scratches, (q_v, k_v, v_v), 0, pitch, i, width, at)

    for copy in others:
        copy.wait()
    held = 2 * order + 10

    def hold(i, _):
        for group in range(groups):
            taps_s[pl.ds(9 * groups + group, 1)] = skip_v[:, lanes_at(i, width, group)]
        rates, resid = by_rate(across(modes_s, Rows(rates_v, i, width)), across(modes_s, Rows(resid_v, i, width)))
        decay = [jnp.exp(-rate) for rate in rates]
        taps = across_taps(taps_s, Rows(taps_v, i, width), (0, 1, 2))
        skip = taps_s[pl.ds(9 * groups, groups)]
        for n, value in enumerate(decay + resid + taps[0] + taps[1] + taps[2] + [skip]):
            held_s[block_at((i - first_step) * held + n, groups)] = value
        for n in range(order):
            table_ref[block_at(i * order + n, groups)] = decay[n]
        return 0

    lax.fori_loop(first_step, end_step, hold, 0)
    arrive(first_step)
    for call in fills_of(first_step, 0):
        call()

    def step(i, _):
        values = [held_s[block_at((i - first_step) * held + n, groups)] for n in range(held)]
        decay, resid, skip = values[:order], values[order : 2 * order], values[-1]
        taps = [values[2 * order + 3 * s : 2 * order + 3 * s + 3] for s in range(3)]

        def row_of(ref, t):
            return ref[pl.ds(t, groups, stride=pitch)]

        def token(t, carry, masked):
            back1, back2, states = carry
            now = [row_of(ref, t) for ref in scratches]
            if masked:
                same = (ids_ref[t] == ids_ref[t - 1]).astype(F32)
                back1 = [value * same for value in back1]
                back2 = [value * same for value in back2]
                states = [value * same for value in states]
            conv = [taps[s][0] * now[s] + taps[s][1] * back1[s] + taps[s][2] * back2[s] for s in range(3)]
            gated = rounded(conv[1] * conv[2])
            states = [states[n] * decay[n] + gated for n in range(order)]
            total = summed([states[n] * resid[n] for n in range(order)])
            live = (ids_ref[t] == ids_ref[1]).astype(F32)
            return (now, back1, states), conv[0] * (total + skip * gated), conv[0] * live

        def chunk(masked, skipped, at, later, later_at, carry):
            coming = fills_of(later, later_at)
            for j in range(skipped):
                share(coming, j)
            for j in range(skipped, CHUNK, 2):
                share(coming, j)
                carry, part0, query0 = token(at + j, carry, masked)
                share(coming, j + 1)
                carry, part1, query1 = token(at + j + 1, carry, masked)
                pair = pl.ds(pl.multiple_of((i * tokens + at + j) * groups, 2 * groups), 2 * groups)
                part_ref[pair] = jnp.concatenate([part0, part1], axis=0).astype(BF16)
                query_ref[pair] = jnp.concatenate([query0, query1], axis=0).astype(BF16)
            return carry

        def any_chunk(c, carry):
            at = pl.multiple_of(c * CHUNK, CHUNK)
            ends_here = c == chunks - 1
            pl.when(ends_here & (i + 1 < end_step))(functools.partial(arrive, i + 1))
            later = jnp.where(ends_here, jnp.minimum(i + 1, end_step - 1), i)
            later_at = pl.multiple_of(jnp.where(ends_here, 0, at + CHUNK), CHUNK)
            return lax.cond(
                ids_ref[at - 1] == ids_ref[at + CHUNK - 1],
                functools.partial(chunk, False, 0, at, later, later_at),
                functools.partial(chunk, True, 0, at, later, later_at),
                carry,
            )

        back1, back2 = ([row_of(ref, t) for ref in scratches] for t in (1, 0))
        same = (ids_ref[1] == ids_ref[0]).astype(F32)
        carry = (back1, [value * same for value in back2], [jnp.zeros((groups, LANES), F32)] * order)
        carry = chunk(True, 2, 0, i, CHUNK, carry)
        lax.fori_loop(1, chunks, any_chunk, carry)
        return 0

    lax.fori_loop(first_step, end_step, step, 0)
    for copy in own:
        copy.wait()


def finish_kernel(width, state_ref, part_ref, query_ref, table_ref, out_hbm, out_v, out_s, modes_s, sems):
    tokens, channels = out_v.shape
    steps = channels // width
    groups = width // LANES
    pitch = pitch_of(tokens)
    wide = state_ref.shape[2]
    order = table_ref.shape[0] // (groups * steps)
    going = columns(out_v, out_hbm, sems, width)

    def step(i, _):
        decay = [table_ref[block_at(i * order + n, groups)] for n in range(order)]
        for group in range(groups):
            chunk_at = i * (width // wide) + (group * LANES) // wide
            modes_s[pl.ds(group * TOLD, TOLD)] = state_ref[chunk_at, :, pl.ds((group * LANES) % wide, LANES)].astype(F32)
        running = [modes_s[pl.ds(n, groups, stride=TOLD)] for n in range(order)]
        weights = [running[0]] + [running[n] - running[n - 1] for n in range(1, order)]

        def pair(t, weights):
            at = pl.ds(pl.multiple_of((i * tokens + t) * groups, 2 * groups), 2 * groups)
            part, live_query = part_ref[at].astype(F32), query_ref[at].astype(F32)
            for k in range(2):
                weights = [weights[n] * decay[n] for n in range(order)]
                rows = slice(k * groups, (k + 1) * groups)
                out_s[pl.ds(t + k, groups, stride=pitch)] = part[rows] + live_query[rows] * summed(weights)
            return weights

        def give(at, group):
            out_v[pl.ds(at, CHUNK), lanes_at(i, width, group)] = out_s[pl.ds(group * pitch + at, CHUNK)].astype(BF16)

        def gives(at):
            return [functools.partial(give, at, group) for group in range(groups)]

        def chunk(c, weights):
            at = pl.multiple_of(c * CHUNK, CHUNK)
            done = gives(at - CHUNK)
            for j in range(0, CHUNK, 2):
                share(done, j)
                share(done, j + 1)
                weights = pair(at + j, weights)
            return weights

        for t in range(2):
            out_s[pl.ds(t, groups, stride=pitch)] = modes_s[pl.ds(order + t, groups, stride=TOLD)]
        for t in range(2, CHUNK, 2):
            weights = pair(t, weights)
        lax.fori_loop(1, tokens // CHUNK, chunk, weights)
        for call in gives(tokens - CHUNK):
            call()
        going(i).start()
        return 0

    lax.fori_loop(0, steps, step, 0)
    for i in range(steps):
        going(i).wait()


def on_device(query, keyed, valued, short_taps, rates, residues, skip_gain, doc_ids):
    tokens, channels = query.shape
    order = rates.shape[0]
    n_ctx = lax.axis_size("ctx")
    meeting = meeting_order(n_ctx)
    turn = [meeting.index(i) for i in range(n_ctx)]
    exchange = lambda value: lax.all_to_all(
        value, "ctx", split_axis=0, concat_axis=0, tiled=True, axis_index_groups=[meeting]
    )
    own = channels // n_ctx
    wide = own if own % LANES == 0 else LANES
    chunks = channels // wide
    width = min(channels, 8 * LANES)
    steps = channels // width
    groups = width // LANES
    pitch = pitch_of(tokens)
    params = pltpu.CompilerParams(vmem_limit_bytes=24 * 1024 * 1024)
    anywhere = pl.BlockSpec(memory_space=pl.ANY)
    smem = pl.BlockSpec(memory_space=pltpu.SMEM)
    vmem = pl.BlockSpec(memory_space=pltpu.VMEM)
    hbm = lambda *arrays: [pltpu.with_memory_space_constraint(array, pltpu.HBM) for array in arrays]
    near = lambda *arrays: [pltpu.with_memory_space_constraint(array, pltpu.VMEM) for array in arrays]

    modes_scratch = pltpu.VMEM(((groups + 1) * order, LANES), F32)
    skip_gain = skip_gain.reshape(1, channels)
    tall = [pltpu.VMEM((channels // LANES * tokens, LANES), dtype) for dtype in (BF16, BF16)]
    table = pltpu.VMEM((steps * order * groups, LANES), F32)
    taps_v, modes_v = pltpu.VMEM((3, 3, channels), F32), pltpu.VMEM((order, channels), F32)

    info = pl.pallas_call(
        functools.partial(ends_kernel, width),
        in_specs=[smem] + [anywhere] * 6,
        out_specs=anywhere,
        out_shape=pltpu.HBM((chunks, INFO, wide), BF16),
        scratch_shapes=[
            pltpu.VMEM((2, 2 * ROWS, channels), BF16),
            pltpu.VMEM((tokens, channels), BF16),
            pltpu.VMEM((tokens, channels), BF16),
            taps_v,
            modes_v,
            modes_v,
            pltpu.VMEM((chunks, INFO, wide), BF16),
            pltpu.VMEM(((2 * groups + 1) * pitch, LANES), F32),
            pltpu.VMEM(((2 * groups + 1) * pitch, LANES), F32),
            modes_scratch,
            pltpu.VMEM((9 * groups, LANES), F32),
            pltpu.VMEM((steps * (2 * order + 6) * groups, LANES), F32),
            pltpu.SemaphoreType.DMA((3 * steps + 5,)),
        ],
        compiler_params=params,
        name="block_ends",
    )(*hbm(doc_ids, query, keyed, valued, short_taps, rates, residues))

    if wide != own:
        info = info.transpose(1, 0, 2).reshape(INFO, n_ctx, own).transpose(1, 0, 2)
    info = exchange(info)

    def local_scan(first, count, filled, owned=()):
        return pl.pallas_call(
            functools.partial(local_kernel, width, first, count, len(filled), turn),
            in_specs=[smem] + [anywhere] * 7 + [vmem] * len(filled),
            out_specs=[vmem] * (3 + len(owned)),
            out_shape=[*tall, table, *owned],
            input_output_aliases={8 + i: i for i in range(len(filled))},
            scratch_shapes=[
                pltpu.VMEM((tokens, channels), BF16),
                pltpu.VMEM((tokens, channels), BF16),
                pltpu.VMEM((tokens, channels), BF16),
                taps_v,
                modes_v,
                modes_v,
                pltpu.VMEM((1, channels), F32),
                *[pltpu.VMEM(((groups + 1) * pitch, LANES), F32)] * 3,
                modes_scratch,
                pltpu.VMEM((10 * groups, LANES), F32),
                pltpu.VMEM((count * (2 * order + 10) * groups, LANES), F32),
                pltpu.SemaphoreType.DMA((3 * count + 4 + len(owned),)),
            ],
            compiler_params=params,
            cost_estimate=pl.CostEstimate(
                flops=count * tokens * width * 64, bytes_accessed=count * tokens * width * 14, transcendentals=0
            ),
            name="local_scan",
        )(
            *hbm(doc_ids, query, keyed, valued, short_taps, rates, residues, skip_gain), *near(*filled),
        )

    half = steps // 2 or steps
    if own % LANES == 0:
        owned = [pltpu.VMEM(value.shape[:-1] + (own,), F32) for value in (short_taps, rates, residues, skip_gain)]
        *filled, own_taps, own_rates, own_resid, own_skip = local_scan(0, half, [], owned)
        own_params = [own_taps, own_rates, own_resid, own_skip]
    else:
        filled = local_scan(0, half, [])
        at = place_in(turn) * own
        own_params = [
            lax.dynamic_slice_in_dim(value, at, own, value.ndim - 1)
            for value in (short_taps, rates, residues, skip_gain)
        ]
    info, *filled = lax.optimization_barrier((info, *filled))
    state = pl.pallas_call(
        functools.partial(carry_kernel, turn, tokens),
        out_shape=pltpu.HBM((n_ctx, TOLD, own), BF16),
        compiler_params=params,
        name="block_carry",
    )(*near(info, *own_params))
    state, *filled = lax.optimization_barrier((state, *filled))
    state = exchange(state)
    if half < steps:
        filled = local_scan(half, steps - half, filled)
    if wide != own:
        state = state.transpose(1, 0, 2).reshape(TOLD, chunks, wide).transpose(1, 0, 2)

    return pl.pallas_call(
        functools.partial(finish_kernel, width),
        in_specs=[vmem] * 4,
        out_specs=anywhere,
        out_shape=pltpu.HBM((tokens, channels), BF16),
        scratch_shapes=[
            pltpu.VMEM((tokens, channels), BF16),
            pltpu.VMEM(((groups + 1) * pitch, LANES), F32),
            pltpu.VMEM(((groups + 1) * TOLD, LANES), F32),
            pltpu.SemaphoreType.DMA((steps,)),
        ],
        compiler_params=params,
        name="add_carry",
    )(*near(state, *filled))


def solution(mesh):
    return jax.shard_map(
        on_device,
        mesh=mesh,
        in_specs=(
            P("ctx", "tp"),
            P("ctx", "tp"),
            P("ctx", "tp"),
            P(None, None, "tp"),
            P(None, "tp"),
            P(None, "tp"),
            P("tp"),
            P("ctx"),
        ),
        out_specs=P("ctx", "tp"),
        check_vma=False,
    )
```
